32 devices in a mesh: dp: 16 (over z, y, x), rep: 2 (over core).
Axes of the slice: x: 2, y: 2, z: 4, core: 2. Of those that a mesh axis runs over, the one named last changes fastest.
Arguments:
- tokens: bfloat16 [32768, 768], P(('dp', 'rep')), may hold values from -6 to 6
- cotangent: bfloat16 [32768, 768], P(('dp', 'rep')), may hold values from -6 to 6
- segments: int32 [64, 512], P(('dp', 'rep')), may hold values from 0 to 3, never falling along the last dimension, each value on 1 to 256 neighbouring positions
- live_count: int32 [32], P(('dp', 'rep')), may hold values from 1 to 2, as said below
- att_master: float32 [2363136], P('dp'), may hold values from -2 to 2, as said below
- att_first: float32 [2363136], P('dp'), may hold values from -60 to 60
- att_second: float32 [2363136], P('dp'), may hold values from 100 to 10000
- ffn_master: float32 [4723968], P('dp'), may hold values from -2 to 2, as said below
- ffn_first: float32 [4723968], P('dp'), may hold values from -60 to 60
- ffn_second: float32 [4723968], P('dp'), may hold values from 100 to 10000
Outputs:
- output: bfloat16 [32768, 768], P(('dp', 'rep'))
- input_grad: bfloat16 [32768, 768], P(('dp', 'rep'))
- att_grad: float32 [2363136], P('dp')
- att_first_new: float32 [2363136], P('dp')
- att_second_new: float32 [2363136], P('dp')
- att_delta: float32 [2363136], P('dp')
- ffn_grad: float32 [4723968], P('dp')
- ffn_first_new: float32 [4723968], P('dp')
- ffn_second_new: float32 [4723968], P('dp')
- ffn_delta: float32 [4723968], P('dp')
The draws below stay inside these ranges and needn't reach their ends.
Inputs may be any that keep to these rules, and one draw needn't show every extreme that they name: `segments`: documents of each packed sequence are numbered in order without falling, each 1 to 256 positions long, one exactly 256. `live_count`: each device's number of its first sequence slots that are live; some device has all 2 in every draw. `att_master`: flat attention parameters in the stated layout. `ffn_master`: flat feed-forward parameters in the stated layout.
All inputs are finite; a program needn't handle non-finite values.
Results may differ from the reference program's by a relative error of at most 0.015.
The reference program's roundings to bfloat16 on the way count: a program that leaves them out, or rounds other values in their place, can miss the bound.
Values may be sent and summed in bfloat16 or wider, within the bound.
A program may use at most 256 MiB of HBM per device.

```python
import math
import jax
import jax.numpy as jnp
import numpy as np
from jax import lax

D = 768
HEADS = 12
HEAD_DIM = 64
FF = 3072
LEN = 512
SEGS = 4
STEP = 10
SEQ_DEV = 2
NSEQ = 64
TOKENS = 32768
ATT_FLAT = 2363136
FFN_FLAT = 4723968
N_DP = 16
N_REP = 2


def rough_piece(key, count, scale):
    first = jax.random.fold_in(key, 0)
    bell = jnp.clip(jax.random.normal(first, (count,), jnp.float32), -4.0, 4.0)
    return bell * scale


def draw_live_count(key, part):
    key = jax.random.fold_in(key, 7)
    first, second = jax.random.split(key)
    devices = N_DP * N_REP
    roll = jax.random.randint(first, (devices,), 0, 4)
    counts = jnp.where(roll == 0, SEQ_DEV, (SEQ_DEV + 1) // 2).astype(jnp.int32)
    spot = jax.random.randint(second, (), 0, devices)
    return counts.at[spot].set(SEQ_DEV)


def draw_att_master(key, part):
    key = jax.random.fold_in(key, 11)
    parts = jax.random.split(key, 6)
    inverse = D ** (-0.5)
    column_scale = jnp.concatenate([jnp.full((D,), 1.5 * inverse, jnp.float32), jnp.full((2 * D,), inverse, jnp.float32)])
    qkv_weight = (rough_piece(parts[0], 3 * D * D, 1.0).reshape(D, 3 * D) * column_scale).reshape(-1)
    out_weight = rough_piece(parts[1], D * D, 8.0 * inverse)
    biases = rough_piece(parts[2], 3 * D, 0.3)
    gains = 1.0 + rough_piece(parts[3], D, 0.2)
    shifts = rough_piece(parts[4], D, 0.3)
    padding = rough_piece(parts[5], ATT_FLAT - 4 * D * D - 5 * D, 0.1)
    return jnp.concatenate([qkv_weight, out_weight, biases, gains, shifts, padding])


def draw_ffn_master(key, part):
    key = jax.random.fold_in(key, 13)
    parts = jax.random.split(key, 7)
    in_weight = rough_piece(parts[0], D * FF, D ** (-0.5))
    down_weight = rough_piece(parts[1], FF * D, 1.6 * FF ** (-0.5))
    in_bias = rough_piece(parts[2], FF, 0.3)
    down_bias = rough_piece(parts[3], D, 0.3)
    gains = 1.0 + rough_piece(parts[4], D, 0.2)
    shifts = rough_piece(parts[5], D, 0.3)
    padding = rough_piece(parts[6], FFN_FLAT - 2 * D * FF - FF - 3 * D, 0.1)
    return jnp.concatenate([in_weight, down_weight, in_bias, down_bias, gains, shifts, padding])


def steps_of(own_key, dims, cuts, smallest, top_value):
    level = 1.0
    for axis_at, blocks in cuts:
        heights = jax.random.uniform(jax.random.fold_in(jax.random.fold_in(own_key, 6), axis_at), (blocks,), jnp.float32, smallest / len(cuts), top_value / len(cuts))
        level = level * jnp.repeat(jnp.exp(heights), dims[axis_at] // blocks).reshape((-1,) + (1,) * (len(dims) - 1 - axis_at))
    return level


def length_profile(number_of, total, most, skew):
    loads = [(1 << 20) // math.isqrt(rank ** skew) + 1 for rank in range(2, number_of + 1)]
    rest, holding = total - most - (number_of - 1), [1] * (number_of - 1)
    while rest > 0:
        free = [i for i in range(number_of - 1) if holding[i] < most]
        whole, remaining = sum([loads[i] for i in free]), rest
        for i in free:
            addition = min(most - holding[i], max(1, remaining * loads[i] // whole), rest)
            holding[i] = holding[i] + addition
            rest = rest - addition
    return np.array([most] + holding)


def uneven(stream_key, number_of, total, limit, lean):
    if number_of == 2:
        one = jax.random.randint(stream_key, (), max(1, total - limit), min(limit, total - 1) + 1)
        return jnp.stack([one, total - one])
    tallies = jnp.asarray(length_profile(number_of, total, limit, lean), jnp.int32)
    pairs = (number_of - 1) // 2
    giver, sink = tallies[1:1 + 2 * pairs:2], tallies[2:2 + 2 * pairs:2]
    room = jnp.minimum(giver - 1, limit - sink)
    shifted = jax.random.randint(jax.random.fold_in(stream_key, 1), (pairs,), 0, 1 << 20) % (room + 1)
    tallies = tallies.at[1:1 + 2 * pairs:2].set(giver - shifted).at[2:2 + 2 * pairs:2].set(sink + shifted)
    return tallies[jax.random.permutation(jax.random.fold_in(stream_key, 2), number_of)]


def noise(key, extent, deviation, limit, shards=(), held_as=jnp.bfloat16):
    array = jax.random.normal(key, extent, jnp.float32) * deviation
    if len(shards) > 0:
        array = steps_of(key, extent, shards, -0.22, 0.18) * array
    return jnp.clip(array, min=-limit, max=limit).astype(held_as)


def setup_inputs(seed: int = 0) -> dict:
    keys = jax.random.split(jax.random.key(seed), 11)
    tokens = noise(keys[0], (TOKENS, D), 1.0, 6.0, ((0, 32),))
    cotangent = noise(keys[1], (TOKENS, D), 1.0, 6.0, ((0, 32),))
    segments = jax.vmap(lambda own: jnp.searchsorted(jnp.cumsum(uneven(own, SEGS, LEN, LEN // 2, 2)), jnp.arange(LEN), side="right"))(jax.random.split(keys[2], NSEQ)).reshape((NSEQ, LEN)).astype(jnp.int32)
    live_count = draw_live_count(jax.random.fold_in(keys[10], 71), 0)
    att_master = draw_att_master(jax.random.fold_in(keys[10], 71), 0)
    att_first = noise(keys[5], (ATT_FLAT,), 10.0, 60.0, ((0, 16),), jnp.float32)
    att_second = jnp.clip(jnp.exp(math.log(10000.0) - 4.6051702 * jax.random.uniform(keys[6], (ATT_FLAT,), jnp.float32) ** steps_of(keys[6], (ATT_FLAT,), ((0, 16),), -0.2, 0.2)), 100.0, 10000.0)
    ffn_master = draw_ffn_master(jax.random.fold_in(keys[10], 71), 0)
    ffn_first = noise(keys[8], (FFN_FLAT,), 10.0, 60.0, ((0, 16),), jnp.float32)
    ffn_second = jnp.clip(jnp.exp(math.log(10000.0) - 4.6051702 * jax.random.uniform(keys[9], (FFN_FLAT,), jnp.float32) ** steps_of(keys[9], (FFN_FLAT,), ((0, 16),), -0.2, 0.2)), 100.0, 10000.0)
    return {"tokens": tokens, "cotangent": cotangent, "segments": segments, "live_count": live_count, "att_master": att_master, "att_first": att_first, "att_second": att_second, "ffn_master": ffn_master, "ffn_first": ffn_first, "ffn_second": ffn_second}


@jax.custom_vjp
def low(v):
    return lax.optimization_barrier(v.astype(jnp.bfloat16)).astype(jnp.float32)

@jax.custom_vjp
def low_back(v):
    return v

def low_keep(v):
    return (low(v), None)

def low_pass(kept, grad):
    return (grad,)

def back_keep(v):
    return (v, None)

def back_low(kept, grad):
    return (low(grad),)
low.defvjp(low_keep, low_pass)
low_back.defvjp(back_keep, back_low)
highest = lax.Precision.HIGHEST
norm_eps = 1e-05
beta_one = 0.9
beta_two = 0.98
decay = 0.01
adam_eps = 1e-08
masked = -1e+30
seq_block = 8

def split_attention(flat_params):
    qkv_weight = flat_params[:3 * D * D].reshape(D, 3 * D)
    offset = 3 * D * D
    out_weight = flat_params[offset:offset + D * D].reshape(D, D)
    offset = offset + D * D
    return (qkv_weight, out_weight, flat_params[offset:offset + 5 * D].reshape(5, D))

def split_ffn(flat_params):
    in_weight = flat_params[:D * FF].reshape(D, FF)
    offset = D * FF
    down_weight = flat_params[offset:offset + FF * D].reshape(FF, D)
    offset = offset + FF * D
    in_bias = flat_params[offset:offset + FF]
    offset = offset + FF
    return (in_weight, down_weight, in_bias, flat_params[offset:offset + 3 * D].reshape(3, D))

def layer_norm(values, gain, shift):
    row_mean = lax.optimization_barrier(jnp.mean(values, -1, keepdims=True))
    centred = values - row_mean
    variance = lax.optimization_barrier(jnp.mean(centred * centred, -1, keepdims=True))
    return centred * lax.rsqrt(variance + norm_eps) * gain + shift

def attend(block):
    query_rows, key_rows, value_rows, seg_ids = block
    scores = jnp.einsum('qhd,khd->hqk', query_rows, key_rows, precision=highest) * HEAD_DIM ** (-0.5)
    scores = low_back(scores)
    same_doc = seg_ids[:, None] == seg_ids[None, :]
    scores = jnp.where(same_doc[None], scores, masked)
    soft_probs = low(jax.nn.softmax(scores, axis=-1))
    return jnp.einsum('hqk,khd->qhd', soft_probs, value_rows, precision=highest)

def forward(values, seg_ids, att_params, ffn_params):
    seq_here = values.shape[0]
    att_params = low(att_params)
    ffn_params = low(ffn_params)
    qkv_weight, out_weight, att_terms = split_attention(att_params)
    query_bias, value_bias, out_bias, gain_one, shift_one = att_terms
    in_weight, down_weight, in_bias, ffn_terms = split_ffn(ffn_params)
    down_bias, gain_two, shift_two = ffn_terms
    rows_in = values.reshape(-1, D)
    bias_qkv = jnp.concatenate([query_bias, jnp.zeros_like(query_bias), value_bias])
    qkv = jnp.dot(rows_in, qkv_weight, precision=highest) + bias_qkv
    qkv = low(low_back(qkv)).reshape(seq_here, LEN, 3, HEADS, HEAD_DIM)
    context = lax.map(jax.checkpoint(attend), (qkv[:, :, 0], qkv[:, :, 1], qkv[:, :, 2], seg_ids))
    context = low(low_back(context.reshape(-1, D)))
    residual = rows_in + low_back(jnp.dot(context, out_weight, precision=highest) + out_bias)
    first_out = layer_norm(residual, gain_one, shift_one)
    ffn_inner = low_back(jnp.dot(low(first_out), in_weight, precision=highest) + in_bias)
    ffn_act = low(jax.nn.gelu(ffn_inner, approximate=False))
    second_in = first_out + low_back(jnp.dot(ffn_act, down_weight, precision=highest) + down_bias)
    return layer_norm(second_in, gain_two, shift_two).reshape(values.shape)

def adam_update(master, first, second, grad):
    first_new = beta_one * first + (1.0 - beta_one) * grad
    second_new = beta_two * second + (1.0 - beta_two) * grad * grad
    fix_one = 1.0 - beta_one ** STEP
    fix_two = 1.0 - beta_two ** STEP
    update = first_new / fix_one / (jnp.sqrt(second_new / fix_two) + adam_eps)
    return (first_new, second_new, update + decay * master)

def reference(tokens, cotangent, segments, live_count, att_master, att_first, att_second, ffn_master, ffn_first, ffn_second):
    seq_count = segments.shape[0]
    seq_order = jnp.arange(seq_count).astype(jnp.int32)
    live_rows = (seq_order % SEQ_DEV < live_count[seq_order // SEQ_DEV]).astype(jnp.float32)
    blocks = seq_count // seq_block
    inputs = tokens.astype(jnp.float32).reshape(blocks, seq_block, LEN, D)
    grads_out = cotangent.astype(jnp.float32).reshape(blocks, seq_block, LEN, D) * live_rows.reshape(blocks, seq_block, 1, 1)
    seg_blocks = segments.reshape(blocks, seq_block, LEN)
    att_params = att_master.astype(jnp.float32)
    ffn_params = ffn_master.astype(jnp.float32)

    def one_block(grad_sums, block):
        block_in, block_grad, block_seg = block

        def layer_fn(values, att_part, ffn_part):
            return forward(values, block_seg, att_part, ffn_part)
        result, pullback = jax.vjp(layer_fn, block_in, att_params, ffn_params)
        grad_in, grad_att, grad_ffn = pullback(block_grad)
        return ((grad_sums[0] + grad_att, grad_sums[1] + grad_ffn), (result.astype(jnp.bfloat16), grad_in.astype(jnp.bfloat16)))
    start_sums = (jnp.zeros(att_master.shape, jnp.float32), jnp.zeros(ffn_master.shape, jnp.float32))
    grad_sums, (outputs, input_grads) = lax.scan(one_block, start_sums, (inputs, grads_out, seg_blocks))
    att_grad, ffn_grad = grad_sums
    att_new = adam_update(att_master, att_first, att_second, att_grad)
    ffn_new = adam_update(ffn_master, ffn_first, ffn_second, ffn_grad)
    return (outputs.reshape(-1, D), input_grads.reshape(-1, D), att_grad, att_new[0], att_new[1], att_new[2], ffn_grad, ffn_new[0], ffn_new[1], ffn_new[2])
```

```python
import functools
import math

import jax
import jax.numpy as jnp
from jax import lax
from jax.experimental import pallas as pl
from jax.experimental.pallas import tpu as pltpu
from jax.sharding import PartitionSpec as P

D = 768
HEADS = 12
HEAD_DIM = 64
FF = 3072
STEP = 10


norm_eps = 1e-05
beta_one = 0.9
beta_two = 0.98
decay = 0.01
adam_eps = 1e-08
masked = -1e30


def split_attention(flat_params):
    qkv_weight = flat_params[: 3 * D * D].reshape(D, 3 * D)
    offset = 3 * D * D
    out_weight = flat_params[offset : offset + D * D].reshape(D, D)
    offset = offset + D * D
    att_terms = flat_params[offset : offset + 5 * D].reshape(5, D).astype(jnp.float32)
    return (qkv_weight, out_weight, att_terms)


def split_ffn(flat_params):
    in_weight = flat_params[: D * FF].reshape(D, FF)
    offset = D * FF
    down_weight = flat_params[offset : offset + FF * D].reshape(FF, D)
    offset = offset + FF * D
    in_bias = flat_params[offset : offset + FF].astype(jnp.float32)
    offset = offset + FF
    ffn_terms = flat_params[offset : offset + 3 * D].reshape(3, D).astype(jnp.float32)
    return (in_weight, down_weight, in_bias, ffn_terms)


def normalize(values, gain, shift):
    row_mean = jnp.mean(values, -1, keepdims=True)
    centred = values - row_mean
    rstd_rows = lax.rsqrt(jnp.mean(centred * centred, -1, keepdims=True) + norm_eps)
    normed = centred * rstd_rows
    return (normed * gain + shift, normed, rstd_rows)


def norm_back(grad_in, normed, rstd_rows, gain):
    scaled = grad_in * gain
    grad_rows = rstd_rows * (
        scaled
        - jnp.mean(scaled, -1, keepdims=True)
        - normed * jnp.mean(scaled * normed, -1, keepdims=True)
    )
    return (grad_rows, jnp.sum(grad_in * normed, 0), jnp.sum(grad_in, 0))


def gelu_slope(values):
    normal_cdf = 0.5 * (1.0 + lax.erf(values * 0.5**0.5))
    return normal_cdf + values * jnp.exp(-0.5 * values * values) * (2.0 * math.pi) ** (-0.5)


def masked_scores(query_rows, key_rows, seg_ids):
    scores = jnp.einsum(
        "qhd,khd->hqk", query_rows, key_rows, preferred_element_type=jnp.float32
    ) * HEAD_DIM ** (-0.5)
    same_doc = seg_ids[:, None] == seg_ids[None, :]
    return jnp.where(same_doc[None], scores, masked)


def attend_forward(block):
    query_rows, key_rows, value_rows, seg_ids = block
    scores = masked_scores(query_rows, key_rows, seg_ids)
    row_top = jnp.max(scores, -1, keepdims=True)
    raised = jnp.exp(scores - row_top)
    row_total = jnp.sum(raised, -1, keepdims=True)
    soft_probs = (raised / row_total).astype(jnp.bfloat16)
    context = jnp.einsum("hqk,khd->qhd", soft_probs, value_rows, preferred_element_type=jnp.float32)
    return (
        context.astype(jnp.bfloat16).reshape(context.shape[0], -1),
        row_top + jnp.log(row_total),
    )


def attend_backward(query_rows, key_rows, value_rows, seg_ids, log_total, grad_context):
    soft_probs = jnp.exp(masked_scores(query_rows, key_rows, seg_ids) - log_total)
    grad_probs = jnp.einsum(
        "qhd,khd->hqk", grad_context, value_rows, preferred_element_type=jnp.float32
    )
    grad_values = jnp.einsum(
        "hqk,qhd->khd",
        soft_probs.astype(jnp.bfloat16),
        grad_context,
        preferred_element_type=jnp.float32,
    )
    grad_scores = soft_probs * (grad_probs - jnp.sum(soft_probs * grad_probs, -1, keepdims=True))
    grad_scores = grad_scores.astype(jnp.bfloat16)
    grad_queries = jnp.einsum(
        "hqk,khd->qhd", grad_scores, key_rows, preferred_element_type=jnp.float32
    ) * HEAD_DIM ** (-0.5)
    grad_keys = jnp.einsum(
        "hqk,qhd->khd", grad_scores, query_rows, preferred_element_type=jnp.float32
    ) * HEAD_DIM ** (-0.5)
    length_here = query_rows.shape[0]
    return jnp.concatenate(
        [
            grad_queries.reshape(length_here, -1),
            grad_keys.reshape(length_here, -1),
            grad_values.reshape(length_here, -1),
        ],
        -1,
    )


def adam_update(master, first, second, grad):
    first_new = beta_one * first + (1.0 - beta_one) * grad
    second_new = beta_two * second + (1.0 - beta_two) * grad * grad
    fix_one = 1.0 - beta_one**STEP
    fix_two = 1.0 - beta_two**STEP
    update = first_new / fix_one / (jnp.sqrt(second_new / fix_two) + adam_eps)
    return (first_new, second_new, update + decay * master)


def general_body(
    tokens,
    cotangent,
    segments,
    live_count,
    att_master,
    att_first,
    att_second,
    ffn_master,
    ffn_first,
    ffn_second,
):
    seq_count = segments.shape[0]
    length = segments.shape[1]
    att_full = lax.all_gather(att_master.astype(jnp.bfloat16), "dp", axis=0, tiled=True)
    qkv_weight, out_weight, att_terms = split_attention(att_full)
    bias_qkv = jnp.concatenate([att_terms[0], jnp.zeros_like(att_terms[0]), att_terms[1]])
    qkv = (jnp.dot(tokens, qkv_weight, preferred_element_type=jnp.float32) + bias_qkv).astype(
        jnp.bfloat16
    )
    head_split = qkv.reshape(seq_count, length, 3, HEADS, HEAD_DIM)
    context, log_total = lax.map(
        attend_forward, (head_split[:, :, 0], head_split[:, :, 1], head_split[:, :, 2], segments)
    )
    context = context.reshape(-1, D)
    residual = (
        tokens.astype(jnp.float32)
        + jnp.dot(context, out_weight, preferred_element_type=jnp.float32)
        + att_terms[2]
    )
    first_out, first_hat, first_rstd = normalize(residual, att_terms[3], att_terms[4])
    ffn_full = lax.all_gather(ffn_master.astype(jnp.bfloat16), "dp", axis=0, tiled=True)
    in_weight, down_weight, in_bias, ffn_terms = split_ffn(ffn_full)
    first_low = first_out.astype(jnp.bfloat16)
    ffn_inner = jnp.dot(first_low, in_weight, preferred_element_type=jnp.float32) + in_bias
    ffn_act = jax.nn.gelu(ffn_inner, approximate=False).astype(jnp.bfloat16)
    second_in = (
        first_out + jnp.dot(ffn_act, down_weight, preferred_element_type=jnp.float32) + ffn_terms[0]
    )
    output, second_hat, second_rstd = normalize(second_in, ffn_terms[1], ffn_terms[2])
    att_back = lax.all_gather(att_master.astype(jnp.bfloat16), "dp", axis=0, tiled=True)
    qkv_weight, out_weight, att_terms = split_attention(att_back)
    ffn_back = lax.all_gather(ffn_master.astype(jnp.bfloat16), "dp", axis=0, tiled=True)
    in_weight, down_weight, in_bias, ffn_terms = split_ffn(ffn_back)

    def microbatch(micro_index, state_now):
        grad_sums, input_grads = state_now

        def take_rows(array_in):
            return lax.dynamic_slice_in_dim(array_in, micro_index * length, length, 0)

        grad_out = take_rows(cotangent).astype(jnp.float32)
        grad_second, grad_gain_two, grad_shift_two = norm_back(
            grad_out, take_rows(second_hat), take_rows(second_rstd), ffn_terms[1]
        )
        grad_down = grad_second.astype(jnp.bfloat16)
        grad_down_bias = jnp.sum(grad_down.astype(jnp.float32), 0)
        grad_down_weight = jnp.dot(
            take_rows(ffn_act).T, grad_down, preferred_element_type=jnp.float32
        )
        grad_act = jnp.dot(grad_down, down_weight.T, preferred_element_type=jnp.float32)
        grad_inner = (grad_act * gelu_slope(take_rows(ffn_inner))).astype(jnp.bfloat16)
        grad_in_bias = jnp.sum(grad_inner.astype(jnp.float32), 0)
        grad_in_weight = jnp.dot(
            take_rows(first_low).T, grad_inner, preferred_element_type=jnp.float32
        )
        grad_first = grad_second + jnp.dot(
            grad_inner, in_weight.T, preferred_element_type=jnp.float32
        )
        grad_residual, grad_gain_one, grad_shift_one = norm_back(
            grad_first, take_rows(first_hat), take_rows(first_rstd), att_terms[3]
        )
        grad_proj = grad_residual.astype(jnp.bfloat16)
        grad_out_bias = jnp.sum(grad_proj.astype(jnp.float32), 0)
        grad_out_weight = jnp.dot(
            take_rows(context).T, grad_proj, preferred_element_type=jnp.float32
        )
        grad_context = jnp.dot(grad_proj, out_weight.T, preferred_element_type=jnp.float32).astype(
            jnp.bfloat16
        )
        this_seq = lax.dynamic_index_in_dim(head_split, micro_index, 0, keepdims=False)
        this_segs = lax.dynamic_index_in_dim(segments, micro_index, 0, keepdims=False)
        this_total = lax.dynamic_index_in_dim(log_total, micro_index, 0, keepdims=False)
        grad_qkv = attend_backward(
            this_seq[:, 0],
            this_seq[:, 1],
            this_seq[:, 2],
            this_segs,
            this_total,
            grad_context.reshape(length, HEADS, HEAD_DIM),
        )
        grad_qkv = grad_qkv.astype(jnp.bfloat16)
        grad_wide = grad_qkv.astype(jnp.float32)
        grad_query_bias = jnp.sum(grad_wide[:, :D], 0)
        grad_value_bias = jnp.sum(grad_wide[:, 2 * D :], 0)
        grad_qkv_weight = jnp.dot(take_rows(tokens).T, grad_qkv, preferred_element_type=jnp.float32)
        grad_tokens = (
            jnp.dot(grad_qkv, qkv_weight.T, preferred_element_type=jnp.float32) + grad_residual
        )
        input_grads = lax.dynamic_update_slice_in_dim(
            input_grads, grad_tokens.astype(jnp.bfloat16), micro_index * length, 0
        )
        terms_now = (
            grad_qkv_weight,
            grad_out_weight,
            grad_query_bias,
            grad_value_bias,
            grad_out_bias,
            grad_gain_one,
            grad_shift_one,
            grad_in_weight,
            grad_down_weight,
            grad_in_bias,
            grad_down_bias,
            grad_gain_two,
            grad_shift_two,
        )
        grad_sums = tuple((running + fresh for running, fresh in zip(grad_sums, terms_now)))
        return (grad_sums, input_grads)

    zero_sums = (
        jnp.zeros((D, 3 * D), jnp.float32),
        jnp.zeros((D, D), jnp.float32),
        jnp.zeros((D,), jnp.float32),
        jnp.zeros((D,), jnp.float32),
        jnp.zeros((D,), jnp.float32),
        jnp.zeros((D,), jnp.float32),
        jnp.zeros((D,), jnp.float32),
        jnp.zeros((D, FF), jnp.float32),
        jnp.zeros((FF, D), jnp.float32),
        jnp.zeros((FF,), jnp.float32),
        jnp.zeros((D,), jnp.float32),
        jnp.zeros((D,), jnp.float32),
        jnp.zeros((D,), jnp.float32),
    )
    zero_inputs = jnp.zeros(tokens.shape, jnp.bfloat16)
    grad_sums, input_grad = lax.fori_loop(0, live_count[0], microbatch, (zero_sums, zero_inputs))
    dp_count = lax.axis_size("dp")
    att_pad = att_master.shape[0] * dp_count - 4 * D * D - 5 * D
    ffn_pad = ffn_master.shape[0] * dp_count - 2 * D * FF - FF - 3 * D
    att_local = jnp.concatenate(
        [
            grad_sums[0].reshape(-1),
            grad_sums[1].reshape(-1),
            grad_sums[2],
            grad_sums[3],
            grad_sums[4],
            grad_sums[5],
            grad_sums[6],
            jnp.zeros((att_pad,), jnp.float32),
        ]
    )
    ffn_local = jnp.concatenate(
        [
            grad_sums[7].reshape(-1),
            grad_sums[8].reshape(-1),
            grad_sums[9],
            grad_sums[10],
            grad_sums[11],
            grad_sums[12],
            jnp.zeros((ffn_pad,), jnp.float32),
        ]
    )
    att_rows, ffn_rows = (
        lax.all_to_all(
            att_local.reshape(dp_count, -1).astype(jnp.bfloat16),
            "dp",
            split_axis=0,
            concat_axis=0,
            tiled=True,
        ).astype(jnp.float32),
        lax.all_to_all(
            ffn_local.reshape(dp_count, -1).astype(jnp.bfloat16),
            "dp",
            split_axis=0,
            concat_axis=0,
            tiled=True,
        ).astype(jnp.float32),
    )
    att_share = jnp.sum(att_rows, 0)
    ffn_share = jnp.sum(ffn_rows, 0)
    att_grad, ffn_grad = (
        lax.psum(att_share.astype(jnp.bfloat16), "rep").astype(jnp.float32),
        lax.psum(ffn_share.astype(jnp.bfloat16), "rep").astype(jnp.float32),
    )
    att_new = adam_update(att_master, att_first, att_second, att_grad)
    ffn_new = adam_update(ffn_master, ffn_first, ffn_second, ffn_grad)
    return (
        output.astype(jnp.bfloat16),
        input_grad,
        att_grad,
        att_new[0],
        att_new[1],
        att_new[2],
        ffn_grad,
        ffn_new[0],
        ffn_new[1],
        ffn_new[2],
    )


MESH_ID = pl.DeviceIdType.MESH


def when(cond, act):
    if cond is None:
        act()
    else:
        pl.when(cond)(act)


class Place:
    def __init__(self, levels):
        self.levels = levels
        d = lax.axis_index("dp")
        c = lax.axis_index("rep")
        self.d, self.c = d, c
        self.z, y, x = d // 4, (d // 2) % 2, d % 2
        x_near, y_near = d + 1 - 2 * x, d + 2 - 4 * y
        self.a_near = x_near + c * (y_near - x_near)
        self.b_near = y_near + c * (x_near - y_near)
        self.far = x_near + y_near - d
        self.a_at = x + c * (y - x)
        self.b_at = y + c * (x - y)
        self.up = (d + 4, c)
        self.down = (d - 4, c)
        self.has_up = self.z < levels - 1
        self.has_down = self.z > 0
        self.across_a = (self.a_near, c)
        self.across_b = (self.b_near, c)
        self.sibling = (d, 1 - c)

    def levels_at(self, distance):
        if distance == 0:
            return [(self.z, None, 0)]
        return [
            (self.z - distance, self.z >= distance, -1),
            (self.z + distance, self.z + distance < self.levels, 1),
        ]

    def at(self, column, level):
        return column + 4 * (level - self.z)

    def along(self, step):
        return (self.up, self.has_up) if step > 0 else (self.down, self.has_down)

    def meet(self, chain):
        barrier = pltpu.get_barrier_semaphore()

        def greet(device):
            pl.semaphore_signal(barrier, inc=1, device_id=device, device_id_type=MESH_ID)

        for device in (self.across_a, self.across_b, self.sibling):
            greet(device)
        count = 3
        edges = [(self.up, self.has_up), (self.down, self.has_down)]
        if chain:
            edges += [((self.d + 1, self.c), self.d < 4 * self.levels - 1), ((self.d - 1, self.c), self.d > 0)]
        for device, there in edges:
            pl.when(there)(functools.partial(greet, device))
            count = count + there.astype(jnp.int32)
        pl.semaphore_wait(barrier, count)


def both(first, second):
    if first is None:
        return second
    return first if second is None else first & second


class Sends:
    def __init__(self):
        self.open = []

    def start(self, cond, make):
        when(cond, lambda: make().start())
        self.open.append((cond, make))

    def finish(self):
        for cond, make in self.open:
            when(cond, lambda make=make: make().wait_send())
        self.open = []


def remote(src, dst, send_sem, recv_sem, device):
    return pltpu.make_async_remote_copy(
        src_ref=src,
        dst_ref=dst,
        send_sem=send_sem,
        recv_sem=recv_sem,
        device_id=device,
        device_id_type=MESH_ID,
    )


class Gather:
    def __init__(self, place, sends, ref, send_sem, recv_sem):
        self.place, self.sends, self.ref = place, sends, ref
        self.send_sem, self.recv_sem = send_sem, recv_sem
        self.half = ref.shape[2] // 2

    def piece(self, chip, core):
        rows = pl.ds(pl.multiple_of(core * self.half, self.half), self.half)
        return self.ref.at[chip, :, rows, :]

    def copy(self, chip, way, device):
        own = self.piece(chip, self.place.c)
        kind = 1 if way == 4 else 0
        return remote(own, own, self.send_sem.at[way, chip], self.recv_sem.at[kind, chip], device)

    def send(self, cond, chip, way, device):
        self.sends.start(cond, lambda: self.copy(chip, way, device))

    def arrived(self, cond, chip, kind=0):
        p = self.place
        part = self.piece(chip, p.c if kind == 0 else 1 - p.c)
        make = lambda: remote(part, part, self.send_sem.at[0, chip], self.recv_sem.at[kind, chip], p.sibling)
        when(cond, lambda: make().wait_recv())

    def own(self):
        p = self.place
        self.send(None, p.d, 3, p.across_b)
        self.send(None, p.d, 2, p.across_a)
        self.send(p.has_up, p.d, 0, p.up)
        self.send(p.has_down, p.d, 1, p.down)

    def line(self, distance):
        p = self.place
        for level, there, step in p.levels_at(distance):
            chip = p.at(p.d, level)
            self.arrived(there, chip)
            onward, more = p.along(-step)
            self.send(both(there, more), chip, 0, onward)
            self.send(there, chip, 3, p.across_b)
            self.send(there, chip, 2, p.across_a)
            self.send(there, chip, 4, p.sibling)

    def over_a(self, distance):
        p = self.place
        for level, there, _ in p.levels_at(distance):
            chip = p.at(p.a_near, level)
            self.arrived(there, chip)
            self.send(there, chip, 3, p.across_b)
            self.send(there, chip, 4, p.sibling)

    def over_b(self, column, distance):
        p = self.place
        for level, there, _ in p.levels_at(distance):
            chip = p.at(column, level)
            self.arrived(there, chip)
            self.send(there, chip, 4, p.sibling)

    def steps(self):
        p = self.place
        todo = [self.own]
        for distance in range(p.levels + 2):
            if 0 < distance < p.levels:
                todo.append(functools.partial(self.line, distance))
            if 0 <= distance - 1 < p.levels:
                todo.append(functools.partial(self.over_a, distance - 1))
            if 0 <= distance - 1 < p.levels:
                todo.append(functools.partial(self.over_b, p.b_near, distance - 1))
            if 0 <= distance - 2 < p.levels:
                todo.append(functools.partial(self.over_b, p.far, distance - 2))
        return todo

    def from_sibling(self):
        p = self.place
        for column in (p.d, p.a_near, p.b_near, p.far):
            for distance in range(p.levels):
                for level, there, _ in p.levels_at(distance):
                    if column is p.d and distance == 0:
                        continue
                    self.arrived(there, p.at(column, level), 1)


class Spread:
    def __init__(self, place, sends, ref, send_sem, recv_sem):
        self.place, self.sends, self.ref = place, sends, ref
        self.send_sem, self.recv_sem = send_sem, recv_sem

    def copy(self, way, device):
        return remote(self.ref, self.ref, self.send_sem.at[way], self.recv_sem, device)

    def wait(self, cond):
        when(cond, lambda: self.copy(0, self.place.sibling).wait_recv())

    def run(self):
        p = self.place
        home = (p.a_at == 1) & (p.b_at == 1)
        self.wait(home & p.has_up)
        self.sends.start(home & p.has_down, lambda: self.copy(0, p.down))
        self.wait((p.a_at == 0) & (p.b_at == 1))
        self.sends.start(home, lambda: self.copy(1, p.across_a))
        self.wait(p.b_at == 0)
        self.sends.start(p.b_at == 1, lambda: self.copy(2, p.across_b))


def shifted(ref, start, rows):
    first, turn = start // 128, start % 128
    here = pltpu.roll(ref[pl.ds(first, rows), :], (128 - turn) % 128, 1)
    after = pltpu.roll(ref[pl.ds(first + 1, rows), :], (128 - turn) % 128, 1)
    lane = lax.broadcasted_iota(jnp.int32, (rows, 128), 1)
    return jnp.where(lane < 128 - turn, here, after)


class Flat:
    def __init__(self, length, chips, parts, split):
        self.length, self.chips, self.parts = length, chips, parts
        self.rows = length // D // parts * parts
        self.slip = length - self.rows * D
        self.deep = self.rows // parts
        self.split = split
        self.lines = self.rows * (D // 128)
        self.most = self.slip * chips
        self.halo = -(-self.most // 1024) * 8
        self.held = -(-length // 1024) * 8
        self.tail_from = (length - self.most) // 1024 * 8
        self.tail = self.held - self.tail_from

    def place_of(self, part, block, split):
        if split:
            return 6 * part + block, 6 * self.parts
        return 6 * self.deep * part + block, 6


class Lead:
    def __init__(self, place, sends, flat, own_ref, long_ref, halo_ref, line_ref, send_sem, recv_sem):
        self.place, self.sends, self.flat = place, sends, flat
        self.own_ref, self.long_ref, self.halo_ref, self.line_ref = own_ref, long_ref, halo_ref, line_ref
        self.send_sem, self.recv_sem = send_sem, recv_sem

    def copy(self):
        f, p = self.flat, self.place
        return remote(
            self.own_ref.at[pl.ds(f.tail_from, f.tail), :],
            self.halo_ref.at[pl.ds(0, f.tail), :],
            self.send_sem,
            self.recv_sem,
            (p.d + 1, p.c),
        )

    def begin(self):
        p, f = self.place, self.flat
        self.sends.start(p.d < f.chips - 1, self.copy)
        self.long_ref[pl.ds(f.halo, f.held), :] = self.own_ref[...]

    def lines(self):
        p, f = self.place, self.flat
        slip = f.slip * p.d
        self.line_ref[...] = shifted(self.long_ref, f.halo * 128 - slip, f.lines)

        def mend():
            self.copy().wait_recv()
            before = shifted(self.halo_ref, f.length - f.tail_from * 128 - slip, f.halo)
            at = lax.broadcasted_iota(jnp.int32, (f.halo, 128), 0) * 128
            at = at + lax.broadcasted_iota(jnp.int32, (f.halo, 128), 1)
            self.line_ref[pl.ds(0, f.halo), :] = jnp.where(at < slip, before, self.line_ref[pl.ds(0, f.halo), :])

        pl.when(p.d > 0)(mend)

    def store(self, out_ref):
        p, f = self.place, self.flat

        def put(split):
            for part in range(f.parts):
                for block in range(D // 128):
                    first, stride = f.place_of(part, block, split)
                    out_ref[p.d, part, :, pl.ds(128 * block, 128)] = self.line_ref[
                        pl.ds(first, f.deep, stride=stride), :
                    ].astype(jnp.bfloat16)

        pl.when(p.d < f.split)(lambda: put(True))
        pl.when(p.d >= f.split)(lambda: put(False))

    def last_rows(self, count):
        f = self.flat
        lines = -(-count * 6 // 8) * 8
        return shifted(self.long_ref, f.halo * 128 + f.length - count * D, lines)


def scratch_lead(flat):
    return [
        pltpu.VMEM((flat.halo + flat.held + 8, 128), jnp.float32),
        pltpu.VMEM((flat.tail + flat.halo + 8, 128), jnp.float32),
        pltpu.VMEM((flat.lines, 128), jnp.float32),
    ]


def gather_kernel(levels, att, ffn, att_ref, ffn_ref, att_out, ffn_out, terms_out, att_w, ffn_w, terms,
                  att_long, att_halo, att_line, ffn_long, ffn_halo, ffn_line, spare,
                  halo_send, halo_recv, att_send, att_recv, ffn_send, ffn_recv, term_send, term_recv, out_sem):
    p = Place(levels)
    p.meet(True)
    sends = Sends()
    lead_a = Lead(p, sends, att, att_ref, att_long, att_halo, att_line, halo_send.at[0], halo_recv.at[0])
    lead_f = Lead(p, sends, ffn, ffn_ref, ffn_long, ffn_halo, ffn_line, halo_send.at[1], halo_recv.at[1])
    lead_a.begin()
    lead_f.begin()
    lead_a.lines()
    lead_a.store(att_w)
    att_go = Gather(p, sends, att_w, att_send, att_recv)
    ffn_go = Gather(p, sends, ffn_w, ffn_send, ffn_recv)
    steps_a, steps_f = att_go.steps(), ffn_go.steps()
    steps_a[0]()

    def last():
        terms[...] = jnp.zeros(terms.shape, terms.dtype)
        for lead, at, count in ((lead_a, 0, 5), (lead_f, 8, 7)):
            rows = lead.last_rows(count)
            spare[pl.ds(0, rows.shape[0]), :] = rows
            for block in range(D // 128):
                terms[pl.ds(at, count), pl.ds(128 * block, 128)] = spare[pl.ds(block, count, stride=6), :]

    pl.when(p.d == att.chips - 1)(last)
    lead_f.lines()
    lead_f.store(ffn_w)
    for step in steps_a[1:3]:
        step()
    steps_f[0]()
    for step in steps_a[3:]:
        step()
    Spread(p, sends, terms, term_send, term_recv).run()
    for step in steps_f[1:]:
        step()
    att_go.from_sibling()
    ffn_go.from_sibling()
    terms_out[...] = terms[...]
    outs = [pltpu.make_async_copy(att_w, att_out, out_sem.at[0]), pltpu.make_async_copy(ffn_w, ffn_out, out_sem.at[1])]
    for copy in outs:
        copy.start()
    sends.finish()
    for copy in outs:
        copy.wait()


def gather_weights(levels, att, ffn, att_lines, ffn_lines):
    vmem = pl.BlockSpec(memory_space=pltpu.VMEM)
    anywhere = pl.BlockSpec(memory_space=pl.ANY)
    chips = att.chips
    att_shape = (chips, att.parts, att.deep, D)
    ffn_shape = (chips, ffn.parts, ffn.deep, D)
    dma = pltpu.SemaphoreType.DMA
    return pl.pallas_call(
        functools.partial(gather_kernel, levels, att, ffn),
        out_shape=(
            jax.ShapeDtypeStruct(att_shape, jnp.bfloat16),
            jax.ShapeDtypeStruct(ffn_shape, jnp.bfloat16),
            jax.ShapeDtypeStruct((16, D), jnp.float32),
        ),
        in_specs=[vmem, vmem],
        out_specs=(anywhere, anywhere, vmem),
        scratch_shapes=[
            pltpu.VMEM(att_shape, jnp.bfloat16),
            pltpu.VMEM(ffn_shape, jnp.bfloat16),
            pltpu.VMEM((16, D), jnp.float32),
            *scratch_lead(att),
            *scratch_lead(ffn),
            pltpu.VMEM((48, 128), jnp.float32),
            dma((2,)),
            dma((2,)),
            dma((5, chips)),
            dma((2, chips)),
            dma((5, chips)),
            dma((2, chips)),
            dma((3,)),
            dma,
            dma((2,)),
        ],
        compiler_params=pltpu.CompilerParams(
            collective_id=1, has_side_effects=True, vmem_limit_bytes=56 * 2**20
        ),
        name="gather_weights",
    )(att_lines, ffn_lines)


class Reduce:
    def __init__(self, place, sends, ref, own_ref, sib_ref, b_ref, a_ref, z_ref, send_sem, recv_sem):
        self.place, self.sends, self.ref, self.own_ref = place, sends, ref, own_ref
        self.sib_ref, self.b_ref, self.a_ref, self.z_ref = sib_ref, b_ref, a_ref, z_ref
        self.send_sem, self.recv_sem = send_sem, recv_sem
        self.half = ref.shape[2] // 2

    def rows(self, core):
        return pl.ds(pl.multiple_of(core * self.half, self.half), self.half)

    def levels(self):
        p = self.place
        return [(p.z + p.levels // 2 + i) % p.levels for i in range(p.levels)]

    def send(self, cond, chip, way, dst, device):
        p = self.place
        core = 1 - p.c if way == 4 else p.c
        src = self.ref.at[chip, :, self.rows(core), :]
        make = lambda: remote(src, dst, self.send_sem.at[way, chip], self.recv_sem.at[way, chip], device)
        self.sends.start(cond, make)

    def add(self, cond, chip, way, src):
        p = self.place

        def act():
            remote(src, src, self.send_sem.at[way, chip], self.recv_sem.at[way, chip], p.sibling).wait_recv()
            for part in range(self.ref.shape[1]):
                at = (chip, part, self.rows(p.c), slice(None))
                self.ref[at] = self.ref[at] + src[part]

        when(cond, act)

    def share(self):
        p = self.place
        for column in (p.far, p.b_near, p.a_near, p.d):
            for level in self.levels():
                chip = p.at(column, level)
                self.send(None, chip, 4, self.sib_ref.at[chip], p.sibling)

    def over_b(self):
        p = self.place
        for kind, column in ((1, p.far), (0, p.b_near)):
            for level in self.levels():
                chip = p.at(column, level)
                self.add(None, chip, 4, self.sib_ref.at[chip])
                self.send(None, chip, 3, self.b_ref.at[kind, level], p.across_b)

    def over_a(self):
        p = self.place
        for level in self.levels():
            chip = p.at(p.a_near, level)
            self.add(None, chip, 4, self.sib_ref.at[chip])
            self.add(None, chip, 3, self.b_ref.at[1, level])
            self.send(None, chip, 2, self.a_ref.at[level], p.across_a)

    def collect(self, cond, chip, level):
        self.add(cond, chip, 4, self.sib_ref.at[chip])
        self.add(cond, chip, 3, self.b_ref.at[0, level])
        self.add(cond, chip, 2, self.a_ref.at[level])

    def line(self):
        p = self.place
        for distance in range(p.levels - 1, 0, -1):
            for level, there, step in p.levels_at(distance):
                chip = p.at(p.d, level)
                way = 0 if step > 0 else 1
                onward, _ = p.along(step)
                _, behind = p.along(-step)
                self.collect(there, chip, level)
                self.add(both(there, behind), chip, way, self.z_ref.at[way, level])
                self.send(there, chip, way, self.z_ref.at[way, level], onward)

    def keep(self):
        p = self.place
        self.collect(None, p.d, p.z)
        for part in range(self.ref.shape[1]):
            self.own_ref[p.c, part] = self.ref[p.d, part, self.rows(p.c), :].astype(jnp.float32)
        for way, there in ((0, p.has_down), (1, p.has_up)):

            def act(way=way):
                src = self.z_ref.at[way, p.z]
                remote(src, src, self.send_sem.at[way, p.d], self.recv_sem.at[way, p.d], p.sibling).wait_recv()
                for part in range(self.ref.shape[1]):
                    self.own_ref[p.c, part] = self.own_ref[p.c, part] + src[part].astype(jnp.float32)

            pl.when(there)(act)

    def hand_over(self, send_sem, recv_sem):
        p = self.place
        own, other = self.own_ref.at[p.c], self.own_ref.at[1 - p.c]
        self.sends.start(None, lambda: remote(own, own, send_sem, recv_sem, p.sibling))
        return lambda: remote(other, other, send_sem, recv_sem, p.sibling).wait_recv()


class Terms:
    def __init__(self, place, sends, ref, got_ref, all_ref, send_sem, recv_sem):
        self.place, self.sends, self.ref, self.got_ref, self.all_ref = place, sends, ref, got_ref, all_ref
        self.send_sem, self.recv_sem = send_sem, recv_sem

    def copy(self, way, core, device):
        return remote(self.ref.at[core], self.got_ref.at[way], self.send_sem.at[way], self.recv_sem.at[way], device)

    def add(self, cond, way):
        def act():
            self.copy(way, 0, self.place.sibling).wait_recv()
            self.ref[self.place.c] = self.ref[self.place.c] + self.got_ref[way]

        when(cond, act)

    def run(self):
        p = self.place
        c = p.c
        self.sends.start(None, lambda: self.copy(0, 1 - c, p.sibling))
        self.add(None, 0)
        self.sends.start(p.b_at == 0, lambda: self.copy(1, c, p.across_b))
        self.add(p.b_at == 1, 1)
        self.sends.start((p.b_at == 1) & (p.a_at == 0), lambda: self.copy(2, c, p.across_a))
        home = (p.b_at == 1) & (p.a_at == 1)
        self.add(home, 2)
        self.add(home & p.has_down, 3)
        self.sends.start(home & p.has_up, lambda: self.copy(3, c, p.up))

    def hand_over(self, last):
        p = self.place
        own = self.ref.at[p.c]
        make = lambda: remote(own, self.all_ref.at[p.c], self.send_sem.at[4], self.recv_sem.at[4], p.sibling)
        self.sends.start(last, make)

        def end():
            make().wait_recv()
            self.all_ref[p.c] = self.ref[p.c]

        return end


class Trail:
    def __init__(self, place, sends, flat, own_ref, line_ref, out_ref, send_sem, recv_sem):
        self.place, self.sends, self.flat = place, sends, flat
        self.own_ref, self.line_ref, self.out_ref = own_ref, line_ref, out_ref
        self.send_sem, self.recv_sem = send_sem, recv_sem

    def copy(self):
        f, p = self.flat, self.place
        return remote(
            self.line_ref.at[pl.ds(0, f.halo), :],
            self.line_ref.at[pl.ds(f.lines, f.halo), :],
            self.send_sem,
            self.recv_sem,
            (p.d - 1, p.c),
        )

    def lines(self):
        p, f = self.place, self.flat
        half = f.deep // 2

        def put(split):
            for core in range(2):
                for part in range(f.parts):
                    for block in range(D // 128):
                        first, stride = f.place_of(part, block, split)
                        first = first + stride * half * core
                        self.line_ref[pl.ds(first, half, stride=stride), :] = self.own_ref[
                            core, part, :, pl.ds(128 * block, 128)
                        ]

        pl.when(p.d < f.split)(lambda: put(True))
        pl.when(p.d >= f.split)(lambda: put(False))
        self.sends.start(p.d > 0, self.copy)

    def last_rows(self, terms_ref, at, count):
        f = self.flat
        for core in range(2):
            for block in range(3):
                self.line_ref[pl.ds(f.lines + 3 * core + block, count, stride=6), :] = terms_ref[
                    core, pl.ds(at, count), pl.ds(128 * block, 128)
                ]

    def out(self):
        p, f = self.place, self.flat
        pl.when(p.d < f.chips - 1)(lambda: self.copy().wait_recv())
        self.out_ref[...] = shifted(self.line_ref, f.slip * p.d, f.held)


def reduce_kernel(levels, att, ffn, att_in, ffn_in, terms_in, att_out, ffn_out, att_g, ffn_g, terms,
                  att_own, att_sib, att_b, att_a, att_z, ffn_own, ffn_sib, ffn_b, ffn_a, ffn_z, terms_got, terms_all,
                  att_line, ffn_line, att_send, att_recv, ffn_send, ffn_recv, term_send, term_recv,
                  own_send, own_recv, halo_send, halo_recv, in_sem):
    p = Place(levels)
    ins = [pltpu.make_async_copy(ffn_in, ffn_g, in_sem.at[0]), pltpu.make_async_copy(att_in, att_g, in_sem.at[1])]
    for copy in ins:
        copy.start()
    p.meet(True)
    sends = Sends()
    terms[...] = terms_in[...]
    add_t = Terms(p, sends, terms, terms_got, terms_all, term_send, term_recv)
    add_f = Reduce(p, sends, ffn_g, ffn_own, ffn_sib, ffn_b, ffn_a, ffn_z, ffn_send, ffn_recv)
    add_a = Reduce(p, sends, att_g, att_own, att_sib, att_b, att_a, att_z, att_send, att_recv)
    for copy in ins:
        copy.wait()
    add_f.share()
    add_a.share()
    for work in (add_f, add_a):
        work.over_b()
    for work in (add_f, add_a):
        work.over_a()
    for work in (add_f, add_a):
        work.line()
    add_t.run()
    add_f.keep()
    end_f = add_f.hand_over(own_send.at[0], own_recv.at[0])
    add_a.keep()
    end_a = add_a.hand_over(own_send.at[1], own_recv.at[1])
    last = p.d == att.chips - 1
    end_t = add_t.hand_over(last)
    trail_f = Trail(p, sends, ffn, ffn_own, ffn_line, ffn_out, halo_send.at[0], halo_recv.at[0])
    trail_a = Trail(p, sends, att, att_own, att_line, att_out, halo_send.at[1], halo_recv.at[1])
    end_f()
    trail_f.lines()
    end_a()
    trail_a.lines()

    def terms_here():
        end_t()
        trail_f.last_rows(terms_all, 8, 7)
        trail_a.last_rows(terms_all, 0, 5)

    pl.when(last)(terms_here)
    trail_f.out()
    trail_a.out()
    sends.finish()


def scratch_reduce(flat, levels):
    half = (flat.parts, flat.deep // 2, D)
    bf16 = jnp.bfloat16
    return [
        pltpu.VMEM((2, *half), jnp.float32),
        pltpu.VMEM((flat.chips, *half), bf16),
        pltpu.VMEM((2, levels, *half), bf16),
        pltpu.VMEM((levels, *half), bf16),
        pltpu.VMEM((2, levels, *half), bf16),
    ]


def reduce_grads(levels, att, ffn, att_grads, ffn_grads, terms):
    vmem = pl.BlockSpec(memory_space=pltpu.VMEM)
    anywhere = pl.BlockSpec(memory_space=pl.ANY)
    chips = att.chips
    dma = pltpu.SemaphoreType.DMA
    return pl.pallas_call(
        functools.partial(reduce_kernel, levels, att, ffn),
        out_shape=(
            jax.ShapeDtypeStruct((att.held, 128), jnp.float32),
            jax.ShapeDtypeStruct((ffn.held, 128), jnp.float32),
        ),
        in_specs=[anywhere, anywhere, vmem],
        out_specs=(vmem, vmem),
        scratch_shapes=[
            pltpu.VMEM((chips, att.parts, att.deep, D), jnp.bfloat16),
            pltpu.VMEM((chips, ffn.parts, ffn.deep, D), jnp.bfloat16),
            pltpu.VMEM((2, 16, D // 2), jnp.float32),
            *scratch_reduce(att, levels),
            *scratch_reduce(ffn, levels),
            pltpu.VMEM((4, 16, D // 2), jnp.float32),
            pltpu.VMEM((2, 16, D // 2), jnp.float32),
            pltpu.VMEM((att.lines + att.halo + 8, 128), jnp.float32),
            pltpu.VMEM((ffn.lines + ffn.halo + 8, 128), jnp.float32),
            dma((5, chips)),
            dma((5, chips)),
            dma((5, chips)),
            dma((5, chips)),
            dma((5,)),
            dma((5,)),
            dma((2,)),
            dma((2,)),
            dma((2,)),
            dma((2,)),
            dma((2,)),
        ],
        compiler_params=pltpu.CompilerParams(
            collective_id=2, has_side_effects=True, vmem_limit_bytes=60 * 2**20
        ),
        name="reduce_grads",
    )(att_grads, ffn_grads, terms)


def as_lines(flat, vector):
    return jnp.pad(vector, (0, flat.held * 128 - flat.length)).reshape(flat.held, 128)


def attend_batch(query_rows, key_rows, value_rows, seg_ids):
    scores = jnp.einsum(
        "sqhd,skhd->shqk", query_rows, key_rows, preferred_element_type=jnp.float32
    ) * HEAD_DIM ** (-0.5)
    same_doc = seg_ids[:, :, None] == seg_ids[:, None, :]
    return jnp.where(same_doc[:, None], scores, masked)


def fast_body(
    levels,
    tokens,
    cotangent,
    segments,
    live_count,
    att_master,
    att_first,
    att_second,
    ffn_master,
    ffn_first,
    ffn_second,
):
    f32, bf16 = jnp.float32, jnp.bfloat16
    seqs, length = segments.shape
    chips = lax.axis_size("dp")
    att = Flat(att_master.shape[0], chips, 3, 3 * chips // 4)
    ffn = Flat(ffn_master.shape[0], chips, 4, chips // 2)
    att_w, ffn_w, terms = gather_weights(levels, att, ffn, as_lines(att, att_master), as_lines(ffn, ffn_master))
    dot = functools.partial(jnp.dot, preferred_element_type=f32)
    qkv_weight = att_w[: att.split].transpose(0, 2, 1, 3).reshape(D, 3 * D)
    out_weight = att_w[att.split :].reshape(D, D)
    in_weight = ffn_w[: ffn.split].transpose(0, 2, 1, 3).reshape(D, FF)
    down_weight = ffn_w[ffn.split :].reshape(FF, D)
    att_terms, in_bias, ffn_terms = terms[:5], terms[8:12].reshape(FF), terms[12:15]
    bias_qkv = jnp.concatenate([att_terms[0], jnp.zeros_like(att_terms[0]), att_terms[1]])
    qkv = (dot(tokens, qkv_weight) + bias_qkv).astype(bf16)
    heads = qkv.reshape(seqs, length, 3, HEADS, HEAD_DIM)
    query_rows, key_rows, value_rows = heads[:, :, 0], heads[:, :, 1], heads[:, :, 2]
    scores = attend_batch(query_rows, key_rows, value_rows, segments)
    row_top = jnp.max(scores, -1, keepdims=True)
    raised = jnp.exp(scores - row_top)
    row_total = jnp.sum(raised, -1, keepdims=True)
    probs = raised / row_total
    context = (
        jnp.einsum("shqk,skhd->sqhd", probs.astype(bf16), value_rows, preferred_element_type=f32)
        .astype(bf16)
        .reshape(-1, D)
    )
    log_total = row_top + jnp.log(row_total)
    residual = tokens.astype(f32) + dot(context, out_weight) + att_terms[2]
    first_out, first_hat, first_rstd = normalize(residual, att_terms[3], att_terms[4])
    first_low = first_out.astype(bf16)
    ffn_inner = dot(first_low, in_weight) + in_bias
    ffn_act = jax.nn.gelu(ffn_inner, approximate=False).astype(bf16)
    second_in = first_out + dot(ffn_act, down_weight) + ffn_terms[0]
    output, second_hat, second_rstd = normalize(second_in, ffn_terms[1], ffn_terms[2])

    live = jnp.arange(seqs * length) // length < live_count[0]
    grad_out = jnp.where(live[:, None], cotangent.astype(f32), 0.0)
    grad_second, grad_gain_two, grad_shift_two = norm_back(grad_out, second_hat, second_rstd, ffn_terms[1])
    grad_down = grad_second.astype(bf16)
    grad_down_bias = jnp.sum(grad_down.astype(f32), 0)
    grad_down_weight = dot(ffn_act.T, grad_down)
    grad_inner = (dot(grad_down, down_weight.T) * gelu_slope(ffn_inner)).astype(bf16)
    grad_in_bias = jnp.sum(grad_inner.astype(f32), 0)
    grad_in_weight = dot(first_low.T, grad_inner)
    grad_first = grad_second + dot(grad_inner, in_weight.T)
    grad_residual, grad_gain_one, grad_shift_one = norm_back(grad_first, first_hat, first_rstd, att_terms[3])
    grad_proj = grad_residual.astype(bf16)
    grad_out_bias = jnp.sum(grad_proj.astype(f32), 0)
    grad_out_weight = dot(context.T, grad_proj)
    grad_context = dot(grad_proj, out_weight.T).astype(bf16).reshape(seqs, length, HEADS, HEAD_DIM)
    probs = jnp.exp(attend_batch(query_rows, key_rows, value_rows, segments) - log_total)
    grad_probs = jnp.einsum("sqhd,skhd->shqk", grad_context, value_rows, preferred_element_type=f32)
    grad_values = jnp.einsum("shqk,sqhd->skhd", probs.astype(bf16), grad_context, preferred_element_type=f32)
    grad_scores = probs * (grad_probs - jnp.sum(probs * grad_probs, -1, keepdims=True))
    grad_scores = grad_scores.astype(bf16)
    scale = HEAD_DIM ** (-0.5)
    grad_queries = jnp.einsum("shqk,skhd->sqhd", grad_scores, key_rows, preferred_element_type=f32) * scale
    grad_keys = jnp.einsum("shqk,sqhd->skhd", grad_scores, query_rows, preferred_element_type=f32) * scale
    grad_qkv = jnp.concatenate([g.reshape(-1, D) for g in (grad_queries, grad_keys, grad_values)], -1).astype(bf16)
    grad_wide = grad_qkv.astype(f32)
    grad_query_bias = jnp.sum(grad_wide[:, :D], 0)
    grad_value_bias = jnp.sum(grad_wide[:, 2 * D :], 0)
    grad_qkv_weight = dot(tokens.T, grad_qkv)
    input_grad = (dot(grad_qkv, qkv_weight.T) + grad_residual).astype(bf16)

    zero = jnp.zeros((D,), f32)
    rows = [grad_query_bias, grad_value_bias, grad_out_bias, grad_gain_one, grad_shift_one, zero, zero, zero]
    rows += [*grad_in_bias.reshape(4, D), grad_down_bias, grad_gain_two, grad_shift_two, zero]
    term_grads = jnp.stack(rows).reshape(16, 2, D // 2).transpose(1, 0, 2)
    att_grads = jnp.concatenate(
        [
            grad_qkv_weight.astype(bf16).reshape(att.split, att.deep, 3, D).transpose(0, 2, 1, 3),
            grad_out_weight.astype(bf16).reshape(chips - att.split, 3, att.deep, D),
        ]
    )
    ffn_grads = jnp.concatenate(
        [
            grad_in_weight.astype(bf16).reshape(ffn.split, ffn.deep, 4, D).transpose(0, 2, 1, 3),
            grad_down_weight.astype(bf16).reshape(chips - ffn.split, 4, ffn.deep, D),
        ]
    )
    att_sum, ffn_sum = reduce_grads(levels, att, ffn, att_grads, ffn_grads, term_grads)
    att_grad = att_sum.reshape(-1)[: att.length]
    ffn_grad = ffn_sum.reshape(-1)[: ffn.length]
    att_new = adam_update(att_master, att_first, att_second, att_grad)
    ffn_new = adam_update(ffn_master, ffn_first, ffn_second, ffn_grad)
    return (output.astype(bf16), input_grad, att_grad, *att_new, ffn_grad, *ffn_new)


def body_for(mesh):
    chips, cores = mesh.shape["dp"], mesh.shape["rep"]
    if chips == 16 and cores == 2:
        return functools.partial(fast_body, chips // 4)
    return general_body


def solution(mesh):
    placed = (
        P(("dp", "rep"), None),
        P(("dp", "rep"), None),
        P(("dp", "rep"), None),
        P(("dp", "rep")),
        P("dp"),
        P("dp"),
        P("dp"),
        P("dp"),
        P("dp"),
        P("dp"),
    )
    return jax.shard_map(
        body_for(mesh),
        mesh=mesh,
        in_specs=placed,
        out_specs=(
            P(("dp", "rep"), None),
            P(("dp", "rep"), None),
            P("dp"),
            P("dp"),
            P("dp"),
            P("dp"),
            P("dp"),
            P("dp"),
            P("dp"),
            P("dp"),
        ),
        check_vma=False,
    )
```

```python
import functools
import math
import types

import jax
import jax.numpy as jnp
from jax import lax
from jax.experimental import pallas as pl
from jax.experimental.pallas import tpu as pltpu
from jax.sharding import PartitionSpec as P

D = 768
HEADS = 12
HEAD_DIM = 64
FF = 3072
STEP = 10


norm_eps = 1e-05
beta_one = 0.9
beta_two = 0.98
decay = 0.01
adam_eps = 1e-08
masked = -1e30


def split_attention(flat_params):
    qkv_weight = flat_params[: 3 * D * D].reshape(D, 3 * D)
    offset = 3 * D * D
    out_weight = flat_params[offset : offset + D * D].reshape(D, D)
    offset = offset + D * D
    att_terms = flat_params[offset : offset + 5 * D].reshape(5, D).astype(jnp.float32)
    return (qkv_weight, out_weight, att_terms)


def split_ffn(flat_params):
    in_weight = flat_params[: D * FF].reshape(D, FF)
    offset = D * FF
    down_weight = flat_params[offset : offset + FF * D].reshape(FF, D)
    offset = offset + FF * D
    in_bias = flat_params[offset : offset + FF].astype(jnp.float32)
    offset = offset + FF
    ffn_terms = flat_params[offset : offset + 3 * D].reshape(3, D).astype(jnp.float32)
    return (in_weight, down_weight, in_bias, ffn_terms)


def normalize(values, gain, shift):
    row_mean = jnp.mean(values, -1, keepdims=True)
    centred = values - row_mean
    rstd_rows = lax.rsqrt(jnp.mean(centred * centred, -1, keepdims=True) + norm_eps)
    normed = centred * rstd_rows
    return (normed * gain + shift, normed, rstd_rows)


def norm_back(grad_in, normed, rstd_rows, gain):
    scaled = grad_in * gain
    grad_rows = rstd_rows * (
        scaled
        - jnp.mean(scaled, -1, keepdims=True)
        - normed * jnp.mean(scaled * normed, -1, keepdims=True)
    )
    return (grad_rows, jnp.sum(grad_in * normed, 0), jnp.sum(grad_in, 0))


def gelu_slope(values):
    normal_cdf = 0.5 * (1.0 + lax.erf(values * 0.5**0.5))
    return normal_cdf + values * jnp.exp(-0.5 * values * values) * (2.0 * math.pi) ** (-0.5)


def masked_scores(query_rows, key_rows, seg_ids):
    scores = jnp.einsum(
        "qhd,khd->hqk", query_rows, key_rows, preferred_element_type=jnp.float32
    ) * HEAD_DIM ** (-0.5)
    same_doc = seg_ids[:, None] == seg_ids[None, :]
    return jnp.where(same_doc[None], scores, masked)


def attend_forward(block):
    query_rows, key_rows, value_rows, seg_ids = block
    scores = masked_scores(query_rows, key_rows, seg_ids)
    row_top = jnp.max(scores, -1, keepdims=True)
    raised = jnp.exp(scores - row_top)
    row_total = jnp.sum(raised, -1, keepdims=True)
    soft_probs = (raised / row_total).astype(jnp.bfloat16)
    context = jnp.einsum("hqk,khd->qhd", soft_probs, value_rows, preferred_element_type=jnp.float32)
    return (
        context.astype(jnp.bfloat16).reshape(context.shape[0], -1),
        row_top + jnp.log(row_total),
    )


def attend_backward(query_rows, key_rows, value_rows, seg_ids, log_total, grad_context):
    soft_probs = jnp.exp(masked_scores(query_rows, key_rows, seg_ids) - log_total)
    grad_probs = jnp.einsum(
        "qhd,khd->hqk", grad_context, value_rows, preferred_element_type=jnp.float32
    )
    grad_values = jnp.einsum(
        "hqk,qhd->khd",
        soft_probs.astype(jnp.bfloat16),
        grad_context,
        preferred_element_type=jnp.float32,
    )
    grad_scores = soft_probs * (grad_probs - jnp.sum(soft_probs * grad_probs, -1, keepdims=True))
    grad_scores = grad_scores.astype(jnp.bfloat16)
    grad_queries = jnp.einsum(
        "hqk,khd->qhd", grad_scores, key_rows, preferred_element_type=jnp.float32
    ) * HEAD_DIM ** (-0.5)
    grad_keys = jnp.einsum(
        "hqk,qhd->khd", grad_scores, query_rows, preferred_element_type=jnp.float32
    ) * HEAD_DIM ** (-0.5)
    length_here = query_rows.shape[0]
    return jnp.concatenate(
        [
            grad_queries.reshape(length_here, -1),
            grad_keys.reshape(length_here, -1),
            grad_values.reshape(length_here, -1),
        ],
        -1,
    )


def adam_update(master, first, second, grad):
    first_new = beta_one * first + (1.0 - beta_one) * grad
    second_new = beta_two * second + (1.0 - beta_two) * grad * grad
    fix_one = 1.0 - beta_one**STEP
    fix_two = 1.0 - beta_two**STEP
    update = first_new / fix_one / (jnp.sqrt(second_new / fix_two) + adam_eps)
    return (first_new, second_new, update + decay * master)


def general_body(
    tokens,
    cotangent,
    segments,
    live_count,
    att_master,
    att_first,
    att_second,
    ffn_master,
    ffn_first,
    ffn_second,
):
    seq_count = segments.shape[0]
    length = segments.shape[1]
    att_full = lax.all_gather(att_master.astype(jnp.bfloat16), "dp", axis=0, tiled=True)
    qkv_weight, out_weight, att_terms = split_attention(att_full)
    bias_qkv = jnp.concatenate([att_terms[0], jnp.zeros_like(att_terms[0]), att_terms[1]])
    qkv = (jnp.dot(tokens, qkv_weight, preferred_element_type=jnp.float32) + bias_qkv).astype(
        jnp.bfloat16
    )
    head_split = qkv.reshape(seq_count, length, 3, HEADS, HEAD_DIM)
    context, log_total = lax.map(
        attend_forward, (head_split[:, :, 0], head_split[:, :, 1], head_split[:, :, 2], segments)
    )
    context = context.reshape(-1, D)
    residual = (
        tokens.astype(jnp.float32)
        + jnp.dot(context, out_weight, preferred_element_type=jnp.float32)
        + att_terms[2]
    )
    first_out, first_hat, first_rstd = normalize(residual, att_terms[3], att_terms[4])
    ffn_full = lax.all_gather(ffn_master.astype(jnp.bfloat16), "dp", axis=0, tiled=True)
    in_weight, down_weight, in_bias, ffn_terms = split_ffn(ffn_full)
    first_low = first_out.astype(jnp.bfloat16)
    ffn_inner = jnp.dot(first_low, in_weight, preferred_element_type=jnp.float32) + in_bias
    ffn_act = jax.nn.gelu(ffn_inner, approximate=False).astype(jnp.bfloat16)
    second_in = (
        first_out + jnp.dot(ffn_act, down_weight, preferred_element_type=jnp.float32) + ffn_terms[0]
    )
    output, second_hat, second_rstd = normalize(second_in, ffn_terms[1], ffn_terms[2])
    att_back = lax.all_gather(att_master.astype(jnp.bfloat16), "dp", axis=0, tiled=True)
    qkv_weight, out_weight, att_terms = split_attention(att_back)
    ffn_back = lax.all_gather(ffn_master.astype(jnp.bfloat16), "dp", axis=0, tiled=True)
    in_weight, down_weight, in_bias, ffn_terms = split_ffn(ffn_back)

    def microbatch(micro_index, state_now):
        grad_sums, input_grads = state_now

        def take_rows(array_in):
            return lax.dynamic_slice_in_dim(array_in, micro_index * length, length, 0)

        grad_out = take_rows(cotangent).astype(jnp.float32)
        grad_second, grad_gain_two, grad_shift_two = norm_back(
            grad_out, take_rows(second_hat), take_rows(second_rstd), ffn_terms[1]
        )
        grad_down = grad_second.astype(jnp.bfloat16)
        grad_down_bias = jnp.sum(grad_down.astype(jnp.float32), 0)
        grad_down_weight = jnp.dot(
            take_rows(ffn_act).T, grad_down, preferred_element_type=jnp.float32
        )
        grad_act = jnp.dot(grad_down, down_weight.T, preferred_element_type=jnp.float32)
        grad_inner = (grad_act * gelu_slope(take_rows(ffn_inner))).astype(jnp.bfloat16)
        grad_in_bias = jnp.sum(grad_inner.astype(jnp.float32), 0)
        grad_in_weight = jnp.dot(
            take_rows(first_low).T, grad_inner, preferred_element_type=jnp.float32
        )
        grad_first = grad_second + jnp.dot(
            grad_inner, in_weight.T, preferred_element_type=jnp.float32
        )
        grad_residual, grad_gain_one, grad_shift_one = norm_back(
            grad_first, take_rows(first_hat), take_rows(first_rstd), att_terms[3]
        )
        grad_proj = grad_residual.astype(jnp.bfloat16)
        grad_out_bias = jnp.sum(grad_proj.astype(jnp.float32), 0)
        grad_out_weight = jnp.dot(
            take_rows(context).T, grad_proj, preferred_element_type=jnp.float32
        )
        grad_context = jnp.dot(grad_proj, out_weight.T, preferred_element_type=jnp.float32).astype(
            jnp.bfloat16
        )
        this_seq = lax.dynamic_index_in_dim(head_split, micro_index, 0, keepdims=False)
        this_segs = lax.dynamic_index_in_dim(segments, micro_index, 0, keepdims=False)
        this_total = lax.dynamic_index_in_dim(log_total, micro_index, 0, keepdims=False)
        grad_qkv = attend_backward(
            this_seq[:, 0],
            this_seq[:, 1],
            this_seq[:, 2],
            this_segs,
            this_total,
            grad_context.reshape(length, HEADS, HEAD_DIM),
        )
        grad_qkv = grad_qkv.astype(jnp.bfloat16)
        grad_wide = grad_qkv.astype(jnp.float32)
        grad_query_bias = jnp.sum(grad_wide[:, :D], 0)
        grad_value_bias = jnp.sum(grad_wide[:, 2 * D :], 0)
        grad_qkv_weight = jnp.dot(take_rows(tokens).T, grad_qkv, preferred_element_type=jnp.float32)
        grad_tokens = (
            jnp.dot(grad_qkv, qkv_weight.T, preferred_element_type=jnp.float32) + grad_residual
        )
        input_grads = lax.dynamic_update_slice_in_dim(
            input_grads, grad_tokens.astype(jnp.bfloat16), micro_index * length, 0
        )
        terms_now = (
            grad_qkv_weight,
            grad_out_weight,
            grad_query_bias,
            grad_value_bias,
            grad_out_bias,
            grad_gain_one,
            grad_shift_one,
            grad_in_weight,
            grad_down_weight,
            grad_in_bias,
            grad_down_bias,
            grad_gain_two,
            grad_shift_two,
        )
        grad_sums = tuple((running + fresh for running, fresh in zip(grad_sums, terms_now)))
        return (grad_sums, input_grads)

    zero_sums = (
        jnp.zeros((D, 3 * D), jnp.float32),
        jnp.zeros((D, D), jnp.float32),
        jnp.zeros((D,), jnp.float32),
        jnp.zeros((D,), jnp.float32),
        jnp.zeros((D,), jnp.float32),
        jnp.zeros((D,), jnp.float32),
        jnp.zeros((D,), jnp.float32),
        jnp.zeros((D, FF), jnp.float32),
        jnp.zeros((FF, D), jnp.float32),
        jnp.zeros((FF,), jnp.float32),
        jnp.zeros((D,), jnp.float32),
        jnp.zeros((D,), jnp.float32),
        jnp.zeros((D,), jnp.float32),
    )
    zero_inputs = jnp.zeros(tokens.shape, jnp.bfloat16)
    grad_sums, input_grad = lax.fori_loop(0, live_count[0], microbatch, (zero_sums, zero_inputs))
    dp_count = lax.axis_size("dp")
    att_pad = att_master.shape[0] * dp_count - 4 * D * D - 5 * D
    ffn_pad = ffn_master.shape[0] * dp_count - 2 * D * FF - FF - 3 * D
    att_local = jnp.concatenate(
        [
            grad_sums[0].reshape(-1),
            grad_sums[1].reshape(-1),
            grad_sums[2],
            grad_sums[3],
            grad_sums[4],
            grad_sums[5],
            grad_sums[6],
            jnp.zeros((att_pad,), jnp.float32),
        ]
    )
    ffn_local = jnp.concatenate(
        [
            grad_sums[7].reshape(-1),
            grad_sums[8].reshape(-1),
            grad_sums[9],
            grad_sums[10],
            grad_sums[11],
            grad_sums[12],
            jnp.zeros((ffn_pad,), jnp.float32),
        ]
    )
    att_rows, ffn_rows = (
        lax.all_to_all(
            att_local.reshape(dp_count, -1).astype(jnp.bfloat16),
            "dp",
            split_axis=0,
            concat_axis=0,
            tiled=True,
        ).astype(jnp.float32),
        lax.all_to_all(
            ffn_local.reshape(dp_count, -1).astype(jnp.bfloat16),
            "dp",
            split_axis=0,
            concat_axis=0,
            tiled=True,
        ).astype(jnp.float32),
    )
    att_share = jnp.sum(att_rows, 0)
    ffn_share = jnp.sum(ffn_rows, 0)
    att_grad, ffn_grad = (
        lax.psum(att_share.astype(jnp.bfloat16), "rep").astype(jnp.float32),
        lax.psum(ffn_share.astype(jnp.bfloat16), "rep").astype(jnp.float32),
    )
    att_new = adam_update(att_master, att_first, att_second, att_grad)
    ffn_new = adam_update(ffn_master, ffn_first, ffn_second, ffn_grad)
    return (
        output.astype(jnp.bfloat16),
        input_grad,
        att_grad,
        att_new[0],
        att_new[1],
        att_new[2],
        ffn_grad,
        ffn_new[0],
        ffn_new[1],
        ffn_new[2],
    )


MESH_ID = pl.DeviceIdType.MESH


def when(cond, act):
    if cond is None:
        act()
    else:
        pl.when(cond)(act)


class Place:
    def __init__(self, levels):
        self.levels = levels
        d = lax.axis_index("dp")
        c = lax.axis_index("rep")
        self.d, self.c = d, c
        self.z, y, x = d // 4, (d // 2) % 2, d % 2
        x_near, y_near = d + 1 - 2 * x, d + 2 - 4 * y
        self.a_near = x_near + c * (y_near - x_near)
        self.b_near = y_near + c * (x_near - y_near)
        self.far = x_near + y_near - d
        self.a_at = x + c * (y - x)
        self.b_at = y + c * (x - y)
        self.up = (d + 4, c)
        self.down = (d - 4, c)
        self.has_up = self.z < levels - 1
        self.has_down = self.z > 0
        self.across_a = (self.a_near, c)
        self.across_b = (self.b_near, c)
        self.sibling = (d, 1 - c)

    def levels_at(self, distance):
        if distance == 0:
            return [(self.z, None, 0)]
        return [
            (self.z - distance, self.z >= distance, -1),
            (self.z + distance, self.z + distance < self.levels, 1),
        ]

    def at(self, column, level):
        return column + 4 * (level - self.z)

    def along(self, step):
        return (self.up, self.has_up) if step > 0 else (self.down, self.has_down)

    def meet(self, chain):
        barrier = pltpu.get_barrier_semaphore()

        def greet(device):
            pl.semaphore_signal(barrier, inc=1, device_id=device, device_id_type=MESH_ID)

        for device in (self.across_a, self.across_b, self.sibling):
            greet(device)
        count = 3
        edges = [(self.up, self.has_up), (self.down, self.has_down)]
        if chain:
            edges += [((self.d + 1, self.c), self.d < 4 * self.levels - 1), ((self.d - 1, self.c), self.d > 0)]
        for device, there in edges:
            pl.when(there)(functools.partial(greet, device))
            count = count + there.astype(jnp.int32)
        pl.semaphore_wait(barrier, count)


def both(first, second):
    if first is None:
        return second
    return first if second is None else first & second


class Sends:
    def __init__(self):
        self.steps, self.closing = [], False

    def go(self, step):
        if not any(step is other for other in self.steps):
            self.steps.append(step)
        step()

    def later(self, step):
        return lambda: self.go(step)

    def start(self, cond, make):
        when(cond, lambda: make().wait_send() if self.closing else make().start())

    def wait(self, cond, make):
        if not self.closing:
            when(cond, lambda: make().wait_recv())

    def finish(self):
        self.closing = True
        for step in self.steps:
            step()


def remote(src, dst, send_sem, recv_sem, device):
    return pltpu.make_async_remote_copy(
        src_ref=src,
        dst_ref=dst,
        send_sem=send_sem,
        recv_sem=recv_sem,
        device_id=device,
        device_id_type=MESH_ID,
    )


class Gather:
    def __init__(self, place, ref, parts, lanes, send_sem, recv_sem, sib_sem):
        self.place, self.ref, self.parts, self.lanes = place, ref, parts, lanes
        self.send_sem, self.recv_sem, self.sib_sem = send_sem, recv_sem, sib_sem
        self.half = ref.shape[2] // 2
        levels = place.levels
        self.leave_up = [k + 1 for k in range(levels)]
        self.leave = (levels, 2 * levels, 4 * levels - 1)

    def rows(self, core):
        return pl.ds(pl.multiple_of(core * self.half, self.half), self.half)

    def piece(self, chip, core):
        return self.ref.at[chip, self.parts, self.rows(core), self.lanes]

    def several(self, count):
        return self.ref.at[pl.ds(0, count), self.parts, pl.ds(0, self.half), self.lanes]

    def send(self, cond, chip, way, device):
        own = self.piece(chip, self.place.c)
        recv = self.sib_sem if way == 4 else self.recv_sem.at[chip]
        when(cond, lambda: remote(own, own, self.send_sem.at[way], recv, device).start())

    def wait(self, cond, part, sem):
        when(cond, lambda: remote(part, part, self.send_sem.at[0], sem, self.place.sibling).wait_recv())

    def arrived(self, cond, chip):
        self.wait(cond, self.piece(chip, self.place.c), self.recv_sem.at[chip])

    def own(self):
        p = self.place
        self.send(p.has_up, p.d, 0, p.up)
        self.send(p.has_down, p.d, 1, p.down)
        self.send(None, p.d, 3, p.across_b)
        self.send(None, p.d, 2, p.across_a)

    def line(self, distance):
        p = self.place
        for level, there, step in p.levels_at(distance):
            chip = p.at(p.d, level)
            self.arrived(there, chip)
            onward, more = p.along(-step)
            self.send(both(there, more), chip, 0 if step < 0 else 1, onward)
            self.send(there, chip, 3, p.across_b)
            self.send(there, chip, 2, p.across_a)
            self.send(there, chip, 4, p.sibling)

    def over_a(self, distance):
        p = self.place
        for level, there, _ in p.levels_at(distance):
            chip = p.at(p.a_near, level)
            self.arrived(there, chip)
            self.send(there, chip, 3, p.across_b)
            self.send(there, chip, 4, p.sibling)

    def over_b(self, distance):
        p = self.place
        for column in (p.b_near, p.far):
            for level, there, _ in p.levels_at(distance):
                chip = p.at(column, level)
                self.arrived(there, chip)
                self.send(there, chip, 4, p.sibling)

    def from_sibling(self):
        self.wait(None, self.several(4 * self.place.levels - 1), self.sib_sem)

    def left(self, cond, way, count):
        part = self.several(count)
        sem = self.send_sem.at[way]
        when(cond, lambda: remote(part, part, sem, self.sib_sem, self.place.sibling).wait_send())

    def finish(self):
        p = self.place
        for level in range(p.levels):
            if level < p.levels - 1:
                self.left(p.z == level, 0, self.leave_up[level])
            if level > 0:
                self.left(p.z == level, 1, self.leave_up[p.levels - 1 - level])
        for way, count in zip((2, 3, 4), self.leave):
            self.left(None, way, count)


class Plane(Gather):
    def __init__(self, place, ref, parts, lanes, send_sem, recv_sem, sib_sem):
        super().__init__(place, ref, parts, lanes, send_sem, recv_sem, sib_sem)
        self.leave_up = [4 * count for count in self.leave_up]
        self.leave = (1, 2, 4 * place.levels - 1)
        self.from_a, self.from_b = place.levels, place.levels + 1

    def send(self, cond, chip, way, device):
        own = self.piece(chip, self.place.c)
        recv = self.sib_sem if way == 4 else self.recv_sem.at[self.from_a if way == 2 else self.from_b]
        when(cond, lambda: remote(own, own, self.send_sem.at[way], recv, device).start())

    def own(self):
        p = self.place
        self.send(None, p.d, 2, p.across_a)
        self.send(None, p.d, 3, p.across_b)

    def near(self):
        p = self.place
        self.wait(None, self.piece(p.a_near, p.c), self.recv_sem.at[self.from_a])
        self.send(None, p.a_near, 3, p.across_b)
        self.send(None, p.a_near, 4, p.sibling)

    def sheet(self, level):
        return self.ref.at[pl.ds(4 * level, 4), self.parts, self.rows(self.place.c), self.lanes]

    def send_sheet(self, cond, level, way, device):
        own = self.sheet(level)
        recv = self.sib_sem if way == 4 else self.recv_sem.at[level]
        when(cond, lambda: remote(own, own, self.send_sem.at[way], recv, device).start())

    def complete(self):
        p = self.place
        self.wait(None, self.several(2), self.recv_sem.at[self.from_b])
        self.send_sheet(p.has_up, p.z, 0, p.up)
        self.send_sheet(p.has_down, p.z, 1, p.down)
        for chip in (p.b_near, p.far):
            self.send(None, chip, 4, p.sibling)

    def line(self, distance):
        p = self.place
        for level, there, step in p.levels_at(distance):
            self.wait(there, self.sheet(level), self.recv_sem.at[level])
            onward, more = p.along(-step)
            self.send_sheet(both(there, more), level, 0 if step < 0 else 1, onward)
            self.send_sheet(there, level, 4, p.sibling)


def steps_of(go, plane):
    levels = go.place.levels
    todo = [functools.partial(go.line, 1), plane.near, functools.partial(go.over_a, 0), plane.complete]
    for distance in range(2, levels):
        todo.append(functools.partial(go.line, distance))
        todo.append(functools.partial(go.over_a, distance - 1))
        todo.append(functools.partial(plane.line, distance - 1))
    todo.append(functools.partial(go.over_a, levels - 1))
    todo.append(functools.partial(go.over_b, 0))
    todo.append(functools.partial(plane.line, levels - 1))
    return todo + [functools.partial(go.over_b, distance) for distance in range(1, levels)]


class Spread:
    def __init__(self, place, sends, ref, send_sem, recv_sem):
        self.place, self.sends, self.ref = place, sends, ref
        self.send_sem, self.recv_sem = send_sem, recv_sem

    def copy(self, way, device):
        return remote(self.ref, self.ref, self.send_sem.at[way], self.recv_sem, device)

    def wait(self, cond):
        self.sends.wait(cond, lambda: self.copy(0, self.place.sibling))

    def run(self):
        p = self.place
        home = (p.a_at == 1) & (p.b_at == 1)
        self.wait(home & p.has_up)
        self.sends.start(home & p.has_down, lambda: self.copy(0, p.down))
        self.wait((p.a_at == 0) & (p.b_at == 1))
        self.sends.start(home, lambda: self.copy(1, p.across_a))
        self.wait(p.b_at == 0)
        self.sends.start(p.b_at == 1, lambda: self.copy(2, p.across_b))


def shifted(ref, start, rows):
    first, turn = start // 128, start % 128
    here = pltpu.roll(ref[pl.ds(first, rows), :], (128 - turn) % 128, 1)
    after = pltpu.roll(ref[pl.ds(first + 1, rows), :], (128 - turn) % 128, 1)
    lane = lax.broadcasted_iota(jnp.int32, (rows, 128), 1)
    return jnp.where(lane < 128 - turn, here, after)


class Flat:
    def __init__(self, length, chips, parts, split, turned):
        self.length, self.chips, self.parts, self.turned = length, chips, parts, turned
        self.rows = length // D // parts * parts
        self.slip = length - self.rows * D
        self.deep = self.rows // parts
        self.split = split
        self.lines = self.rows * (D // 128)
        self.most = self.slip * chips
        self.halo = -(-self.most // 1024) * 8
        self.held = -(-length // 1024) * 8
        self.tail_from = (length - self.most) // 1024 * 8
        self.tail = self.held - self.tail_from

    def place_of(self, part, block, split):
        if split:
            return 6 * part + block, 6 * self.parts
        return 6 * self.deep * part + block, 6


class Lead:
    def __init__(self, place, sends, flat, long_ref, halo_ref, line_ref, send_sem, recv_sem):
        self.place, self.sends, self.flat = place, sends, flat
        self.long_ref, self.halo_ref, self.line_ref = long_ref, halo_ref, line_ref
        self.send_sem, self.recv_sem = send_sem, recv_sem

    def copy(self):
        f, p = self.flat, self.place
        return remote(
            self.long_ref.at[pl.ds(f.halo + f.tail_from, f.tail), :],
            self.halo_ref.at[pl.ds(0, f.tail), :],
            self.send_sem,
            self.recv_sem,
            (p.d + 1, p.c),
        )

    def begin(self):
        self.sends.start(self.place.d < self.flat.chips - 1, self.copy)

    def lines(self):
        p, f = self.place, self.flat
        slip = f.slip * p.d
        self.line_ref[pl.ds(0, f.lines), :] = shifted(self.long_ref, f.halo * 128 - slip, f.lines)

        def mend():
            self.copy().wait_recv()
            before = shifted(self.halo_ref, f.length - f.tail_from * 128 - slip, f.halo)
            at = lax.broadcasted_iota(jnp.int32, (f.halo, 128), 0) * 128
            at = at + lax.broadcasted_iota(jnp.int32, (f.halo, 128), 1)
            self.line_ref[pl.ds(0, f.halo), :] = jnp.where(at < slip, before, self.line_ref[pl.ds(0, f.halo), :])

        pl.when(p.d > 0)(mend)

    def store(self, out_ref):
        p, f = self.place, self.flat

        def put(split):
            for part in range(f.parts):
                for block in range(D // 128):
                    first, stride = f.place_of(part, block, split)
                    out_ref[p.d, part, :, pl.ds(128 * block, 128)] = self.line_ref[
                        pl.ds(first, f.deep, stride=stride), :
                    ].astype(jnp.bfloat16)

        pl.when(p.d < f.split)(lambda: put(True))
        pl.when(p.d >= f.split)(lambda: put(False))

    def last_rows(self, count):
        f = self.flat
        lines = -(-count * 6 // 8) * 8
        return shifted(self.long_ref, f.halo * 128 + f.length - count * D, lines)


class Reduce:
    def __init__(self, place, parts, chips, batches, view, slots, extra, kept, send_sem, recv_sem, whole=None):
        self.place, self.parts, self.batches = place, parts, batches
        self.view, self.slots, self.extra, self.kept = view, slots, extra, kept
        self.send_sem, self.recv_sem, self.whole = send_sem, recv_sem, whole
        self.levels = [level for batch in batches for level in batch]
        self.from_b, self.from_a = chips, chips + 2 * place.levels
        self.from_z = chips + 3 * place.levels

    @staticmethod
    def semaphores(batches):
        return 4 * len(batches) + 2 * sum(map(len, batches))

    def arrival(self, kind, batch):
        return self.recv_sem.at[4 * batch + kind]

    def along(self, way, level):
        return self.recv_sem.at[4 * len(self.batches) + 2 * self.levels.index(level) + way]

    def wait(self, part, sem):
        remote(part, part, self.send_sem.at[0], sem, self.place.sibling).wait_recv()

    def send(self, cond, chip, way, dst, recv, device):
        p = self.place
        src = self.view(chip, 1 - p.c if way == 4 else p.c)
        when(cond, lambda: remote(src, dst, self.send_sem.at[way], recv, device).start())

    def add(self, chip, src):
        here = self.view(chip, self.place.c)
        for part in range(self.parts):
            here[part] = here[part] + src[part]

    def share(self, batch):
        p = self.place
        recv = self.arrival(0, batch)
        if self.whole is not None:
            src, dst = self.whole
            remote(src, dst, self.send_sem.at[4], recv, p.sibling).start()
            return
        for level in self.batches[batch]:
            for column in (p.far, p.b_near, p.a_near, p.d):
                chip = p.at(column, level)
                self.send(None, chip, 4, self.slots(chip, 1), recv, p.sibling)

    def over_b(self, batch):
        p = self.place
        levels = self.batches[batch]
        self.wait(self.slots(4 * levels[0], 4 * len(levels)), self.arrival(0, batch))
        for kind, column in ((1, p.far), (0, p.b_near)):
            for level in levels:
                chip = p.at(column, level)
                self.add(chip, self.slots(chip, 1))
                dst = self.slots(self.from_b + p.levels * kind + level, 1)
                self.send(None, chip, 3, dst, self.arrival(1 + kind, batch), p.across_b)

    def over_a(self, batch):
        p = self.place
        levels = self.batches[batch]
        first = self.from_b + p.levels
        self.wait(self.slots(first + levels[0], len(levels)), self.arrival(2, batch))
        for level in levels:
            chip = p.at(p.a_near, level)
            self.add(chip, self.slots(chip, 1))
            self.add(chip, self.slots(first + level, 1))
            self.send(None, chip, 2, self.slots(self.from_a + level, 1), self.arrival(3, batch), p.across_a)

    def collect(self, batch):
        p = self.place
        levels = self.batches[batch]
        self.wait(self.slots(self.from_b + levels[0], len(levels)), self.arrival(1, batch))
        self.wait(self.slots(self.from_a + levels[0], len(levels)), self.arrival(3, batch))
        for level in levels:
            chip = p.at(p.d, level)
            for first in (0, self.from_b, self.from_a):
                self.add(chip, self.slots(first + level if first else chip, 1))

    def pass_on(self, here, level, way, waits, dst, device):
        p = self.place
        chip = p.at(p.d, level)
        slot = self.slots(self.from_z + level, 1)

        def act():
            if waits:
                self.wait(slot, self.along(way, level))
                self.add(chip, slot)
            self.send(None, chip, way, dst, self.along(way, level), device)

        pl.when(here)(act)

    def line(self, distance, batch):
        p = self.place
        for level in self.batches[batch]:
            slot = self.slots(self.from_z + level, 1)
            if level >= distance:
                self.pass_on(p.z == level - distance, level, 0, level > distance, slot, p.up)
            if level + distance < p.levels:
                dst = slot if distance > 1 else self.extra
                self.pass_on(p.z == level + distance, level, 1, level + distance < p.levels - 1, dst, p.down)

    def keep(self):
        p = self.place
        own = self.kept(p.c)

        def at(level):
            here = self.view(p.d, p.c)
            for part in range(self.parts):
                own[part] = here[part].astype(jnp.float32)
            sources = [(0, self.slots(self.from_z + level, 1))] if level > 0 else []
            sources += [(1, self.extra)] if level < p.levels - 1 else []
            for way, src in sources:
                self.wait(src, self.along(way, level))
                for part in range(self.parts):
                    own[part] = own[part] + src[part].astype(jnp.float32)

        for level in self.levels:
            pl.when(p.z == level)(functools.partial(at, level))

    def left(self, cond, way, count):
        part = self.slots(0, count)
        sem = self.send_sem.at[way]
        when(cond, lambda: remote(part, part, sem, self.recv_sem.at[0], self.place.sibling).wait_send())

    def finish(self):
        p = self.place
        count = len(self.levels)
        for way, pieces in ((4, 4 * count), (3, 2 * count), (2, count)):
            self.left(None, way, pieces)
        for z in range(p.levels):
            for way, pieces in enumerate((sum(n > z for n in self.levels), sum(n < z for n in self.levels))):
                if pieces:
                    self.left(p.z == z, way, pieces)


def handed(place, own_ref, core, send_sem, recv_sem):
    own = own_ref.at[core]
    return remote(own, own, send_sem, recv_sem, place.sibling)


class Terms:
    def __init__(self, place, sends, ref, got_ref, all_ref, send_sem, recv_sem):
        self.place, self.sends, self.ref, self.got_ref, self.all_ref = place, sends, ref, got_ref, all_ref
        self.send_sem, self.recv_sem = send_sem, recv_sem

    def copy(self, way, core, device):
        return remote(self.ref.at[core], self.got_ref.at[way], self.send_sem.at[way], self.recv_sem.at[way], device)

    def add(self, cond, way):
        if self.sends.closing:
            return

        def act():
            self.copy(way, 0, self.place.sibling).wait_recv()
            self.ref[self.place.c] = self.ref[self.place.c] + self.got_ref[way]

        when(cond, act)

    def share(self):
        self.sends.start(None, lambda: self.copy(0, 1 - self.place.c, self.place.sibling))

    def over_b(self):
        p = self.place
        self.add(None, 0)
        self.sends.start(p.b_at == 0, lambda: self.copy(1, p.c, p.across_b))

    def over_a(self):
        p = self.place
        self.add(p.b_at == 1, 1)
        self.sends.start((p.b_at == 1) & (p.a_at == 0), lambda: self.copy(2, p.c, p.across_a))

    def line(self, distance):
        p = self.place
        home = (p.b_at == 1) & (p.a_at == 1) & (p.z == p.levels - 1 - distance)
        self.add(home, 2)
        if distance < p.levels - 1:
            self.add(home, 3)
        if distance > 0:
            self.sends.start(home, lambda: self.copy(3, p.c, p.up))

    def final(self):
        return remote(
            self.ref.at[self.place.c],
            self.all_ref.at[self.place.c],
            self.send_sem.at[4],
            self.recv_sem.at[4],
            self.place.sibling,
        )

    def hand_over(self):
        p = self.place
        self.sends.start(p.d == 4 * p.levels - 1, self.final)

    def take_over(self):
        self.final().wait_recv()
        self.all_ref[self.place.c] = self.ref[self.place.c]


class Trail:
    def __init__(self, place, sends, flat, own_ref, line_ref, out_ref, send_sem, recv_sem):
        self.place, self.sends, self.flat = place, sends, flat
        self.own_ref, self.line_ref, self.out_ref = own_ref, line_ref, out_ref
        self.send_sem, self.recv_sem = send_sem, recv_sem

    def copy(self):
        f, p = self.flat, self.place
        return remote(
            self.line_ref.at[pl.ds(0, f.halo), :],
            self.line_ref.at[pl.ds(f.lines, f.halo), :],
            self.send_sem,
            self.recv_sem,
            (p.d - 1, p.c),
        )

    def lines(self):
        p, f = self.place, self.flat
        half = f.deep // 2

        def put(split):
            for core in range(2):
                for part in range(f.parts):
                    for block in range(D // 128):
                        first, stride = f.place_of(part, block, split)
                        first = first + stride * half * core
                        self.line_ref[pl.ds(first, half, stride=stride), :] = self.own_ref[
                            core, part, :, pl.ds(128 * block, 128)
                        ]

        def put_turned():
            for j in range(f.rows // 128):
                blocks = []
                for i in range(D // f.deep):
                    lanes = pl.ds(128 * (3 * (i % 2) + j), 128)
                    blocks += [self.own_ref[core, i // 2, :, lanes] for core in range(2)]
                turned = jnp.concatenate(blocks, 0).T
                for block in range(D // 128):
                    first = 6 * 128 * j + block
                    self.line_ref[pl.ds(first, 128, stride=6), :] = turned[:, 128 * block : 128 * (block + 1)]

        pl.when(p.d < f.split)(lambda: put(True))
        pl.when(p.d >= f.split)(put_turned if f.turned else lambda: put(False))

    def pass_back(self):
        self.sends.start(self.place.d > 0, self.copy)

    def last_rows(self, terms_ref, at, count):
        f = self.flat
        for core in range(2):
            for block in range(3):
                self.line_ref[pl.ds(f.lines + 3 * core + block, count, stride=6), :] = terms_ref[
                    core, pl.ds(at, count), pl.ds(128 * block, 128)
                ]

    def out(self):
        p, f = self.place, self.flat
        pl.when(p.d < f.chips - 1)(lambda: self.copy().wait_recv())
        self.out_ref[pl.ds(0, f.held), :] = shifted(self.line_ref, f.slip * p.d, f.held)


def dot(a, b):
    return jnp.dot(a, b, preferred_element_type=jnp.float32)


def dot_nt(a, b):
    return lax.dot_general(a, b, (((1,), (1,)), ((), ())), preferred_element_type=jnp.float32)


def square(values):
    return values.reshape(D, D)


def tile(index, size):
    return pl.ds(pl.multiple_of(index * size, size), size)


def loop(count, step, beside=()):
    def body(i, _):
        step(i)
        for at, act in beside:
            pl.when(i == at)(act)
        return 0

    lax.fori_loop(0, count, body, 0)


TILE = 256


class Layer:
    def __init__(self, refs, att_split, ffn_split, seqs, length):
        self.__dict__.update(refs)
        self.att_split, self.ffn_split = att_split, ffn_split
        self.seqs, self.length = seqs, length
        self.tiles = seqs * length // TILE

    def whole(self, blocks, part):
        count = blocks.shape[0] // 4
        return blocks[pl.ds(count * part, count)].reshape(self.seqs * self.length, D)

    def some(self, blocks, part, r):
        count = TILE // blocks.shape[1]
        return pl.ds(blocks.shape[0] // 4 * part + count * r, count)

    def qkv_weight(self, part):
        return square(self.att_w[pl.ds(0, self.att_split), part])

    def out_weight(self):
        return square(self.att_w[pl.ds(self.att_split, self.att_w.shape[0] - self.att_split)])

    def in_weight(self, part):
        return square(self.ffn_w[pl.ds(0, self.ffn_split), part])

    def down_weight(self, part):
        return square(self.ffn_w[pl.ds(self.ffn_split + 2 * part, 2)])

    def term(self, row):
        return self.terms[pl.ds(row, 1), :]

    def add_term(self, row, values):
        self.term_grads[pl.ds(row, 1), :] += jnp.sum(values, 0, keepdims=True)


    def qkv(self, beside=()):
        def step(r):
            rows = tile(r, TILE)
            x = self.tok[rows, :]
            queries = (dot(x, self.qkv_weight(0)) + self.term(0)).astype(jnp.bfloat16)
            self.heads[0, rows, :] = queries * HEAD_DIM ** (-0.5)
            self.heads[1, rows, :] = dot(x, self.qkv_weight(1)).astype(jnp.bfloat16)
            self.heads[2, rows, :] = (dot(x, self.qkv_weight(2)) + self.term(1)).astype(jnp.bfloat16)

        loop(self.tiles, step, beside)

    def make_bias(self):
        for seq in range(self.seqs):
            same = self.seg_col[:, seq : seq + 1] == self.seg_row[seq : seq + 1, :]
            self.bias[pl.ds(seq * self.length, self.length), :] = jnp.where(same, 0.0, masked)

    def lane_half(self, half):
        lane = lax.broadcasted_iota(jnp.int32, (self.length, 2 * HEAD_DIM), 1)
        return (lane // HEAD_DIM) == half

    def attend(self, beside=()):
        self.make_bias()

        def step(i):
            seq, pair = i // (HEADS // 2), i % (HEADS // 2)
            lanes = tile(pair, 2 * HEAD_DIM)
            rows = tile(seq, self.length)
            queries, keys, values = (self.heads[j, rows, lanes] for j in range(3))
            values_t = values.T
            parts = []
            for half in range(2):
                own = jnp.where(self.lane_half(half), queries, jnp.zeros_like(queries))
                scores = dot_nt(keys, own) + self.bias[rows, :]
                top = jnp.max(scores, 0, keepdims=True)
                raised = jnp.exp(scores - top)
                total = jnp.sum(raised, 0, keepdims=True)
                probs = (raised * (1.0 / total)).astype(jnp.bfloat16)
                self.totals[pl.ds(HEADS * seq + 2 * pair + half, 1), :] = top + jnp.log(total)
                parts.append(dot(values_t[HEAD_DIM * half : HEAD_DIM * (half + 1)], probs))
            both_t = jnp.concatenate(parts, 0).astype(jnp.bfloat16)
            self.ctx_t[lanes, rows] = both_t
            self.ctx[rows, lanes] = both_t.T

        loop(self.seqs * HEADS // 2, step, beside)

    def first_norm(self, beside=()):
        def step(r):
            rows = tile(r, TILE)
            residual = self.tok[rows, :].astype(jnp.float32) + dot(self.ctx[rows, :], self.out_weight()) + self.term(2)
            first, normed, rstd = normalize(residual, self.term(3), self.term(4))
            self.hat[rows, :] = normed
            self.rstd[rows, :] = rstd
            self.low_t[:, rows] = first.astype(jnp.bfloat16).T

        loop(self.tiles, step, beside)

    def feed(self, beside=()):
        def step(r):
            rows = tile(r, TILE)
            first = self.hat[rows, :] * self.term(3) + self.term(4)
            low = first.astype(jnp.bfloat16)
            second = first + self.term(12)
            for part in range(4):
                inner = dot(low, self.in_weight(part)) + self.term(8 + part)
                cdf, slope = gelu_parts(inner)
                act = (inner * cdf).astype(jnp.bfloat16)
                self.act[self.some(self.act, part, r)] = act.reshape(-1, self.act.shape[1], D)
                slope = slope.astype(jnp.bfloat16).reshape(-1, self.slope.shape[1], D)
                self.slope[self.some(self.slope, part, r)] = slope
                second = second + dot(act, self.down_weight(part))
            out, normed, rstd = normalize(second, self.term(13), self.term(14))
            seq = r // (self.length // TILE)
            grad_out = self.cot[rows, :].astype(jnp.float32) * self.live[pl.ds(seq, 1), 0:1]
            self.out[rows, :] = out.astype(jnp.bfloat16)
            scaled = grad_out * self.term(13)
            grad = rstd * (
                scaled
                - jnp.mean(scaled, -1, keepdims=True)
                - normed * jnp.mean(scaled * normed, -1, keepdims=True)
            )
            self.add_term(13, grad_out * normed)
            self.add_term(14, grad_out)
            grad_down = grad.astype(jnp.bfloat16)
            self.add_term(12, grad_down.astype(jnp.float32))
            self.grad[rows, :] = grad
            self.down[rows, :] = grad_down
            self.down_t[:, rows] = grad_down.T

        loop(self.tiles, step, beside)


    def hidden_back(self, part, beside=()):
        def step(r):
            rows = tile(r, TILE)
            grad_act = dot_nt(self.down[rows, :], self.down_weight(part))
            at = self.some(self.slope, part, r)
            slope = self.slope[at].reshape(TILE, D).astype(jnp.float32)
            inner = (grad_act * slope).astype(jnp.bfloat16)
            self.slope[at] = inner.reshape(-1, self.slope.shape[1], D)
            self.add_term(8 + part, inner.astype(jnp.float32))

        loop(self.tiles, step, beside)

    def down_grads(self, part, beside=()):
        deep = self.ffn_w.shape[2]
        first = self.ffn_split + 2 * part

        def step(m):
            grads = dot(self.down_t[tile(m, 2 * deep), :], self.whole(self.act, part)).astype(jnp.bfloat16)
            for owner in range(2):
                for block in range(6):
                    at = 128 * (3 * owner + block % 3)
                    self.ffn_w[first + owner, m, :, pl.ds(128 * block, 128)] = grads[
                        deep * (block // 3) : deep * (block // 3 + 1), at : at + 128
                    ]

        loop(4, step, beside)

    def in_back(self, part, beside=()):
        def step(r):
            rows = tile(r, TILE)
            self.grad[rows, :] += dot_nt(
                self.slope[self.some(self.slope, part, r)].reshape(TILE, D), self.in_weight(part)
            )

        loop(self.tiles, step, beside)

    def in_grads(self, part, beside=()):
        deep = self.ffn_w.shape[2]

        def step(m):
            grads = dot(self.low_t[tile(m, 2 * deep), :], self.whole(self.slope, part)).astype(jnp.bfloat16)
            self.ffn_w[pl.ds(2 * m, 2), part] = grads.reshape(2, deep, D)

        loop(4, step, beside)

    def first_back(self, beside=()):
        def step(r):
            rows = tile(r, TILE)
            grad_first, normed = self.grad[rows, :], self.hat[rows, :]
            scaled = grad_first * self.term(3)
            grad = self.rstd[rows, :] * (
                scaled
                - jnp.mean(scaled, -1, keepdims=True)
                - normed * jnp.mean(scaled * normed, -1, keepdims=True)
            )
            self.add_term(3, grad_first * normed)
            self.add_term(4, grad_first)
            proj = grad.astype(jnp.bfloat16)
            self.add_term(2, proj.astype(jnp.float32))
            self.grad[rows, :] = grad
            shape = (-1, self.act.shape[1], D)
            self.act[self.some(self.act, 3, r)] = proj.reshape(shape)
            grad_context = dot_nt(proj, self.out_weight()).astype(jnp.bfloat16)
            self.act[self.some(self.act, 0, r)] = grad_context.reshape(shape)
            self.tok_t[:, rows] = self.tok[rows, :].T

        loop(self.tiles, step, beside)

    def out_grads(self, beside=()):
        def step(m):
            grads = dot(self.ctx_t[tile(m, 192), :], self.whole(self.act, 3)).astype(jnp.bfloat16)
            self.att_w[self.att_split + m] = grads.reshape(self.att_w.shape[1:])

        loop(4, step, beside)

    def attend_back(self, group, beside=()):
        def step(i):
            seq, pair = i % self.seqs, 2 * group + i // self.seqs
            lanes = tile(pair, 2 * HEAD_DIM)
            rows = tile(seq, self.length)
            count = self.length // self.act.shape[1]
            queries, keys, values = (self.heads[j, rows, lanes] for j in range(3))
            grads = self.act[pl.ds(count * seq, count), :, lanes].reshape(self.length, 2 * HEAD_DIM)
            keys_t = keys.T
            parts = []
            grad_keys = grad_values = 0.0
            for half in range(2):
                here = self.lane_half(half)
                own = jnp.where(here, queries, jnp.zeros_like(queries))
                own_grads = jnp.where(here, grads, jnp.zeros_like(grads))
                total = self.totals[pl.ds(HEADS * seq + 2 * pair + half, 1), :]
                probs = jnp.exp(dot_nt(keys, own) + self.bias[rows, :] - total)
                grad_values = grad_values + dot(probs.astype(jnp.bfloat16), own_grads)
                grad_probs = dot_nt(values, own_grads)
                row_sum = jnp.sum(probs * grad_probs, 0, keepdims=True)
                grad_scores = (probs * (grad_probs - row_sum)).astype(jnp.bfloat16)
                grad_keys = grad_keys + dot(grad_scores, own)
                parts.append(dot(keys_t[HEAD_DIM * half : HEAD_DIM * (half + 1)], grad_scores))
            grad_queries = (jnp.concatenate(parts, 0) * HEAD_DIM ** (-0.5)).astype(jnp.bfloat16).T
            grad_values = grad_values.astype(jnp.bfloat16)
            self.heads[0, rows, lanes] = grad_queries
            self.heads[1, rows, lanes] = grad_keys.astype(jnp.bfloat16)
            self.heads[2, rows, lanes] = grad_values
            for row, grad in ((0, grad_queries), (1, grad_values)):
                self.term_grads[pl.ds(row, 1), lanes] += jnp.sum(grad.astype(jnp.float32), 0, keepdims=True)

        loop(2 * self.seqs, step, beside)

    def qkv_grads(self, group):
        lanes = pl.ds(4 * HEAD_DIM * group, 4 * HEAD_DIM)
        deep = self.att_w.shape[2]

        def step(part):
            grads = dot(self.tok_t[...], self.heads[part, :, lanes]).astype(jnp.bfloat16)
            for chip in range(self.att_split):
                self.act[self.act_first + 3 * chip + part, :, lanes] = grads[deep * chip : deep * (chip + 1)]

        loop(3, step)

    def input_back(self, beside=()):
        def step(r):
            rows = tile(r, TILE)
            total = self.grad[rows, :]
            for part in range(3):
                total = total + dot_nt(self.heads[part, rows, :], self.qkv_weight(part))
            self.gin[rows, :] = total.astype(jnp.bfloat16)

        loop(self.tiles, step, beside)


def gelu_parts(values):
    cdf = 0.5 * (1.0 + lax.erf(values * 0.5**0.5))
    return cdf, cdf + values * jnp.exp(-0.5 * values * values) * (2.0 * math.pi) ** (-0.5)


def batches(levels):
    return [(level,) for level in range(levels)], [(levels - 1,)], [tuple(range(levels - 1))]


def scratch_shapes(levels, att, ffn, rows, seqs, length):
    bf16, f32 = jnp.bfloat16, jnp.float32
    vmem, dma = pltpu.VMEM, pltpu.SemaphoreType.DMA
    chips = att.chips
    turned = vmem((D, rows), bf16)
    f_batches, o_batches, q_batches = batches(levels)
    shapes = dict(
        att_w=vmem((chips, att.parts, att.deep, D), bf16),
        ffn_w=vmem((chips, ffn.parts, ffn.deep, D), bf16),
        tok=vmem((rows, D), bf16),
        heads=vmem((3, rows, D), bf16),
        totals=vmem((seqs * HEADS, length), f32),
        ctx=vmem((rows, D), bf16),
        ctx_t=turned,
        hat=vmem((rows, D), f32),
        rstd=vmem((rows, 1), f32),
        low_t=turned,
        act=vmem((4 * rows // att.deep, att.deep, D), bf16),
        slope=vmem((8 * rows // att.deep, att.deep // 2, D), bf16),
        grad=vmem((rows, D), f32),
        down_t=turned,
        terms=vmem((16, D), f32),
        term_grads=vmem((16, D), f32),
        spare=vmem((48, 128), f32),
        terms_sum=vmem((2, 16, D // 2), f32),
        terms_got=vmem((4, 16, D // 2), f32),
        terms_all=vmem((2, 16, D // 2), f32),
        ffn_slots=vmem((chips + 4 * levels, ffn.parts, ffn.deep // 2, D), bf16),
        local_sem=dma((8,)),
        term_send=dma((3,)),
        term_recv=dma,
        sum_send=dma((5,)),
        sum_recv=dma((5,)),
        free=pltpu.SemaphoreType.REGULAR,
        f_send=dma((5,)),
        f_recv=dma((Reduce.semaphores(f_batches),)),
        o_send=dma((5,)),
        o_recv=dma((Reduce.semaphores(o_batches),)),
        q_send=dma((3, 5)),
        q_recv=dma((3, Reduce.semaphores(q_batches))),
    )
    for name, flat in (("att_", att), ("ffn_", ffn)):
        half = (flat.parts, flat.deep // 2, D)
        own = dict(
            long=vmem((flat.halo + flat.held + 8, 128), f32),
            halo=vmem((flat.tail + flat.halo + 8, 128), f32),
            line=vmem((flat.lines + flat.halo + 8, 128), f32),
            own=vmem((2, *half), f32),
            extra=vmem(half, bf16),
            send=dma((5,)),
            recv=dma((chips,)),
            sib=dma,
            plane_send=dma((5,)),
            plane_recv=dma((levels + 2,)),
            plane_sib=dma,
            halo_send=dma,
            halo_recv=dma,
            own_send=dma,
            own_recv=dma,
            back_send=dma,
            back_recv=dma,
        )
        shapes.update({name + key: shape for key, shape in own.items()})
    return shapes


def spaced(acts, first, every=1):
    return tuple((first + every * i, act) for i, act in enumerate(acts))


def run(acts):
    for act in acts:
        act()


def layer_kernel(names, levels, att, ffn, seqs, length, att_in, ffn_in, tok_in, cot_in, seg_row, seg_col, live,
                 out_out, gin_out, att_out, ffn_out, *scratch):
    s = types.SimpleNamespace(**dict(zip(names, scratch)))
    act_first = s.act.shape[0] // 4
    refs = dict(vars(s), seg_row=seg_row, seg_col=seg_col, live=live)
    refs.update(cot=s.tok, out=s.tok, down=s.ctx, tok_t=s.low_t)
    refs.update(bias=s.hat.at[:, pl.ds(0, length)], gin=s.tok, act_first=act_first)
    work = Layer(refs, att.split, ffn.split, seqs, length)

    def local(src, dst, at):
        copy = pltpu.make_async_copy(src, dst, s.local_sem.at[at])
        copy.start()
        return copy

    p = Place(levels)
    get_a = local(att_in, s.att_long.at[pl.ds(att.halo, att.held), :], 0)
    get_f = local(ffn_in, s.ffn_long.at[pl.ds(ffn.halo, ffn.held), :], 1)
    get_t = local(tok_in, s.tok, 2)
    p.meet(True)
    sends = Sends()
    lead_a = Lead(p, sends, att, s.att_long, s.att_halo, s.att_line, s.att_halo_send, s.att_halo_recv)
    lead_f = Lead(p, sends, ffn, s.ffn_long, s.ffn_halo, s.ffn_line, s.ffn_halo_send, s.ffn_halo_recv)
    get_a.wait()
    sends.go(lead_a.begin)
    get_f.wait()
    sends.go(lead_f.begin)
    lead_a.lines()
    lead_a.store(s.att_w)
    def gathers(ref, cut, *sems):
        parts, lanes = ref.shape[1], pl.ds(0, D)
        if cut[0]:
            first, last = (pl.ds(0, parts - cut[0]), lanes), (pl.ds(parts - cut[0], cut[0]), lanes)
        else:
            first = (pl.ds(0, parts), pl.ds(0, D - cut[1]))
            last = (pl.ds(0, parts), pl.ds(D - cut[1], cut[1]))
        go, plane = Gather(p, ref, *first, *sems[:3]), Plane(p, ref, *last, *sems[3:])
        return [go.own, plane.own, *steps_of(go, plane)], (go, plane)

    steps_a, go_a = gathers(
        s.att_w, (0, 128), s.att_send, s.att_recv, s.att_sib, s.att_plane_send, s.att_plane_recv, s.att_plane_sib
    )
    steps_f, go_f = gathers(
        s.ffn_w, (1, 0), s.ffn_send, s.ffn_recv, s.ffn_sib, s.ffn_plane_send, s.ffn_plane_recv, s.ffn_plane_sib
    )
    run(steps_a[:2])

    def last():
        terms, spare = s.terms, s.spare
        terms[...] = jnp.zeros(terms.shape, terms.dtype)
        for lead, at, count in ((lead_a, 0, 5), (lead_f, 8, 7)):
            rows = lead.last_rows(count)
            spare[pl.ds(0, rows.shape[0]), :] = rows
            for block in range(D // 128):
                terms[pl.ds(at, count), pl.ds(128 * block, 128)] = spare[pl.ds(block, count, stride=6), :]

    pl.when(p.d == att.chips - 1)(last)
    lead_f.lines()
    lead_f.store(s.ffn_w)
    s.term_grads[...] = jnp.zeros(s.term_grads.shape, jnp.float32)
    run(steps_a[2:5])
    run(steps_f[:2])
    run(steps_a[5:])
    sends.go(Spread(p, sends, s.terms, s.term_send, s.term_recv).run)
    for go in go_a:
        go.from_sibling()
    get_t.wait()

    rest = steps_f[2:]
    work.qkv(spaced(rest[:4], 0))
    work.attend(spaced(rest[4:16], 0))
    work.first_norm(spaced(rest[16:20], 0))
    run(rest[20:])
    get_c = local(cot_in, s.tok, 2)
    for go in go_f:
        go.from_sibling()
    get_c.wait()
    work.feed()
    put_o = local(s.tok, out_out, 3)
    sends.finish()
    for go in (*go_a, *go_f):
        go.finish()

    sums = Sends()
    slots, slope, act = s.ffn_slots, s.slope, s.act
    half_a, half_f = att.deep // 2, ffn.deep // 2

    def of(ref, half):
        return lambda chip, core: ref.at[chip, :, tile(core, half), :]

    def att_slots(lanes):
        return lambda i, count: slope.at[pl.ds(3 * i, 3 * count), :, lanes]

    f_batches, o_batches, q_batches = batches(levels)
    everything = pl.ds(0, D)
    ffn_slots = lambda i, count: slots.at[i] if count == 1 else slots.at[pl.ds(i, count)]
    add_f = Reduce(
        p, 4, ffn.chips, f_batches, of(s.ffn_w, half_f), ffn_slots, s.ffn_extra,
        lambda core: s.ffn_own.at[core], s.f_send, s.f_recv,
    )
    add_o = Reduce(
        p, 3, att.chips, o_batches, of(s.att_w, half_a), att_slots(everything), s.att_extra,
        lambda core: s.att_own.at[core], s.o_send, s.o_recv,
    )
    add_q = []
    for group in range(3):
        lanes = pl.ds(256 * group, 256)
        blocks = pl.ds(act_first, 3 * att.split)
        view = lambda chip, core, lanes=lanes: act.at[pl.ds(act_first + 3 * chip, 3), tile(core, half_a), lanes]
        whole = (act.at[blocks, tile(1 - p.c, half_a), lanes], slope.at[pl.ds(0, 3 * att.split), :, lanes])
        add_q.append(
            Reduce(
                p, 3, att.chips, q_batches, view, att_slots(lanes), s.att_extra.at[:, :, lanes],
                lambda core, lanes=lanes: s.att_own.at[core, :, :, lanes], s.q_send.at[group], s.q_recv.at[group], whole,
            )
        )
    add_t = Terms(p, sums, s.terms_sum, s.terms_got, s.terms_all, s.sum_send, s.sum_recv)

    def do(act, *at):
        return sums.later(functools.partial(act, *at))

    def q(group, act, *at):
        return functools.partial(act, add_q[group], *at, 0)

    def f(act, *at):
        return functools.partial(act, *at)

    work.hidden_back(0)
    work.down_grads(0)
    work.hidden_back(1)
    work.down_grads(1)
    f(add_f.share, 2)()
    put_o.wait()
    get_t = local(tok_in, s.tok, 2)
    work.hidden_back(2)
    work.down_grads(2, ((0, f(add_f.over_b, 2)),))
    work.hidden_back(3)
    work.down_grads(3)
    f(add_f.share, 3)()
    work.in_back(0, ((3, f(add_f.over_b, 3)),))
    work.in_grads(0)
    work.in_back(1, ((2, f(add_f.over_a, 2)),))
    work.in_grads(1)
    work.in_back(2)
    work.in_grads(2)
    work.in_back(3, ((2, f(add_f.collect, 2)), (2, f(add_f.line, 2, 2))))
    work.in_grads(3, ((1, f(add_f.over_a, 3)),))
    f(add_f.share, 0)()
    f(add_f.share, 1)()

    def greet(device):
        pl.semaphore_signal(s.free, inc=1, device_id=device, device_id_type=MESH_ID)

    for device in (p.sibling, p.across_a, p.across_b):
        greet(device)
    pl.when(p.has_up)(lambda: greet(p.up))
    pl.when(p.has_down)(lambda: greet(p.down))

    get_t.wait()
    work.first_back(((1, f(add_f.over_b, 0)),))
    work.out_grads(((3, f(add_f.line, 1, 2)),))
    pl.semaphore_wait(s.free, 3 + p.has_up.astype(jnp.int32) + p.has_down.astype(jnp.int32))
    f(add_o.share, 0)()
    work.make_bias()
    work.attend_back(
        0,
        (
            (0, f(add_f.over_b, 1)),
            (1, f(add_f.collect, 3)),
            (1, f(add_f.line, 3, 3)),
            (2, f(add_f.over_a, 0)),
            (3, f(add_o.over_b, 0)),
        ),
    )
    work.qkv_grads(0)
    add_q[0].share(0)
    work.attend_back(
        1,
        (
            (0, q(0, Reduce.over_b)),
            (1, f(add_f.line, 2, 3)),
            (1, f(add_f.collect, 0)),
            (1, f(add_f.line, 3, 0)),
            (2, f(add_f.over_a, 1)),
            (3, q(0, Reduce.over_a)),
            (3, f(add_o.over_a, 0)),
        ),
    )
    work.qkv_grads(1)
    add_q[1].share(0)
    work.attend_back(
        2,
        (
            (0, f(add_f.line, 1, 3)),
            (0, f(add_f.line, 2, 0)),
            (0, f(add_f.collect, 1)),
            (0, f(add_f.line, 2, 1)),
            (0, q(1, Reduce.over_b)),
            (1, q(0, Reduce.collect)),
            (1, f(add_o.collect, 0)),
            (1, f(add_o.line, 3, 0)),
            (1, q(0, Reduce.line, 3)),
            (2, q(0, Reduce.line, 2)),
            (3, f(add_o.line, 2, 0)),
            (3, q(1, Reduce.over_a)),
        ),
    )
    work.qkv_grads(2)
    add_q[2].share(0)
    for core in range(2):
        s.terms_sum[core] = s.term_grads[:, pl.ds(D // 2 * core, D // 2)]
    do(add_t.share)()
    f(add_f.line, 1, 0)()
    f(add_f.line, 1, 1)()
    q(0, Reduce.line, 1)()
    work.input_back(
        (
            (0, q(2, Reduce.over_b)),
            (0, do(add_t.over_b)),
            (0, f(add_o.line, 1, 0)),
            (1, q(1, Reduce.collect)),
            (1, q(1, Reduce.line, 3)),
            (2, q(1, Reduce.line, 2)),
            (2, do(add_t.over_a)),
            (3, q(2, Reduce.over_a)),
            (3, q(1, Reduce.line, 1)),
        )
    )
    put_g = local(work.gin, gin_out, 4)
    trail_f = Trail(p, sums, ffn, s.ffn_own, s.ffn_line, s.ffn_long, s.ffn_back_send, s.ffn_back_recv)
    trail_a = Trail(p, sums, att, s.att_own, s.att_line, s.att_long, s.att_back_send, s.att_back_recv)
    given_f = lambda core: handed(p, s.ffn_own, core, s.ffn_own_send, s.ffn_own_recv)
    given_a = lambda core: handed(p, s.att_own, core, s.att_own_send, s.att_own_recv)
    do(add_t.line, 3)()
    add_f.keep()
    sums.go(lambda: sums.start(None, lambda: given_f(p.c)))
    q(2, Reduce.collect)()
    q(2, Reduce.line, 3)()
    do(add_t.line, 2)()
    given_f(1 - p.c).wait_recv()
    trail_f.lines()
    q(2, Reduce.line, 2)()
    do(add_t.line, 1)()
    sums.go(trail_f.pass_back)
    q(2, Reduce.line, 1)()
    do(add_t.line, 0)()
    do(add_t.hand_over)()
    final = p.d == att.chips - 1

    def terms_here():
        add_t.take_over()
        trail_f.last_rows(s.terms_all, 8, 7)
        trail_a.last_rows(s.terms_all, 0, 5)

    pl.when(final)(terms_here)
    trail_f.out()
    put_f = local(s.ffn_long.at[pl.ds(0, ffn.held), :], ffn_out, 1)
    for who in (add_o, *add_q):
        who.keep()
    sums.go(lambda: sums.start(None, lambda: given_a(p.c)))
    given_a(1 - p.c).wait_recv()
    trail_a.lines()
    sums.go(trail_a.pass_back)
    trail_a.out()
    put_a = local(s.att_long.at[pl.ds(0, att.held), :], att_out, 0)
    sums.finish()
    for who in (add_f, add_o, *add_q):
        who.finish()
    for copy in (put_g, put_f, put_a):
        copy.wait()


def run_layer(levels, att, ffn, att_lines, ffn_lines, tokens, cotangent, segments, live_count):
    vmem = pl.BlockSpec(memory_space=pltpu.VMEM)
    anywhere = pl.BlockSpec(memory_space=pl.ANY)
    seqs, length = segments.shape
    rows = tokens.shape[0]
    bf16, f32 = jnp.bfloat16, jnp.float32
    live = jnp.broadcast_to((jnp.arange(seqs) < live_count[0]).astype(f32)[:, None], (seqs, 128))
    shape = jax.ShapeDtypeStruct
    scratch = scratch_shapes(levels, att, ffn, rows, seqs, length)
    return pl.pallas_call(
        functools.partial(layer_kernel, tuple(scratch), levels, att, ffn, seqs, length),
        out_shape=(
            shape(tokens.shape, bf16),
            shape(tokens.shape, bf16),
            shape((att.held, 128), f32),
            shape((ffn.held, 128), f32),
        ),
        in_specs=[anywhere, anywhere, anywhere, anywhere, vmem, vmem, vmem],
        out_specs=(anywhere, anywhere, anywhere, anywhere),
        scratch_shapes=list(scratch.values()),
        compiler_params=pltpu.CompilerParams(
            collective_id=1, has_side_effects=True, vmem_limit_bytes=64 * 2**20
        ),
        name="layer",
    )(att_lines, ffn_lines, tokens, cotangent, segments, segments.T, live)


def as_lines(flat, vector):
    return jnp.pad(vector, (0, flat.held * 128 - flat.length)).reshape(flat.held, 128)


def fast_body(
    levels,
    tokens,
    cotangent,
    segments,
    live_count,
    att_master,
    att_first,
    att_second,
    ffn_master,
    ffn_first,
    ffn_second,
):
    chips = lax.axis_size("dp")
    att = Flat(att_master.shape[0], chips, 3, 3 * chips // 4, False)
    ffn = Flat(ffn_master.shape[0], chips, 4, chips // 2, True)
    output, input_grad, att_sum, ffn_sum = run_layer(
        levels,
        att,
        ffn,
        as_lines(att, att_master),
        as_lines(ffn, ffn_master),
        tokens,
        cotangent,
        segments,
        live_count,
    )
    att_grad = att_sum.reshape(-1)[: att.length]
    ffn_grad = ffn_sum.reshape(-1)[: ffn.length]
    att_new = adam_update(att_master, att_first, att_second, att_grad)
    ffn_new = adam_update(ffn_master, ffn_first, ffn_second, ffn_grad)
    return (output, input_grad, att_grad, *att_new, ffn_grad, *ffn_new)


def body_for(mesh):
    chips, cores = mesh.shape["dp"], mesh.shape["rep"]
    if chips == 16 and cores == 2:
        return functools.partial(fast_body, chips // 4)
    return general_body


def solution(mesh):
    placed = (
        P(("dp", "rep"), None),
        P(("dp", "rep"), None),
        P(("dp", "rep"), None),
        P(("dp", "rep")),
        P("dp"),
        P("dp"),
        P("dp"),
        P("dp"),
        P("dp"),
        P("dp"),
    )
    return jax.shard_map(
        body_for(mesh),
        mesh=mesh,
        in_specs=placed,
        out_specs=(
            P(("dp", "rep"), None),
            P(("dp", "rep"), None),
            P("dp"),
            P("dp"),
            P("dp"),
            P("dp"),
            P("dp"),
            P("dp"),
            P("dp"),
            P("dp"),
        ),
        check_vma=False,
    )
```

```python
import functools
import math
import types

import jax
import jax.numpy as jnp
from jax import lax
from jax.experimental import pallas as pl
from jax.experimental.pallas import tpu as pltpu
from jax.sharding import PartitionSpec as P

D = 768
HEADS = 12
HEAD_DIM = 64
FF = 3072
STEP = 10


norm_eps = 1e-05
beta_one = 0.9
beta_two = 0.98
decay = 0.01
adam_eps = 1e-08
masked = -1e30


def split_attention(flat_params):
    qkv_weight = flat_params[: 3 * D * D].reshape(D, 3 * D)
    offset = 3 * D * D
    out_weight = flat_params[offset : offset + D * D].reshape(D, D)
    offset = offset + D * D
    att_terms = flat_params[offset : offset + 5 * D].reshape(5, D).astype(jnp.float32)
    return (qkv_weight, out_weight, att_terms)


def split_ffn(flat_params):
    in_weight = flat_params[: D * FF].reshape(D, FF)
    offset = D * FF
    down_weight = flat_params[offset : offset + FF * D].reshape(FF, D)
    offset = offset + FF * D
    in_bias = flat_params[offset : offset + FF].astype(jnp.float32)
    offset = offset + FF
    ffn_terms = flat_params[offset : offset + 3 * D].reshape(3, D).astype(jnp.float32)
    return (in_weight, down_weight, in_bias, ffn_terms)


def normalize(values, gain, shift):
    row_mean = jnp.mean(values, -1, keepdims=True)
    centred = values - row_mean
    rstd_rows = lax.rsqrt(jnp.mean(centred * centred, -1, keepdims=True) + norm_eps)
    normed = centred * rstd_rows
    return (normed * gain + shift, normed, rstd_rows)


def norm_back(grad_in, normed, rstd_rows, gain):
    scaled = grad_in * gain
    grad_rows = rstd_rows * (
        scaled
        - jnp.mean(scaled, -1, keepdims=True)
        - normed * jnp.mean(scaled * normed, -1, keepdims=True)
    )
    return (grad_rows, jnp.sum(grad_in * normed, 0), jnp.sum(grad_in, 0))


def gelu_slope(values):
    normal_cdf = 0.5 * (1.0 + lax.erf(values * 0.5**0.5))
    return normal_cdf + values * jnp.exp(-0.5 * values * values) * (2.0 * math.pi) ** (-0.5)


def masked_scores(query_rows, key_rows, seg_ids):
    scores = jnp.einsum(
        "qhd,khd->hqk", query_rows, key_rows, preferred_element_type=jnp.float32
    ) * HEAD_DIM ** (-0.5)
    same_doc = seg_ids[:, None] == seg_ids[None, :]
    return jnp.where(same_doc[None], scores, masked)


def attend_forward(block):
    query_rows, key_rows, value_rows, seg_ids = block
    scores = masked_scores(query_rows, key_rows, seg_ids)
    row_top = jnp.max(scores, -1, keepdims=True)
    raised = jnp.exp(scores - row_top)
    row_total = jnp.sum(raised, -1, keepdims=True)
    soft_probs = (raised / row_total).astype(jnp.bfloat16)
    context = jnp.einsum("hqk,khd->qhd", soft_probs, value_rows, preferred_element_type=jnp.float32)
    return (
        context.astype(jnp.bfloat16).reshape(context.shape[0], -1),
        row_top + jnp.log(row_total),
    )


def attend_backward(query_rows, key_rows, value_rows, seg_ids, log_total, grad_context):
    soft_probs = jnp.exp(masked_scores(query_rows, key_rows, seg_ids) - log_total)
    grad_probs = jnp.einsum(
        "qhd,khd->hqk", grad_context, value_rows, preferred_element_type=jnp.float32
    )
    grad_values = jnp.einsum(
        "hqk,qhd->khd",
        soft_probs.astype(jnp.bfloat16),
        grad_context,
        preferred_element_type=jnp.float32,
    )
    grad_scores = soft_probs * (grad_probs - jnp.sum(soft_probs * grad_probs, -1, keepdims=True))
    grad_scores = grad_scores.astype(jnp.bfloat16)
    grad_queries = jnp.einsum(
        "hqk,khd->qhd", grad_scores, key_rows, preferred_element_type=jnp.float32
    ) * HEAD_DIM ** (-0.5)
    grad_keys = jnp.einsum(
        "hqk,qhd->khd", grad_scores, query_rows, preferred_element_type=jnp.float32
    ) * HEAD_DIM ** (-0.5)
    length_here = query_rows.shape[0]
    return jnp.concatenate(
        [
            grad_queries.reshape(length_here, -1),
            grad_keys.reshape(length_here, -1),
            grad_values.reshape(length_here, -1),
        ],
        -1,
    )


def adam_update(master, first, second, grad):
    first_new = beta_one * first + (1.0 - beta_one) * grad
    second_new = beta_two * second + (1.0 - beta_two) * grad * grad
    fix_one = 1.0 - beta_one**STEP
    fix_two = 1.0 - beta_two**STEP
    update = first_new / fix_one / (jnp.sqrt(second_new / fix_two) + adam_eps)
    return (first_new, second_new, update + decay * master)


def general_body(
    tokens,
    cotangent,
    segments,
    live_count,
    att_master,
    att_first,
    att_second,
    ffn_master,
    ffn_first,
    ffn_second,
):
    seq_count = segments.shape[0]
    length = segments.shape[1]
    att_full = lax.all_gather(att_master.astype(jnp.bfloat16), "dp", axis=0, tiled=True)
    qkv_weight, out_weight, att_terms = split_attention(att_full)
    bias_qkv = jnp.concatenate([att_terms[0], jnp.zeros_like(att_terms[0]), att_terms[1]])
    qkv = (jnp.dot(tokens, qkv_weight, preferred_element_type=jnp.float32) + bias_qkv).astype(
        jnp.bfloat16
    )
    head_split = qkv.reshape(seq_count, length, 3, HEADS, HEAD_DIM)
    context, log_total = lax.map(
        attend_forward, (head_split[:, :, 0], head_split[:, :, 1], head_split[:, :, 2], segments)
    )
    context = context.reshape(-1, D)
    residual = (
        tokens.astype(jnp.float32)
        + jnp.dot(context, out_weight, preferred_element_type=jnp.float32)
        + att_terms[2]
    )
    first_out, first_hat, first_rstd = normalize(residual, att_terms[3], att_terms[4])
    ffn_full = lax.all_gather(ffn_master.astype(jnp.bfloat16), "dp", axis=0, tiled=True)
    in_weight, down_weight, in_bias, ffn_terms = split_ffn(ffn_full)
    first_low = first_out.astype(jnp.bfloat16)
    ffn_inner = jnp.dot(first_low, in_weight, preferred_element_type=jnp.float32) + in_bias
    ffn_act = jax.nn.gelu(ffn_inner, approximate=False).astype(jnp.bfloat16)
    second_in = (
        first_out + jnp.dot(ffn_act, down_weight, preferred_element_type=jnp.float32) + ffn_terms[0]
    )
    output, second_hat, second_rstd = normalize(second_in, ffn_terms[1], ffn_terms[2])
    att_back = lax.all_gather(att_master.astype(jnp.bfloat16), "dp", axis=0, tiled=True)
    qkv_weight, out_weight, att_terms = split_attention(att_back)
    ffn_back = lax.all_gather(ffn_master.astype(jnp.bfloat16), "dp", axis=0, tiled=True)
    in_weight, down_weight, in_bias, ffn_terms = split_ffn(ffn_back)

    def microbatch(micro_index, state_now):
        grad_sums, input_grads = state_now

        def take_rows(array_in):
            return lax.dynamic_slice_in_dim(array_in, micro_index * length, length, 0)

        grad_out = take_rows(cotangent).astype(jnp.float32)
        grad_second, grad_gain_two, grad_shift_two = norm_back(
            grad_out, take_rows(second_hat), take_rows(second_rstd), ffn_terms[1]
        )
        grad_down = grad_second.astype(jnp.bfloat16)
        grad_down_bias = jnp.sum(grad_down.astype(jnp.float32), 0)
        grad_down_weight = jnp.dot(
            take_rows(ffn_act).T, grad_down, preferred_element_type=jnp.float32
        )
        grad_act = jnp.dot(grad_down, down_weight.T, preferred_element_type=jnp.float32)
        grad_inner = (grad_act * gelu_slope(take_rows(ffn_inner))).astype(jnp.bfloat16)
        grad_in_bias = jnp.sum(grad_inner.astype(jnp.float32), 0)
        grad_in_weight = jnp.dot(
            take_rows(first_low).T, grad_inner, preferred_element_type=jnp.float32
        )
        grad_first = grad_second + jnp.dot(
            grad_inner, in_weight.T, preferred_element_type=jnp.float32
        )
        grad_residual, grad_gain_one, grad_shift_one = norm_back(
            grad_first, take_rows(first_hat), take_rows(first_rstd), att_terms[3]
        )
        grad_proj = grad_residual.astype(jnp.bfloat16)
        grad_out_bias = jnp.sum(grad_proj.astype(jnp.float32), 0)
        grad_out_weight = jnp.dot(
            take_rows(context).T, grad_proj, preferred_element_type=jnp.float32
        )
        grad_context = jnp.dot(grad_proj, out_weight.T, preferred_element_type=jnp.float32).astype(
            jnp.bfloat16
        )
        this_seq = lax.dynamic_index_in_dim(head_split, micro_index, 0, keepdims=False)
        this_segs = lax.dynamic_index_in_dim(segments, micro_index, 0, keepdims=False)
        this_total = lax.dynamic_index_in_dim(log_total, micro_index, 0, keepdims=False)
        grad_qkv = attend_backward(
            this_seq[:, 0],
            this_seq[:, 1],
            this_seq[:, 2],
            this_segs,
            this_total,
            grad_context.reshape(length, HEADS, HEAD_DIM),
        )
        grad_qkv = grad_qkv.astype(jnp.bfloat16)
        grad_wide = grad_qkv.astype(jnp.float32)
        grad_query_bias = jnp.sum(grad_wide[:, :D], 0)
        grad_value_bias = jnp.sum(grad_wide[:, 2 * D :], 0)
        grad_qkv_weight = jnp.dot(take_rows(tokens).T, grad_qkv, preferred_element_type=jnp.float32)
        grad_tokens = (
            jnp.dot(grad_qkv, qkv_weight.T, preferred_element_type=jnp.float32) + grad_residual
        )
        input_grads = lax.dynamic_update_slice_in_dim(
            input_grads, grad_tokens.astype(jnp.bfloat16), micro_index * length, 0
        )
        terms_now = (
            grad_qkv_weight,
            grad_out_weight,
            grad_query_bias,
            grad_value_bias,
            grad_out_bias,
            grad_gain_one,
            grad_shift_one,
            grad_in_weight,
            grad_down_weight,
            grad_in_bias,
            grad_down_bias,
            grad_gain_two,
            grad_shift_two,
        )
        grad_sums = tuple((running + fresh for running, fresh in zip(grad_sums, terms_now)))
        return (grad_sums, input_grads)

    zero_sums = (
        jnp.zeros((D, 3 * D), jnp.float32),
        jnp.zeros((D, D), jnp.float32),
        jnp.zeros((D,), jnp.float32),
        jnp.zeros((D,), jnp.float32),
        jnp.zeros((D,), jnp.float32),
        jnp.zeros((D,), jnp.float32),
        jnp.zeros((D,), jnp.float32),
        jnp.zeros((D, FF), jnp.float32),
        jnp.zeros((FF, D), jnp.float32),
        jnp.zeros((FF,), jnp.float32),
        jnp.zeros((D,), jnp.float32),
        jnp.zeros((D,), jnp.float32),
        jnp.zeros((D,), jnp.float32),
    )
    zero_inputs = jnp.zeros(tokens.shape, jnp.bfloat16)
    grad_sums, input_grad = lax.fori_loop(0, live_count[0], microbatch, (zero_sums, zero_inputs))
    dp_count = lax.axis_size("dp")
    att_pad = att_master.shape[0] * dp_count - 4 * D * D - 5 * D
    ffn_pad = ffn_master.shape[0] * dp_count - 2 * D * FF - FF - 3 * D
    att_local = jnp.concatenate(
        [
            grad_sums[0].reshape(-1),
            grad_sums[1].reshape(-1),
            grad_sums[2],
            grad_sums[3],
            grad_sums[4],
            grad_sums[5],
            grad_sums[6],
            jnp.zeros((att_pad,), jnp.float32),
        ]
    )
    ffn_local = jnp.concatenate(
        [
            grad_sums[7].reshape(-1),
            grad_sums[8].reshape(-1),
            grad_sums[9],
            grad_sums[10],
            grad_sums[11],
            grad_sums[12],
            jnp.zeros((ffn_pad,), jnp.float32),
        ]
    )
    att_rows, ffn_rows = (
        lax.all_to_all(
            att_local.reshape(dp_count, -1).astype(jnp.bfloat16),
            "dp",
            split_axis=0,
            concat_axis=0,
            tiled=True,
        ).astype(jnp.float32),
        lax.all_to_all(
            ffn_local.reshape(dp_count, -1).astype(jnp.bfloat16),
            "dp",
            split_axis=0,
            concat_axis=0,
            tiled=True,
        ).astype(jnp.float32),
    )
    att_share = jnp.sum(att_rows, 0)
    ffn_share = jnp.sum(ffn_rows, 0)
    att_grad, ffn_grad = (
        lax.psum(att_share.astype(jnp.bfloat16), "rep").astype(jnp.float32),
        lax.psum(ffn_share.astype(jnp.bfloat16), "rep").astype(jnp.float32),
    )
    att_new = adam_update(att_master, att_first, att_second, att_grad)
    ffn_new = adam_update(ffn_master, ffn_first, ffn_second, ffn_grad)
    return (
        output.astype(jnp.bfloat16),
        input_grad,
        att_grad,
        att_new[0],
        att_new[1],
        att_new[2],
        ffn_grad,
        ffn_new[0],
        ffn_new[1],
        ffn_new[2],
    )


MESH_ID = pl.DeviceIdType.MESH


def when(cond, act):
    if cond is None:
        act()
    else:
        pl.when(cond)(act)


class Place:
    def __init__(self, levels):
        self.levels = levels
        d = lax.axis_index("dp")
        c = lax.axis_index("rep")
        self.d, self.c = d, c
        self.z, y, x = d // 4, (d // 2) % 2, d % 2
        x_near, y_near = d + 1 - 2 * x, d + 2 - 4 * y
        self.a_near = x_near + c * (y_near - x_near)
        self.b_near = y_near + c * (x_near - y_near)
        self.far = x_near + y_near - d
        self.a_at = x + c * (y - x)
        self.b_at = y + c * (x - y)
        self.up = (d + 4, c)
        self.down = (d - 4, c)
        self.has_up = self.z < levels - 1
        self.has_down = self.z > 0
        self.across_a = (self.a_near, c)
        self.across_b = (self.b_near, c)
        self.sibling = (d, 1 - c)

    def levels_at(self, distance):
        if distance == 0:
            return [(self.z, None, 0)]
        return [
            (self.z - distance, self.z >= distance, -1),
            (self.z + distance, self.z + distance < self.levels, 1),
        ]

    def at(self, column, level):
        return column + 4 * (level - self.z)

    def turn(self, distance):
        return self.at(self.d, (self.z + distance) % self.levels)

    def along(self, step):
        return (self.up, self.has_up) if step > 0 else (self.down, self.has_down)

    def meet(self):
        barrier = pltpu.get_barrier_semaphore()

        def greet(device):
            pl.semaphore_signal(barrier, inc=1, device_id=device, device_id_type=MESH_ID)

        for device in (self.across_a, self.across_b, self.sibling):
            greet(device)
        count = 3
        for distance in range(1, self.levels):
            greet((self.turn(distance), self.c))
            count += 1
        edges = [((self.d + 1, self.c), self.d < 4 * self.levels - 1), ((self.d - 1, self.c), self.d > 0)]
        for device, there in edges:
            pl.when(there)(functools.partial(greet, device))
            count = count + there.astype(jnp.int32)
        pl.semaphore_wait(barrier, count)


def both(first, second):
    if first is None:
        return second
    return first if second is None else first & second


class Sends:
    def __init__(self):
        self.steps, self.closing = [], False

    def go(self, step):
        if not any(step is other for other in self.steps):
            self.steps.append(step)
        step()

    def later(self, step):
        return lambda: self.go(step)

    def start(self, cond, make):
        when(cond, lambda: make().wait_send() if self.closing else make().start())

    def wait(self, cond, make):
        if not self.closing:
            when(cond, lambda: make().wait_recv())

    def finish(self):
        self.closing = True
        for step in self.steps:
            step()


def remote(src, dst, send_sem, recv_sem, device):
    return pltpu.make_async_remote_copy(
        src_ref=src,
        dst_ref=dst,
        send_sem=send_sem,
        recv_sem=recv_sem,
        device_id=device,
        device_id_type=MESH_ID,
    )


class Gather:
    def __init__(self, place, ref, parts, lanes, send_sem, recv_sem, sib_sem):
        self.place, self.ref, self.parts, self.lanes = place, ref, parts, lanes
        self.send_sem, self.recv_sem, self.sib_sem = send_sem, recv_sem, sib_sem
        self.half = ref.shape[2] // 2
        levels = place.levels
        self.leave = {2: levels, 3: 2 * levels, 4: 4 * levels - 1}
        self.together = 1

    def rows(self, core):
        return pl.ds(pl.multiple_of(core * self.half, self.half), self.half)

    def piece(self, chip, core):
        return self.ref.at[chip, self.parts, self.rows(core), self.lanes]

    def several(self, count):
        return self.ref.at[pl.ds(0, count), self.parts, pl.ds(0, self.half), self.lanes]

    def send(self, cond, chip, way, device):
        own = self.piece(chip, self.place.c)
        recv = self.sib_sem if way == 4 else self.recv_sem.at[chip]
        when(cond, lambda: remote(own, own, self.send_sem.at[way], recv, device).start())

    def wait(self, cond, part, sem):
        when(cond, lambda: remote(part, part, self.send_sem.at[0], sem, self.place.sibling).wait_recv())

    def arrived(self, cond, chip):
        self.wait(cond, self.piece(chip, self.place.c), self.recv_sem.at[chip])

    def own(self):
        p = self.place
        self.send(p.has_up, p.d, 0, p.up)
        self.send(p.has_down, p.d, 1, p.down)
        self.send(None, p.d, 3, p.across_b)
        self.send(None, p.d, 2, p.across_a)

    def line(self, distance):
        p = self.place
        for level, there, step in p.levels_at(distance):
            chip = p.at(p.d, level)
            self.arrived(there, chip)
            onward, more = p.along(-step)
            self.send(both(there, more), chip, 0 if step < 0 else 1, onward)
            self.send(there, chip, 3, p.across_b)
            self.send(there, chip, 2, p.across_a)
            self.send(there, chip, 4, p.sibling)

    def over_a(self, distance):
        p = self.place
        for level, there, _ in p.levels_at(distance):
            chip = p.at(p.a_near, level)
            self.arrived(there, chip)
            self.send(there, chip, 3, p.across_b)
            self.send(there, chip, 4, p.sibling)

    def over_b(self, distance):
        p = self.place
        for column in (p.b_near, p.far):
            for level, there, _ in p.levels_at(distance):
                chip = p.at(column, level)
                self.arrived(there, chip)
                self.send(there, chip, 4, p.sibling)

    def from_sibling(self):
        self.wait(None, self.several(4 * self.place.levels - 1), self.sib_sem)

    def left(self, cond, way, count):
        part = self.several(count)
        sem = self.send_sem.at[way]
        when(cond, lambda: remote(part, part, sem, self.sib_sem, self.place.sibling).wait_send())

    def finish(self):
        p = self.place
        for way, count in self.leave.items():
            self.left(None, way, count)
        for level in range(p.levels):
            if level < p.levels - 1:
                self.left(p.z == level, 0, self.together * (level + 1))
            if level > 0:
                self.left(p.z == level, 1, self.together * (p.levels - level))


class Plane(Gather):
    def __init__(self, place, ref, parts, lanes, send_sem, recv_sem, sib_sem):
        super().__init__(place, ref, parts, lanes, send_sem, recv_sem, sib_sem)
        self.leave = {2: 1, 3: 2, 4: 4 * place.levels - 1}
        self.together = 4
        self.from_a, self.from_b = place.levels, place.levels + 1

    def send(self, cond, chip, way, device):
        own = self.piece(chip, self.place.c)
        recv = self.sib_sem if way == 4 else self.recv_sem.at[self.from_a if way == 2 else self.from_b]
        when(cond, lambda: remote(own, own, self.send_sem.at[way], recv, device).start())

    def own(self):
        p = self.place
        self.send(None, p.d, 2, p.across_a)
        self.send(None, p.d, 3, p.across_b)

    def near(self):
        p = self.place
        self.wait(None, self.piece(p.a_near, p.c), self.recv_sem.at[self.from_a])
        self.send(None, p.a_near, 3, p.across_b)
        self.send(None, p.a_near, 4, p.sibling)

    def sheet(self, level):
        return self.ref.at[pl.ds(4 * level, 4), self.parts, self.rows(self.place.c), self.lanes]

    def send_sheet(self, cond, level, way, device):
        own = self.sheet(level)
        recv = self.sib_sem if way == 4 else self.recv_sem.at[level]
        when(cond, lambda: remote(own, own, self.send_sem.at[way], recv, device).start())

    def complete(self):
        p = self.place
        self.wait(None, self.several(2), self.recv_sem.at[self.from_b])
        self.send_sheet(p.has_up, p.z, 0, p.up)
        self.send_sheet(p.has_down, p.z, 1, p.down)
        for chip in (p.b_near, p.far):
            self.send(None, chip, 4, p.sibling)

    def line(self, distance):
        p = self.place
        for level, there, step in p.levels_at(distance):
            self.wait(there, self.sheet(level), self.recv_sem.at[level])
            onward, more = p.along(-step)
            self.send_sheet(both(there, more), level, 0 if step < 0 else 1, onward)
            self.send_sheet(there, level, 4, p.sibling)


class Spread:
    def __init__(self, place, sends, ref, send_sem, recv_sem):
        self.place, self.sends, self.ref = place, sends, ref
        self.send_sem, self.recv_sem = send_sem, recv_sem

    def copy(self, way, device):
        return remote(self.ref, self.ref, self.send_sem.at[way], self.recv_sem, device)

    def wait(self, cond):
        self.sends.wait(cond, lambda: self.copy(0, self.place.sibling))

    def run(self):
        p = self.place
        home = (p.a_at == 1) & (p.b_at == 1)
        self.wait(home & p.has_up)
        self.sends.start(home & p.has_down, lambda: self.copy(0, p.down))
        self.wait((p.a_at == 0) & (p.b_at == 1))
        self.sends.start(home, lambda: self.copy(1, p.across_a))
        self.wait(p.b_at == 0)
        self.sends.start(p.b_at == 1, lambda: self.copy(2, p.across_b))


def shifted(ref, start, rows):
    first, turn = start // 128, start % 128
    here = pltpu.roll(ref[pl.ds(first, rows), :], (128 - turn) % 128, 1)
    after = pltpu.roll(ref[pl.ds(first + 1, rows), :], (128 - turn) % 128, 1)
    lane = lax.broadcasted_iota(jnp.int32, (rows, 128), 1)
    return jnp.where(lane < 128 - turn, here, after)


class Flat:
    def __init__(self, length, chips, parts, split, turned):
        self.length, self.chips, self.parts, self.turned = length, chips, parts, turned
        self.rows = length // D // parts * parts
        self.slip = length - self.rows * D
        self.deep = self.rows // parts
        self.split = split
        self.lines = self.rows * (D // 128)
        self.most = self.slip * chips
        self.halo = -(-self.most // 1024) * 8
        self.held = -(-length // 1024) * 8
        self.tail_from = (length - self.most) // 1024 * 8
        self.tail = self.held - self.tail_from

    def place_of(self, part, block, split):
        if split:
            return 6 * part + block, 6 * self.parts
        return 6 * self.deep * part + block, 6


class Lead:
    def __init__(self, place, sends, flat, long_ref, halo_ref, line_ref, send_sem, recv_sem):
        self.place, self.sends, self.flat = place, sends, flat
        self.long_ref, self.halo_ref, self.line_ref = long_ref, halo_ref, line_ref
        self.send_sem, self.recv_sem = send_sem, recv_sem

    def copy(self):
        f, p = self.flat, self.place
        return remote(
            self.long_ref.at[pl.ds(f.halo + f.tail_from, f.tail), :],
            self.halo_ref.at[pl.ds(0, f.tail), :],
            self.send_sem,
            self.recv_sem,
            (p.d + 1, p.c),
        )

    def begin(self):
        self.sends.start(self.place.d < self.flat.chips - 1, self.copy)

    def lines(self):
        p, f = self.place, self.flat
        slip = f.slip * p.d
        self.line_ref[pl.ds(0, f.lines), :] = shifted(self.long_ref, f.halo * 128 - slip, f.lines)

        def mend():
            self.copy().wait_recv()
            before = shifted(self.halo_ref, f.length - f.tail_from * 128 - slip, f.halo)
            at = lax.broadcasted_iota(jnp.int32, (f.halo, 128), 0) * 128
            at = at + lax.broadcasted_iota(jnp.int32, (f.halo, 128), 1)
            self.line_ref[pl.ds(0, f.halo), :] = jnp.where(at < slip, before, self.line_ref[pl.ds(0, f.halo), :])

        pl.when(p.d > 0)(mend)

    def store(self, out_ref):
        p, f = self.place, self.flat

        def put(split):
            for part in range(f.parts):
                for block in range(D // 128):
                    first, stride = f.place_of(part, block, split)
                    out_ref[p.d, part, :, pl.ds(128 * block, 128)] = self.line_ref[
                        pl.ds(first, f.deep, stride=stride), :
                    ].astype(jnp.bfloat16)

        pl.when(p.d < f.split)(lambda: put(True))
        pl.when(p.d >= f.split)(lambda: put(False))

    def last_rows(self, count):
        f = self.flat
        lines = -(-count * 6 // 8) * 8
        return shifted(self.long_ref, f.halo * 128 + f.length - count * D, lines)


class Reduce:
    def __init__(self, place, parts, chips, batches, view, slots, kept, send_sem, recv_sem, whole=None):
        self.place, self.parts, self.batches = place, parts, batches
        self.view, self.slots, self.kept = view, slots, kept
        self.send_sem, self.recv_sem, self.whole = send_sem, recv_sem, whole
        self.levels = [level for batch in batches for level in batch]
        self.from_b, self.from_a = chips, chips + 2 * place.levels
        self.from_z = chips + 3 * place.levels

    def arrival(self, kind, batch):
        return self.recv_sem.at[batch, kind]

    def wait(self, part, sem):
        remote(part, part, self.send_sem.at[0], sem, self.place.sibling).wait_recv()

    def send(self, cond, chip, way, dst, recv, device):
        p = self.place
        src = self.view(chip, 1 - p.c if way == 4 else p.c)
        when(cond, lambda: remote(src, dst, self.send_sem.at[way], recv, device).start())

    def add(self, chip, src):
        here = self.view(chip, self.place.c)
        for part in range(self.parts):
            here[part] = here[part] + src[part]

    def share(self, batch):
        p = self.place
        recv = self.arrival(0, batch)
        if self.whole is not None:
            src, dst = self.whole
            remote(src, dst, self.send_sem.at[4], recv, p.sibling).start()
            return
        for level in self.batches[batch]:
            for column in (p.far, p.b_near, p.a_near, p.d):
                chip = p.at(column, level)
                self.send(None, chip, 4, self.slots(chip, 1), recv, p.sibling)

    def over_b(self, batch):
        p = self.place
        levels = self.batches[batch]
        self.wait(self.slots(4 * levels[0], 4 * len(levels)), self.arrival(0, batch))
        for kind, column in ((1, p.far), (0, p.b_near)):
            for level in levels:
                chip = p.at(column, level)
                self.add(chip, self.slots(chip, 1))
                dst = self.slots(self.from_b + p.levels * kind + level, 1)
                self.send(None, chip, 3, dst, self.arrival(1 + kind, batch), p.across_b)

    def over_a(self, batch):
        p = self.place
        levels = self.batches[batch]
        first = self.from_b + p.levels
        self.wait(self.slots(first + levels[0], len(levels)), self.arrival(2, batch))
        for level in levels:
            chip = p.at(p.a_near, level)
            self.add(chip, self.slots(chip, 1))
            self.add(chip, self.slots(first + level, 1))
            self.send(None, chip, 2, self.slots(self.from_a + level, 1), self.arrival(3, batch), p.across_a)

    def collect(self, batch):
        p = self.place
        levels = self.batches[batch]
        self.wait(self.slots(self.from_b + levels[0], len(levels)), self.arrival(1, batch))
        self.wait(self.slots(self.from_a + levels[0], len(levels)), self.arrival(3, batch))
        for level in levels:
            chip = p.at(p.d, level)
            for first in (0, self.from_b, self.from_a):
                self.add(chip, self.slots(first + level if first else chip, 1))

    def line(self, batch):
        p = self.place
        dst = self.slots(self.from_z + p.z, 1)
        for level in self.batches[batch]:
            chip = p.at(p.d, level)
            self.send(p.z != level, chip, 0, dst, self.arrival(4, batch), (chip, p.c))

    def keep(self):
        p = self.place
        own = self.kept(p.c)

        def total(batch):
            self.wait(self.slots(self.from_z, p.levels - 1), self.arrival(4, batch))
            here = self.view(p.d, p.c)
            others = [self.slots(self.from_z + (p.z + i) % p.levels, 1) for i in range(1, p.levels)]
            for part in range(self.parts):
                sum_now = here[part].astype(jnp.float32)
                for other in others:
                    sum_now = sum_now + other[part].astype(jnp.float32)
                own[part] = sum_now

        for batch, levels in enumerate(self.batches):
            pl.when((p.z >= levels[0]) & (p.z <= levels[-1]))(functools.partial(total, batch))

    def left(self, cond, way, count):
        part = self.slots(0, count)
        sem = self.send_sem.at[way]
        when(cond, lambda: remote(part, part, sem, self.recv_sem.at[0, 0], self.place.sibling).wait_send())

    def finish(self):
        p = self.place
        count = len(self.levels)
        for way, pieces in ((4, 4 * count), (3, 2 * count), (2, count)):
            self.left(None, way, pieces)
        for z in range(p.levels):
            self.left(p.z == z, 0, count - (z in self.levels))


class Chain(Reduce):
    def __init__(self, extra, line_sem, *rest):
        super().__init__(*rest)
        self.extra, self.line_sem = extra, line_sem

    def pass_on(self, here, level, way, waits, dst, device):
        p = self.place
        chip = p.at(p.d, level)
        slot = self.slots(self.from_z + level, 1)

        def act():
            if waits:
                self.wait(slot, self.line_sem.at[way, level])
                self.add(chip, slot)
            self.send(None, chip, way, dst, self.line_sem.at[way, level], device)

        pl.when(here)(act)

    def line(self, distance, batch):
        p = self.place
        for level in self.batches[batch]:
            slot = self.slots(self.from_z + level, 1)
            if level >= distance:
                self.pass_on(p.z == level - distance, level, 0, level > distance, slot, p.up)
            if level + distance < p.levels:
                dst = slot if distance > 1 else self.extra
                self.pass_on(p.z == level + distance, level, 1, level + distance < p.levels - 1, dst, p.down)

    def keep(self):
        p = self.place
        own = self.kept(p.c)

        def at(level):
            here = self.view(p.d, p.c)
            for part in range(self.parts):
                own[part] = here[part].astype(jnp.float32)
            sources = [(0, self.slots(self.from_z + level, 1))] if level > 0 else []
            sources += [(1, self.extra)] if level < p.levels - 1 else []
            for way, src in sources:
                self.wait(src, self.line_sem.at[way, level])
                for part in range(self.parts):
                    own[part] = own[part] + src[part].astype(jnp.float32)

        for level in self.levels:
            pl.when(p.z == level)(functools.partial(at, level))

    def finish(self):
        p = self.place
        count = len(self.levels)
        for way, pieces in ((4, 4 * count), (3, 2 * count), (2, count)):
            self.left(None, way, pieces)
        for z in range(p.levels):
            for way, pieces in enumerate((sum(n > z for n in self.levels), sum(n < z for n in self.levels))):
                if pieces:
                    self.left(p.z == z, way, pieces)


def handed(place, own_ref, core, send_sem, recv_sem):
    own = own_ref.at[core]
    return remote(own, own, send_sem, recv_sem, place.sibling)


class Terms:
    def __init__(self, place, sends, ref, got_ref, all_ref, send_sem, recv_sem):
        self.place, self.sends, self.ref, self.got_ref, self.all_ref = place, sends, ref, got_ref, all_ref
        self.send_sem, self.recv_sem = send_sem, recv_sem

    def copy(self, way, core, device):
        return remote(self.ref.at[core], self.got_ref.at[way], self.send_sem.at[way], self.recv_sem.at[way], device)

    def add(self, cond, way):
        if self.sends.closing:
            return

        def act():
            self.copy(way, 0, self.place.sibling).wait_recv()
            self.ref[self.place.c] = self.ref[self.place.c] + self.got_ref[way]

        when(cond, act)

    def share(self):
        self.sends.start(None, lambda: self.copy(0, 1 - self.place.c, self.place.sibling))

    def over_b(self):
        p = self.place
        self.add(None, 0)
        self.sends.start(p.b_at == 0, lambda: self.copy(1, p.c, p.across_b))

    def over_a(self):
        p = self.place
        self.add(p.b_at == 1, 1)
        self.sends.start((p.b_at == 1) & (p.a_at == 0), lambda: self.copy(2, p.c, p.across_a))

    def line(self):
        p = self.place
        home = (p.b_at == 1) & (p.a_at == 1)
        self.add(home, 2)
        here, top = self.ref.at[p.c], p.at(p.d, p.levels - 1)
        self.sends.start(
            home & p.has_up,
            lambda: remote(here, self.got_ref.at[3 + p.z], self.send_sem.at[3], self.recv_sem.at[3], (top, p.c)),
        )

    def keep(self):
        p = self.place
        got = self.got_ref.at[pl.ds(3, p.levels - 1)]
        remote(got, got, self.send_sem.at[3], self.recv_sem.at[3], p.sibling).wait_recv()
        for level in range(p.levels - 1):
            self.ref[p.c] = self.ref[p.c] + self.got_ref[3 + level]

    def final(self):
        return remote(
            self.ref.at[self.place.c],
            self.all_ref.at[self.place.c],
            self.send_sem.at[4],
            self.recv_sem.at[4],
            self.place.sibling,
        )

    def hand_over(self):
        p = self.place
        last = p.d == 4 * p.levels - 1
        if not self.sends.closing:
            pl.when(last)(self.keep)
        self.sends.start(last, self.final)

    def take_over(self):
        self.final().wait_recv()
        self.all_ref[self.place.c] = self.ref[self.place.c]


class Trail:
    def __init__(self, place, sends, flat, own_ref, line_ref, out_ref, send_sem, recv_sem):
        self.place, self.sends, self.flat = place, sends, flat
        self.own_ref, self.line_ref, self.out_ref = own_ref, line_ref, out_ref
        self.send_sem, self.recv_sem = send_sem, recv_sem

    def copy(self):
        f, p = self.flat, self.place
        return remote(
            self.line_ref.at[pl.ds(0, f.halo), :],
            self.line_ref.at[pl.ds(f.lines, f.halo), :],
            self.send_sem,
            self.recv_sem,
            (p.d - 1, p.c),
        )

    def lines(self):
        p, f = self.place, self.flat
        half = f.deep // 2

        def put(split):
            for core in range(2):
                for part in range(f.parts):
                    for block in range(D // 128):
                        first, stride = f.place_of(part, block, split)
                        first = first + stride * half * core
                        self.line_ref[pl.ds(first, half, stride=stride), :] = self.own_ref[
                            core, part, :, pl.ds(128 * block, 128)
                        ]

        def put_turned():
            for j in range(f.rows // 128):
                blocks = []
                for i in range(D // f.deep):
                    lanes = pl.ds(128 * (3 * (i % 2) + j), 128)
                    blocks += [self.own_ref[core, i // 2, :, lanes] for core in range(2)]
                turned = jnp.concatenate(blocks, 0).T
                for block in range(D // 128):
                    first = 6 * 128 * j + block
                    self.line_ref[pl.ds(first, 128, stride=6), :] = turned[:, 128 * block : 128 * (block + 1)]

        pl.when(p.d < f.split)(lambda: put(True))
        pl.when(p.d >= f.split)(put_turned if f.turned else lambda: put(False))

    def pass_back(self):
        self.sends.start(self.place.d > 0, self.copy)

    def last_rows(self, terms_ref, at, count):
        f = self.flat
        for core in range(2):
            for block in range(3):
                self.line_ref[pl.ds(f.lines + 3 * core + block, count, stride=6), :] = terms_ref[
                    core, pl.ds(at, count), pl.ds(128 * block, 128)
                ]

    def out(self):
        p, f = self.place, self.flat
        pl.when(p.d < f.chips - 1)(lambda: self.copy().wait_recv())
        self.out_ref[pl.ds(0, f.held), :] = shifted(self.line_ref, f.slip * p.d, f.held)


def dot(a, b):
    return jnp.dot(a, b, preferred_element_type=jnp.float32)


def dot_nt(a, b):
    return lax.dot_general(a, b, (((1,), (1,)), ((), ())), preferred_element_type=jnp.float32)


def square(values):
    return values.reshape(D, D)


def tile(index, size):
    return pl.ds(pl.multiple_of(index * size, size), size)


def loop(count, step, beside=()):
    def body(i, _):
        step(i)
        for at, act in beside:
            pl.when(i == at)(act)
        return 0

    lax.fori_loop(0, count, body, 0)


TILE, WIDE = 256, 512


class Layer:
    def __init__(self, refs, att_split, ffn_split, seqs, length):
        self.__dict__.update(refs)
        self.att_split, self.ffn_split = att_split, ffn_split
        self.seqs, self.length = seqs, length
        self.tiles = seqs * length // TILE

    def whole(self, blocks, part):
        count = blocks.shape[0] // 4
        return blocks[pl.ds(count * part, count)].reshape(self.seqs * self.length, D)

    def some(self, blocks, part, r, size=TILE):
        count = size // blocks.shape[1]
        return pl.ds(blocks.shape[0] // 4 * part + count * r, count)

    def qkv_weight(self, part):
        return square(self.att_w[pl.ds(0, self.att_split), part])

    def out_weight(self):
        return square(self.att_w[pl.ds(self.att_split, self.att_w.shape[0] - self.att_split)])

    def in_weight(self, part):
        return square(self.ffn_w[pl.ds(0, self.ffn_split), part])

    def down_weight(self, part):
        return square(self.ffn_w[pl.ds(self.ffn_split + 2 * part, 2)])

    def term(self, row):
        return self.terms[pl.ds(row, 1), :]

    def add_term(self, row, values):
        self.term_grads[pl.ds(row, 1), :] += jnp.sum(values, 0, keepdims=True)


    def qkv(self, beside=()):
        def step(r):
            rows = tile(r, TILE)
            x = self.tok[rows, :]
            queries = (dot(x, self.qkv_weight(0)) + self.term(0)).astype(jnp.bfloat16)
            self.heads[0, rows, :] = queries * HEAD_DIM ** (-0.5)
            self.heads[1, rows, :] = dot(x, self.qkv_weight(1)).astype(jnp.bfloat16)
            self.heads[2, rows, :] = (dot(x, self.qkv_weight(2)) + self.term(1)).astype(jnp.bfloat16)

        loop(self.tiles, step, beside)

    def make_bias(self):
        segs = self.segs[...].astype(jnp.float32)
        columns = jnp.concatenate([segs, jnp.zeros((8 - self.seqs, self.length), jnp.float32)], 0).T
        for seq in range(self.seqs):
            same = columns[:, seq : seq + 1] == segs[seq : seq + 1, :]
            self.bias[pl.ds(seq * self.length, self.length), :] = jnp.where(same, 0.0, masked)

    def lane_half(self, half):
        lane = lax.broadcasted_iota(jnp.int32, (self.length, 2 * HEAD_DIM), 1)
        return (lane // HEAD_DIM) == half

    def attend(self, beside=()):
        self.make_bias()

        def step(i):
            seq, pair = i // (HEADS // 2), i % (HEADS // 2)
            lanes = tile(pair, 2 * HEAD_DIM)
            rows = tile(seq, self.length)
            queries, keys, values = (self.heads[j, rows, lanes] for j in range(3))
            values_t = values.T
            parts = []
            for half in range(2):
                own = jnp.where(self.lane_half(half), queries, jnp.zeros_like(queries))
                scores = dot_nt(keys, own) + self.bias[rows, :]
                top = jnp.max(scores, 0, keepdims=True)
                raised = jnp.exp(scores - top)
                total = jnp.sum(raised, 0, keepdims=True)
                probs = (raised * (1.0 / total)).astype(jnp.bfloat16)
                self.totals[pl.ds(HEADS * seq + 2 * pair + half, 1), :] = top + jnp.log(total)
                parts.append(dot(values_t[HEAD_DIM * half : HEAD_DIM * (half + 1)], probs))
            both_t = jnp.concatenate(parts, 0).astype(jnp.bfloat16)
            self.ctx_t[lanes, rows] = both_t
            self.ctx[rows, lanes] = both_t.T

        loop(self.seqs * HEADS // 2, step, beside)

    def first_norm(self, beside=()):
        def step(r):
            rows = tile(r, TILE)
            residual = self.tok[rows, :].astype(jnp.float32) + dot(self.ctx[rows, :], self.out_weight()) + self.term(2)
            first, normed, rstd = normalize(residual, self.term(3), self.term(4))
            self.hat[rows, :] = normed
            self.rstd[rows, :] = rstd
            self.low_t[:, rows] = first.astype(jnp.bfloat16).T

        loop(self.tiles, step, beside)

    def feed(self, beside=()):
        def step(r):
            rows = tile(r, TILE)
            first = self.hat[rows, :] * self.term(3) + self.term(4)
            low = first.astype(jnp.bfloat16)
            second = first + self.term(12)
            for part in range(4):
                inner = dot(low, self.in_weight(part)) + self.term(8 + part)
                cdf, slope = gelu_parts(inner)
                act = (inner * cdf).astype(jnp.bfloat16)
                self.act[self.some(self.act, part, r)] = act.reshape(-1, self.act.shape[1], D)
                slope = slope.astype(jnp.bfloat16).reshape(-1, self.slope.shape[1], D)
                self.slope[self.some(self.slope, part, r)] = slope
                second = second + dot(act, self.down_weight(part))
            out, normed, rstd = normalize(second, self.term(13), self.term(14))
            seq = r // (self.length // TILE)
            live = jnp.clip(self.live_count[0] - seq, 0, 1).astype(jnp.float32)
            grad_out = self.cot[rows, :].astype(jnp.float32) * live
            self.out[rows, :] = out.astype(jnp.bfloat16)
            scaled = grad_out * self.term(13)
            grad = rstd * (
                scaled
                - jnp.mean(scaled, -1, keepdims=True)
                - normed * jnp.mean(scaled * normed, -1, keepdims=True)
            )
            self.add_term(13, grad_out * normed)
            self.add_term(14, grad_out)
            grad_down = grad.astype(jnp.bfloat16)
            self.add_term(12, grad_down.astype(jnp.float32))
            self.grad[rows, :] = grad
            self.down[rows, :] = grad_down
            self.down_t[:, rows] = grad_down.T

        loop(self.tiles, step, beside)


    def hidden_back(self, part, beside=()):
        def step(r):
            rows = tile(r, WIDE)
            grad_act = dot_nt(self.down[rows, :], self.down_weight(part))
            at = self.some(self.slope, part, r, WIDE)
            slope = self.slope[at].reshape(WIDE, D).astype(jnp.float32)
            inner = (grad_act * slope).astype(jnp.bfloat16)
            self.slope[at] = inner.reshape(-1, self.slope.shape[1], D)
            self.add_term(8 + part, inner.astype(jnp.float32))

        loop(self.seqs * self.length // WIDE, step, beside)

    def down_grads(self, part, beside=()):
        deep = self.ffn_w.shape[2]
        first = self.ffn_split + 2 * part

        def step(m):
            grads = dot(self.down_t[tile(m, 2 * deep), :], self.whole(self.act, part)).astype(jnp.bfloat16)
            for owner in range(2):
                for block in range(6):
                    at = 128 * (3 * owner + block % 3)
                    self.ffn_w[first + owner, m, :, pl.ds(128 * block, 128)] = grads[
                        deep * (block // 3) : deep * (block // 3 + 1), at : at + 128
                    ]

        loop(4, step, beside)

    def in_back(self, part, beside=()):
        def step(r):
            rows = tile(r, WIDE)
            self.grad[rows, :] += dot_nt(
                self.slope[self.some(self.slope, part, r, WIDE)].reshape(WIDE, D), self.in_weight(part)
            )

        loop(self.seqs * self.length // WIDE, step, beside)

    def in_grads(self, part, beside=()):
        deep = self.ffn_w.shape[2]

        def step(m):
            grads = dot(self.low_t[tile(m, 2 * deep), :], self.whole(self.slope, part)).astype(jnp.bfloat16)
            self.ffn_w[pl.ds(2 * m, 2), part] = grads.reshape(2, deep, D)

        loop(4, step, beside)

    def first_back(self, beside=()):
        def step(r):
            rows = tile(r, TILE)
            grad_first, normed = self.grad[rows, :], self.hat[rows, :]
            scaled = grad_first * self.term(3)
            grad = self.rstd[rows, :] * (
                scaled
                - jnp.mean(scaled, -1, keepdims=True)
                - normed * jnp.mean(scaled * normed, -1, keepdims=True)
            )
            self.add_term(3, grad_first * normed)
            self.add_term(4, grad_first)
            proj = grad.astype(jnp.bfloat16)
            self.add_term(2, proj.astype(jnp.float32))
            self.grad[rows, :] = grad
            shape = (-1, self.act.shape[1], D)
            self.act[self.some(self.act, 3, r)] = proj.reshape(shape)
            grad_context = dot_nt(proj, self.out_weight()).astype(jnp.bfloat16)
            self.act[self.some(self.act, 0, r)] = grad_context.reshape(shape)
            self.tok_t[:, rows] = self.tok[rows, :].T

        loop(self.tiles, step, beside)

    def out_grads(self, beside=()):
        def step(m):
            grads = dot(self.ctx_t[tile(m, 192), :], self.whole(self.act, 3)).astype(jnp.bfloat16)
            self.att_w[self.att_split + m] = grads.reshape(self.att_w.shape[1:])

        loop(4, step, beside)

    def attend_back(self, group, beside=()):
        def step(i):
            seq, pair = i % self.seqs, 2 * group + i // self.seqs
            lanes = tile(pair, 2 * HEAD_DIM)
            rows = tile(seq, self.length)
            count = self.length // self.act.shape[1]
            queries, keys, values = (self.heads[j, rows, lanes] for j in range(3))
            grads = self.act[pl.ds(count * seq, count), :, lanes].reshape(self.length, 2 * HEAD_DIM)
            keys_t = keys.T
            parts = []
            grad_keys = grad_values = 0.0
            for half in range(2):
                here = self.lane_half(half)
                own = jnp.where(here, queries, jnp.zeros_like(queries))
                own_grads = jnp.where(here, grads, jnp.zeros_like(grads))
                total = self.totals[pl.ds(HEADS * seq + 2 * pair + half, 1), :]
                probs = jnp.exp(dot_nt(keys, own) + self.bias[rows, :] - total)
                grad_values = grad_values + dot(probs.astype(jnp.bfloat16), own_grads)
                grad_probs = dot_nt(values, own_grads)
                row_sum = jnp.sum(probs * grad_probs, 0, keepdims=True)
                grad_scores = (probs * (grad_probs - row_sum)).astype(jnp.bfloat16)
                grad_keys = grad_keys + dot(grad_scores, own)
                parts.append(dot(keys_t[HEAD_DIM * half : HEAD_DIM * (half + 1)], grad_scores))
            grad_queries = (jnp.concatenate(parts, 0) * HEAD_DIM ** (-0.5)).astype(jnp.bfloat16).T
            grad_values = grad_values.astype(jnp.bfloat16)
            self.heads[0, rows, lanes] = grad_queries
            self.heads[1, rows, lanes] = grad_keys.astype(jnp.bfloat16)
            self.heads[2, rows, lanes] = grad_values
            for row, grad in ((0, grad_queries), (1, grad_values)):
                self.term_grads[pl.ds(row, 1), lanes] += jnp.sum(grad.astype(jnp.float32), 0, keepdims=True)

        loop(2 * self.seqs, step, beside)

    def qkv_grads(self, group):
        lanes = pl.ds(4 * HEAD_DIM * group, 4 * HEAD_DIM)
        deep = self.att_w.shape[2]

        def step(part):
            grads = dot(self.tok_t[...], self.heads[part, :, lanes]).astype(jnp.bfloat16)
            for chip in range(self.att_split):
                self.act[self.act_first + 3 * chip + part, :, lanes] = grads[deep * chip : deep * (chip + 1)]

        loop(3, step)

    def input_back(self, beside=()):
        def step(r):
            rows = tile(r, TILE)
            total = self.grad[rows, :]
            for part in range(3):
                total = total + dot_nt(self.heads[part, rows, :], self.qkv_weight(part))
            self.gin[rows, :] = total.astype(jnp.bfloat16)

        loop(self.tiles, step, beside)


def gelu_parts(values):
    cdf = 0.5 * (1.0 + lax.erf(values * 0.5**0.5))
    return cdf, cdf + values * jnp.exp(-0.5 * values * values) * (2.0 * math.pi) ** (-0.5)


def batches(levels):
    return [(level,) for level in range(levels)], [(levels - 1,)], [tuple(range(levels - 1))]


def scratch_shapes(levels, att, ffn, rows, seqs, length):
    bf16, f32 = jnp.bfloat16, jnp.float32
    vmem, dma = pltpu.VMEM, pltpu.SemaphoreType.DMA
    chips = att.chips
    turned = vmem((D, rows), bf16)
    f_batches, o_batches, q_batches = batches(levels)
    shapes = dict(
        att_w=vmem((chips, att.parts, att.deep, D), bf16),
        ffn_w=vmem((chips, ffn.parts, ffn.deep, D), bf16),
        tok=vmem((rows, D), bf16),
        heads=vmem((3, rows, D), bf16),
        totals=vmem((seqs * HEADS, length), f32),
        ctx=vmem((rows, D), bf16),
        ctx_t=turned,
        hat=vmem((rows, D), f32),
        rstd=vmem((rows, 1), f32),
        low_t=turned,
        act=vmem((4 * rows // att.deep, att.deep, D), bf16),
        slope=vmem((8 * rows // att.deep, att.deep // 2, D), bf16),
        grad=vmem((rows, D), f32),
        down_t=turned,
        terms=vmem((16, D), f32),
        term_grads=vmem((16, D), f32),
        spare=vmem((48, 128), f32),
        terms_sum=vmem((2, 16, D // 2), f32),
        terms_got=vmem((2 + levels, 16, D // 2), f32),
        terms_all=vmem((2, 16, D // 2), f32),
        ffn_slots=vmem((chips + 4 * levels, ffn.parts, ffn.deep // 2, D), bf16),
        local_sem=dma((8,)),
        term_send=dma((3,)),
        term_recv=dma,
        sum_send=dma((5,)),
        sum_recv=dma((5,)),
        free=pltpu.SemaphoreType.REGULAR,
        ffn_extra=vmem((ffn.parts, ffn.deep // 2, D), bf16),
        f_send=dma((5,)),
        f_line=dma((2, levels)),
        f_recv=dma((len(f_batches), 5)),
        o_send=dma((5,)),
        o_recv=dma((len(o_batches), 5)),
        q_send=dma((3, 5)),
        q_recv=dma((3, len(q_batches), 5)),
    )
    for name, flat in (("att_", att), ("ffn_", ffn)):
        half = (flat.parts, flat.deep // 2, D)
        own = dict(
            long=vmem((flat.halo + flat.held + 8, 128), f32),
            halo=vmem((flat.tail + flat.halo + 8, 128), f32),
            line=vmem((flat.lines + flat.halo + 8, 128), f32),
            own=vmem((2, *half), f32),
            send=dma((5,)),
            recv=dma((chips,)),
            sib=dma,
            plane_send=dma((5,)),
            plane_recv=dma((levels + 2,)),
            plane_sib=dma,
            halo_send=dma,
            halo_recv=dma,
            own_send=dma,
            own_recv=dma,
            back_send=dma,
            back_recv=dma,
        )
        shapes.update({name + key: shape for key, shape in own.items()})
    return shapes


def layer_kernel(names, levels, att, ffn, seqs, length, att_in, ffn_in, tok_in, cot_in, segs, live_count,
                 out_out, gin_out, att_out, ffn_out, *scratch):
    s = types.SimpleNamespace(**dict(zip(names, scratch)))
    act_first = s.act.shape[0] // 4
    refs = dict(vars(s), segs=segs, live_count=live_count)
    refs.update(cot=s.tok, out=s.tok, down=s.ctx, tok_t=s.low_t)
    refs.update(bias=s.hat.at[:, pl.ds(0, length)], gin=s.tok, act_first=act_first)
    work = Layer(refs, att.split, ffn.split, seqs, length)

    def local(src, dst, at):
        copy = pltpu.make_async_copy(src, dst, s.local_sem.at[at])
        copy.start()
        return copy

    p = Place(levels)
    get_a = local(att_in, s.att_long.at[pl.ds(att.halo, att.held), :], 0)
    get_f = local(ffn_in, s.ffn_long.at[pl.ds(ffn.halo, ffn.held), :], 1)
    get_t = local(tok_in, s.tok, 2)
    p.meet()
    sends = Sends()
    lead_a = Lead(p, sends, att, s.att_long, s.att_halo, s.att_line, s.att_halo_send, s.att_halo_recv)
    lead_f = Lead(p, sends, ffn, s.ffn_long, s.ffn_halo, s.ffn_line, s.ffn_halo_send, s.ffn_halo_recv)
    get_a.wait()
    sends.go(lead_a.begin)
    get_f.wait()
    sends.go(lead_f.begin)
    lead_a.lines()
    lead_a.store(s.att_w)
    def gathers(ref, cut, *sems):
        parts, lanes = ref.shape[1], pl.ds(0, D)
        if cut[0]:
            first, last = (pl.ds(0, parts - cut[0]), lanes), (pl.ds(parts - cut[0], cut[0]), lanes)
        else:
            first = (pl.ds(0, parts), pl.ds(0, D - cut[1]))
            last = (pl.ds(0, parts), pl.ds(D - cut[1], cut[1]))
        go, plane = Gather(p, ref, *first, *sems[:3]), Plane(p, ref, *last, *sems[3:])
        return go, plane

    go_a = gathers(
        s.att_w, (0, 128), s.att_send, s.att_recv, s.att_sib, s.att_plane_send, s.att_plane_recv, s.att_plane_sib
    )
    go_f = gathers(
        s.ffn_w, (1, 0), s.ffn_send, s.ffn_recv, s.ffn_sib, s.ffn_plane_send, s.ffn_plane_recv, s.ffn_plane_sib
    )
    (a, a_plane), (f, f_plane) = go_a, go_f
    a.own()
    a_plane.own()

    def last():
        terms, spare = s.terms, s.spare
        terms[...] = jnp.zeros(terms.shape, terms.dtype)
        for lead, at, count in ((lead_a, 0, 5), (lead_f, 8, 7)):
            rows = lead.last_rows(count)
            spare[pl.ds(0, rows.shape[0]), :] = rows
            for block in range(D // 128):
                terms[pl.ds(at, count), pl.ds(128 * block, 128)] = spare[pl.ds(block, count, stride=6), :]

    pl.when(p.d == att.chips - 1)(last)
    lead_f.lines()
    lead_f.store(s.ffn_w)
    s.term_grads[...] = jnp.zeros(s.term_grads.shape, jnp.float32)
    a.over_a(0)
    a_plane.near()
    a.line(1)
    a.line(2)
    a_plane.complete()
    a.over_a(1)
    a_plane.line(1)
    a.over_a(2)
    f_plane.own()
    a.line(3)
    a_plane.line(2)
    a.over_a(3)
    a.over_b(0)
    f.own()
    f_plane.near()
    a.over_b(1)
    f.line(1)
    a.over_b(2)
    a.over_b(3)
    a_plane.line(3)
    sends.go(Spread(p, sends, s.terms, s.term_send, s.term_recv).run)
    for go in go_a:
        go.from_sibling()
    get_t.wait()

    on = functools.partial
    work.qkv(((3, on(f.line, 2)), (3, on(f.over_a, 0))))
    work.attend(
        (
            (0, f_plane.complete),
            (3, on(f.line, 3)),
            (5, on(f_plane.line, 1)),
            (7, on(f.over_a, 1)),
            (8, on(f.over_a, 2)),
            (9, on(f_plane.line, 2)),
            (9, on(f.over_b, 0)),
            (9, on(f.over_a, 3)),
        )
    )
    work.first_norm()
    f.over_b(1)
    f.over_b(2)
    f_plane.line(3)
    f.over_b(3)
    get_c = local(cot_in, s.tok, 2)
    for go in go_f:
        go.from_sibling()
    get_c.wait()
    work.feed()
    put_o = local(s.tok, out_out, 3)
    sends.finish()
    for go in (*go_a, *go_f):
        go.finish()

    sums = Sends()
    slots, slope, act = s.ffn_slots, s.slope, s.act
    half_a, half_f = att.deep // 2, ffn.deep // 2

    def of(ref, half):
        return lambda chip, core: ref.at[chip, :, tile(core, half), :]

    def att_slots(lanes):
        return lambda i, count: slope.at[pl.ds(3 * i, 3 * count), :, lanes]

    f_batches, o_batches, q_batches = batches(levels)
    everything = pl.ds(0, D)
    ffn_slots = lambda i, count: slots.at[i] if count == 1 else slots.at[pl.ds(i, count)]
    add_f = Chain(
        s.ffn_extra, s.f_line, p, 4, ffn.chips, f_batches, of(s.ffn_w, half_f), ffn_slots,
        lambda core: s.ffn_own.at[core], s.f_send, s.f_recv,
    )
    add_o = Reduce(
        p, 3, att.chips, o_batches, of(s.att_w, half_a), att_slots(everything),
        lambda core: s.att_own.at[core], s.o_send, s.o_recv,
    )
    add_q = []
    for group in range(3):
        lanes = pl.ds(256 * group, 256)
        blocks = pl.ds(act_first, 3 * att.split)
        view = lambda chip, core, lanes=lanes: act.at[pl.ds(act_first + 3 * chip, 3), tile(core, half_a), lanes]
        whole = (act.at[blocks, tile(1 - p.c, half_a), lanes], slope.at[pl.ds(0, 3 * att.split), :, lanes])
        add_q.append(
            Reduce(
                p, 3, att.chips, q_batches, view, att_slots(lanes),
                lambda core, lanes=lanes: s.att_own.at[core, :, :, lanes], s.q_send.at[group], s.q_recv.at[group], whole,
            )
        )
    add_t = Terms(p, sums, s.terms_sum, s.terms_got, s.terms_all, s.sum_send, s.sum_recv)

    def do(act, *at):
        return sums.later(functools.partial(act, *at))

    work.hidden_back(0)
    work.down_grads(0)
    work.hidden_back(1)
    work.down_grads(1)
    add_f.share(2)
    put_o.wait()
    get_t = local(tok_in, s.tok, 2)
    work.hidden_back(2)
    work.down_grads(2, ((0, on(add_f.over_b, 2)),))
    work.hidden_back(3)
    work.down_grads(3)
    add_f.share(3)
    work.in_back(0, ((1, on(add_f.over_b, 3)),))
    work.in_grads(0)
    work.in_back(1, ((1, on(add_f.over_a, 2)),))
    work.in_grads(1)
    work.in_back(2)
    work.in_grads(2)
    work.in_back(3, ((1, on(add_f.collect, 2)), (1, on(add_f.line, 2, 2))))
    work.in_grads(3, ((1, on(add_f.over_a, 3)),))
    add_f.share(0)
    add_f.share(1)

    line = [(p.turn(distance), p.c) for distance in range(1, levels)]
    for device in (p.sibling, p.across_a, p.across_b, *line):
        pl.semaphore_signal(s.free, inc=1, device_id=device, device_id_type=MESH_ID)
    get_t.wait()
    work.first_back(((1, on(add_f.over_b, 0)),))
    work.out_grads(((3, on(add_f.line, 1, 2)),))
    pl.semaphore_wait(s.free, 2 + levels)
    add_o.share(0)
    work.make_bias()
    work.attend_back(
        0,
        (
            (0, on(add_f.over_b, 1)),
            (1, on(add_f.collect, 3)),
            (1, on(add_f.line, 3, 3)),
            (2, on(add_f.over_a, 0)),
            (3, on(add_o.over_b, 0)),
        ),
    )
    work.qkv_grads(0)
    q = add_q
    q[0].share(0)
    work.attend_back(
        1,
        (
            (0, on(q[0].over_b, 0)),
            (1, on(add_f.line, 2, 3)),
            (1, on(add_f.collect, 0)),
            (1, on(add_f.line, 3, 0)),
            (2, on(add_f.over_a, 1)),
            (3, on(q[0].over_a, 0)),
            (3, on(add_o.over_a, 0)),
        ),
    )
    work.qkv_grads(1)
    q[1].share(0)
    work.attend_back(
        2,
        (
            (0, on(add_f.line, 1, 3)),
            (0, on(add_f.line, 2, 0)),
            (0, on(add_f.collect, 1)),
            (0, on(add_f.line, 2, 1)),
            (0, on(q[1].over_b, 0)),
            (1, on(q[0].collect, 0)),
            (1, on(q[0].line, 0)),
            (1, on(add_o.collect, 0)),
            (1, on(add_o.line, 0)),
            (3, on(q[1].over_a, 0)),
        ),
    )
    work.qkv_grads(2)
    q[2].share(0)
    for core in range(2):
        s.terms_sum[core] = s.term_grads[:, pl.ds(D // 2 * core, D // 2)]
    do(add_t.share)()
    trail_f = Trail(p, sums, ffn, s.ffn_own, s.ffn_line, s.ffn_long, s.ffn_back_send, s.ffn_back_recv)
    trail_a = Trail(p, sums, att, s.att_own, s.att_line, s.att_long, s.att_back_send, s.att_back_recv)
    given_f = lambda core: handed(p, s.ffn_own, core, s.ffn_own_send, s.ffn_own_recv)
    given_a = lambda core: handed(p, s.att_own, core, s.att_own_send, s.att_own_recv)
    add_f.line(1, 0)
    add_f.line(1, 1)
    work.input_back(
        (
            (0, on(q[2].over_b, 0)),
            (0, do(add_t.over_b)),
            (1, on(q[1].collect, 0)),
            (1, on(q[1].line, 0)),
            (2, do(add_t.over_a)),
            (3, on(q[2].over_a, 0)),
            (3, do(add_t.line)),
        )
    )
    put_g = local(work.gin, gin_out, 4)
    add_f.keep()
    sums.go(lambda: sums.start(None, lambda: given_f(p.c)))
    add_o.keep()
    q[0].keep()
    q[2].collect(0)
    q[2].line(0)
    given_f(1 - p.c).wait_recv()
    trail_f.lines()
    sums.go(trail_f.pass_back)
    q[1].keep()
    do(add_t.hand_over)()
    final = p.d == att.chips - 1

    def terms_here():
        add_t.take_over()
        trail_f.last_rows(s.terms_all, 8, 7)
        trail_a.last_rows(s.terms_all, 0, 5)

    pl.when(final)(terms_here)
    trail_f.out()
    put_f = local(s.ffn_long.at[pl.ds(0, ffn.held), :], ffn_out, 1)
    q[2].keep()
    sums.go(lambda: sums.start(None, lambda: given_a(p.c)))
    given_a(1 - p.c).wait_recv()
    trail_a.lines()
    sums.go(trail_a.pass_back)
    trail_a.out()
    put_a = local(s.att_long.at[pl.ds(0, att.held), :], att_out, 0)
    sums.finish()
    for who in (add_f, add_o, *q):
        who.finish()
    for copy in (put_g, put_f, put_a):
        copy.wait()


def run_layer(levels, att, ffn, att_lines, ffn_lines, tokens, cotangent, segments, live_count):
    vmem = pl.BlockSpec(memory_space=pltpu.VMEM)
    anywhere = pl.BlockSpec(memory_space=pl.ANY)
    seqs, length = segments.shape
    rows = tokens.shape[0]
    bf16, f32 = jnp.bfloat16, jnp.float32
    shape = jax.ShapeDtypeStruct
    scratch = scratch_shapes(levels, att, ffn, rows, seqs, length)
    return pl.pallas_call(
        functools.partial(layer_kernel, tuple(scratch), levels, att, ffn, seqs, length),
        out_shape=(
            shape(tokens.shape, bf16),
            shape(tokens.shape, bf16),
            shape((att.held, 128), f32),
            shape((ffn.held, 128), f32),
        ),
        in_specs=[anywhere, anywhere, anywhere, anywhere, vmem, pl.BlockSpec(memory_space=pltpu.SMEM)],
        out_specs=(anywhere, anywhere, anywhere, anywhere),
        scratch_shapes=list(scratch.values()),
        compiler_params=pltpu.CompilerParams(
            collective_id=1, has_side_effects=True, vmem_limit_bytes=64 * 2**20
        ),
        name="layer",
    )(att_lines, ffn_lines, tokens, cotangent, segments, live_count)


def as_lines(flat, vector):
    return jnp.pad(vector, (0, flat.held * 128 - flat.length)).reshape(flat.held, 128)


def fast_body(
    levels,
    tokens,
    cotangent,
    segments,
    live_count,
    att_master,
    att_first,
    att_second,
    ffn_master,
    ffn_first,
    ffn_second,
):
    chips = lax.axis_size("dp")
    att = Flat(att_master.shape[0], chips, 3, 3 * chips // 4, False)
    ffn = Flat(ffn_master.shape[0], chips, 4, chips // 2, True)
    output, input_grad, att_sum, ffn_sum = run_layer(
        levels,
        att,
        ffn,
        as_lines(att, att_master),
        as_lines(ffn, ffn_master),
        tokens,
        cotangent,
        segments,
        live_count,
    )
    att_grad = att_sum.reshape(-1)[: att.length]
    ffn_grad = ffn_sum.reshape(-1)[: ffn.length]
    att_new = adam_update(att_master, att_first, att_second, att_grad)
    ffn_new = adam_update(ffn_master, ffn_first, ffn_second, ffn_grad)
    return (output, input_grad, att_grad, *att_new, ffn_grad, *ffn_new)


def body_for(mesh):
    chips, cores = mesh.shape["dp"], mesh.shape["rep"]
    if chips == 16 and cores == 2:
        return functools.partial(fast_body, chips // 4)
    return general_body


def solution(mesh):
    placed = (
        P(("dp", "rep"), None),
        P(("dp", "rep"), None),
        P(("dp", "rep"), None),
        P(("dp", "rep")),
        P("dp"),
        P("dp"),
        P("dp"),
        P("dp"),
        P("dp"),
        P("dp"),
    )
    return jax.shard_map(
        body_for(mesh),
        mesh=mesh,
        in_specs=placed,
        out_specs=(
            P(("dp", "rep"), None),
            P(("dp", "rep"), None),
            P("dp"),
            P("dp"),
            P("dp"),
            P("dp"),
            P("dp"),
            P("dp"),
            P("dp"),
            P("dp"),
        ),
        check_vma=False,
    )
```

```python
import functools
import math
import types

import jax
import jax.numpy as jnp
from jax import lax
from jax.experimental import pallas as pl
from jax.experimental.pallas import tpu as pltpu
from jax.sharding import PartitionSpec as P

D = 768
HEADS = 12
HEAD_DIM = 64
FF = 3072
STEP = 10


norm_eps = 1e-05
beta_one = 0.9
beta_two = 0.98
decay = 0.01
adam_eps = 1e-08
masked = -1e30


def split_attention(flat_params):
    qkv_weight = flat_params[: 3 * D * D].reshape(D, 3 * D)
    offset = 3 * D * D
    out_weight = flat_params[offset : offset + D * D].reshape(D, D)
    offset = offset + D * D
    att_terms = flat_params[offset : offset + 5 * D].reshape(5, D).astype(jnp.float32)
    return (qkv_weight, out_weight, att_terms)


def split_ffn(flat_params):
    in_weight = flat_params[: D * FF].reshape(D, FF)
    offset = D * FF
    down_weight = flat_params[offset : offset + FF * D].reshape(FF, D)
    offset = offset + FF * D
    in_bias = flat_params[offset : offset + FF].astype(jnp.float32)
    offset = offset + FF
    ffn_terms = flat_params[offset : offset + 3 * D].reshape(3, D).astype(jnp.float32)
    return (in_weight, down_weight, in_bias, ffn_terms)


def normalize(values, gain, shift):
    row_mean = jnp.mean(values, -1, keepdims=True)
    centred = values - row_mean
    rstd_rows = lax.rsqrt(jnp.mean(centred * centred, -1, keepdims=True) + norm_eps)
    normed = centred * rstd_rows
    return (normed * gain + shift, normed, rstd_rows)


def norm_back(grad_in, normed, rstd_rows, gain):
    scaled = grad_in * gain
    grad_rows = rstd_rows * (
        scaled
        - jnp.mean(scaled, -1, keepdims=True)
        - normed * jnp.mean(scaled * normed, -1, keepdims=True)
    )
    return (grad_rows, jnp.sum(grad_in * normed, 0), jnp.sum(grad_in, 0))


def gelu_slope(values):
    normal_cdf = 0.5 * (1.0 + lax.erf(values * 0.5**0.5))
    return normal_cdf + values * jnp.exp(-0.5 * values * values) * (2.0 * math.pi) ** (-0.5)


def masked_scores(query_rows, key_rows, seg_ids):
    scores = jnp.einsum(
        "qhd,khd->hqk", query_rows, key_rows, preferred_element_type=jnp.float32
    ) * HEAD_DIM ** (-0.5)
    same_doc = seg_ids[:, None] == seg_ids[None, :]
    return jnp.where(same_doc[None], scores, masked)


def attend_forward(block):
    query_rows, key_rows, value_rows, seg_ids = block
    scores = masked_scores(query_rows, key_rows, seg_ids)
    row_top = jnp.max(scores, -1, keepdims=True)
    raised = jnp.exp(scores - row_top)
    row_total = jnp.sum(raised, -1, keepdims=True)
    soft_probs = (raised / row_total).astype(jnp.bfloat16)
    context = jnp.einsum("hqk,khd->qhd", soft_probs, value_rows, preferred_element_type=jnp.float32)
    return (
        context.astype(jnp.bfloat16).reshape(context.shape[0], -1),
        row_top + jnp.log(row_total),
    )


def attend_backward(query_rows, key_rows, value_rows, seg_ids, log_total, grad_context):
    soft_probs = jnp.exp(masked_scores(query_rows, key_rows, seg_ids) - log_total)
    grad_probs = jnp.einsum(
        "qhd,khd->hqk", grad_context, value_rows, preferred_element_type=jnp.float32
    )
    grad_values = jnp.einsum(
        "hqk,qhd->khd",
        soft_probs.astype(jnp.bfloat16),
        grad_context,
        preferred_element_type=jnp.float32,
    )
    grad_scores = soft_probs * (grad_probs - jnp.sum(soft_probs * grad_probs, -1, keepdims=True))
    grad_scores = grad_scores.astype(jnp.bfloat16)
    grad_queries = jnp.einsum(
        "hqk,khd->qhd", grad_scores, key_rows, preferred_element_type=jnp.float32
    ) * HEAD_DIM ** (-0.5)
    grad_keys = jnp.einsum(
        "hqk,qhd->khd", grad_scores, query_rows, preferred_element_type=jnp.float32
    ) * HEAD_DIM ** (-0.5)
    length_here = query_rows.shape[0]
    return jnp.concatenate(
        [
            grad_queries.reshape(length_here, -1),
            grad_keys.reshape(length_here, -1),
            grad_values.reshape(length_here, -1),
        ],
        -1,
    )


def adam_update(master, first, second, grad):
    first_new = beta_one * first + (1.0 - beta_one) * grad
    second_new = beta_two * second + (1.0 - beta_two) * grad * grad
    fix_one = 1.0 - beta_one**STEP
    fix_two = 1.0 - beta_two**STEP
    update = first_new / fix_one / (jnp.sqrt(second_new / fix_two) + adam_eps)
    return (first_new, second_new, update + decay * master)


def general_body(
    tokens,
    cotangent,
    segments,
    live_count,
    att_master,
    att_first,
    att_second,
    ffn_master,
    ffn_first,
    ffn_second,
):
    seq_count = segments.shape[0]
    length = segments.shape[1]
    att_full = lax.all_gather(att_master.astype(jnp.bfloat16), "dp", axis=0, tiled=True)
    qkv_weight, out_weight, att_terms = split_attention(att_full)
    bias_qkv = jnp.concatenate([att_terms[0], jnp.zeros_like(att_terms[0]), att_terms[1]])
    qkv = (jnp.dot(tokens, qkv_weight, preferred_element_type=jnp.float32) + bias_qkv).astype(
        jnp.bfloat16
    )
    head_split = qkv.reshape(seq_count, length, 3, HEADS, HEAD_DIM)
    context, log_total = lax.map(
        attend_forward, (head_split[:, :, 0], head_split[:, :, 1], head_split[:, :, 2], segments)
    )
    context = context.reshape(-1, D)
    residual = (
        tokens.astype(jnp.float32)
        + jnp.dot(context, out_weight, preferred_element_type=jnp.float32)
        + att_terms[2]
    )
    first_out, first_hat, first_rstd = normalize(residual, att_terms[3], att_terms[4])
    ffn_full = lax.all_gather(ffn_master.astype(jnp.bfloat16), "dp", axis=0, tiled=True)
    in_weight, down_weight, in_bias, ffn_terms = split_ffn(ffn_full)
    first_low = first_out.astype(jnp.bfloat16)
    ffn_inner = jnp.dot(first_low, in_weight, preferred_element_type=jnp.float32) + in_bias
    ffn_act = jax.nn.gelu(ffn_inner, approximate=False).astype(jnp.bfloat16)
    second_in = (
        first_out + jnp.dot(ffn_act, down_weight, preferred_element_type=jnp.float32) + ffn_terms[0]
    )
    output, second_hat, second_rstd = normalize(second_in, ffn_terms[1], ffn_terms[2])
    att_back = lax.all_gather(att_master.astype(jnp.bfloat16), "dp", axis=0, tiled=True)
    qkv_weight, out_weight, att_terms = split_attention(att_back)
    ffn_back = lax.all_gather(ffn_master.astype(jnp.bfloat16), "dp", axis=0, tiled=True)
    in_weight, down_weight, in_bias, ffn_terms = split_ffn(ffn_back)

    def microbatch(micro_index, state_now):
        grad_sums, input_grads = state_now

        def take_rows(array_in):
            return lax.dynamic_slice_in_dim(array_in, micro_index * length, length, 0)

        grad_out = take_rows(cotangent).astype(jnp.float32)
        grad_second, grad_gain_two, grad_shift_two = norm_back(
            grad_out, take_rows(second_hat), take_rows(second_rstd), ffn_terms[1]
        )
        grad_down = grad_second.astype(jnp.bfloat16)
        grad_down_bias = jnp.sum(grad_down.astype(jnp.float32), 0)
        grad_down_weight = jnp.dot(
            take_rows(ffn_act).T, grad_down, preferred_element_type=jnp.float32
        )
        grad_act = jnp.dot(grad_down, down_weight.T, preferred_element_type=jnp.float32)
        grad_inner = (grad_act * gelu_slope(take_rows(ffn_inner))).astype(jnp.bfloat16)
        grad_in_bias = jnp.sum(grad_inner.astype(jnp.float32), 0)
        grad_in_weight = jnp.dot(
            take_rows(first_low).T, grad_inner, preferred_element_type=jnp.float32
        )
        grad_first = grad_second + jnp.dot(
            grad_inner, in_weight.T, preferred_element_type=jnp.float32
        )
        grad_residual, grad_gain_one, grad_shift_one = norm_back(
            grad_first, take_rows(first_hat), take_rows(first_rstd), att_terms[3]
        )
        grad_proj = grad_residual.astype(jnp.bfloat16)
        grad_out_bias = jnp.sum(grad_proj.astype(jnp.float32), 0)
        grad_out_weight = jnp.dot(
            take_rows(context).T, grad_proj, preferred_element_type=jnp.float32
        )
        grad_context = jnp.dot(grad_proj, out_weight.T, preferred_element_type=jnp.float32).astype(
            jnp.bfloat16
        )
        this_seq = lax.dynamic_index_in_dim(head_split, micro_index, 0, keepdims=False)
        this_segs = lax.dynamic_index_in_dim(segments, micro_index, 0, keepdims=False)
        this_total = lax.dynamic_index_in_dim(log_total, micro_index, 0, keepdims=False)
        grad_qkv = attend_backward(
            this_seq[:, 0],
            this_seq[:, 1],
            this_seq[:, 2],
            this_segs,
            this_total,
            grad_context.reshape(length, HEADS, HEAD_DIM),
        )
        grad_qkv = grad_qkv.astype(jnp.bfloat16)
        grad_wide = grad_qkv.astype(jnp.float32)
        grad_query_bias = jnp.sum(grad_wide[:, :D], 0)
        grad_value_bias = jnp.sum(grad_wide[:, 2 * D :], 0)
        grad_qkv_weight = jnp.dot(take_rows(tokens).T, grad_qkv, preferred_element_type=jnp.float32)
        grad_tokens = (
            jnp.dot(grad_qkv, qkv_weight.T, preferred_element_type=jnp.float32) + grad_residual
        )
        input_grads = lax.dynamic_update_slice_in_dim(
            input_grads, grad_tokens.astype(jnp.bfloat16), micro_index * length, 0
        )
        terms_now = (
            grad_qkv_weight,
            grad_out_weight,
            grad_query_bias,
            grad_value_bias,
            grad_out_bias,
            grad_gain_one,
            grad_shift_one,
            grad_in_weight,
            grad_down_weight,
            grad_in_bias,
            grad_down_bias,
            grad_gain_two,
            grad_shift_two,
        )
        grad_sums = tuple((running + fresh for running, fresh in zip(grad_sums, terms_now)))
        return (grad_sums, input_grads)

    zero_sums = (
        jnp.zeros((D, 3 * D), jnp.float32),
        jnp.zeros((D, D), jnp.float32),
        jnp.zeros((D,), jnp.float32),
        jnp.zeros((D,), jnp.float32),
        jnp.zeros((D,), jnp.float32),
        jnp.zeros((D,), jnp.float32),
        jnp.zeros((D,), jnp.float32),
        jnp.zeros((D, FF), jnp.float32),
        jnp.zeros((FF, D), jnp.float32),
        jnp.zeros((FF,), jnp.float32),
        jnp.zeros((D,), jnp.float32),
        jnp.zeros((D,), jnp.float32),
        jnp.zeros((D,), jnp.float32),
    )
    zero_inputs = jnp.zeros(tokens.shape, jnp.bfloat16)
    grad_sums, input_grad = lax.fori_loop(0, live_count[0], microbatch, (zero_sums, zero_inputs))
    dp_count = lax.axis_size("dp")
    att_pad = att_master.shape[0] * dp_count - 4 * D * D - 5 * D
    ffn_pad = ffn_master.shape[0] * dp_count - 2 * D * FF - FF - 3 * D
    att_local = jnp.concatenate(
        [
            grad_sums[0].reshape(-1),
            grad_sums[1].reshape(-1),
            grad_sums[2],
            grad_sums[3],
            grad_sums[4],
            grad_sums[5],
            grad_sums[6],
            jnp.zeros((att_pad,), jnp.float32),
        ]
    )
    ffn_local = jnp.concatenate(
        [
            grad_sums[7].reshape(-1),
            grad_sums[8].reshape(-1),
            grad_sums[9],
            grad_sums[10],
            grad_sums[11],
            grad_sums[12],
            jnp.zeros((ffn_pad,), jnp.float32),
        ]
    )
    att_rows, ffn_rows = (
        lax.all_to_all(
            att_local.reshape(dp_count, -1).astype(jnp.bfloat16),
            "dp",
            split_axis=0,
            concat_axis=0,
            tiled=True,
        ).astype(jnp.float32),
        lax.all_to_all(
            ffn_local.reshape(dp_count, -1).astype(jnp.bfloat16),
            "dp",
            split_axis=0,
            concat_axis=0,
            tiled=True,
        ).astype(jnp.float32),
    )
    att_share = jnp.sum(att_rows, 0)
    ffn_share = jnp.sum(ffn_rows, 0)
    att_grad, ffn_grad = (
        lax.psum(att_share.astype(jnp.bfloat16), "rep").astype(jnp.float32),
        lax.psum(ffn_share.astype(jnp.bfloat16), "rep").astype(jnp.float32),
    )
    att_new = adam_update(att_master, att_first, att_second, att_grad)
    ffn_new = adam_update(ffn_master, ffn_first, ffn_second, ffn_grad)
    return (
        output.astype(jnp.bfloat16),
        input_grad,
        att_grad,
        att_new[0],
        att_new[1],
        att_new[2],
        ffn_grad,
        ffn_new[0],
        ffn_new[1],
        ffn_new[2],
    )


MESH_ID = pl.DeviceIdType.MESH


def when(cond, act):
    if cond is None:
        act()
    else:
        pl.when(cond)(act)


class Place:
    def __init__(self, levels):
        self.levels = levels
        d = lax.axis_index("dp")
        c = lax.axis_index("rep")
        self.d, self.c = d, c
        self.z, y, x = d // 4, (d // 2) % 2, d % 2
        x_near, y_near = d + 1 - 2 * x, d + 2 - 4 * y
        self.a_near = x_near + c * (y_near - x_near)
        self.b_near = y_near + c * (x_near - y_near)
        self.far = x_near + y_near - d
        self.a_at = x + c * (y - x)
        self.b_at = y + c * (x - y)
        self.up = (d + 4, c)
        self.down = (d - 4, c)
        self.has_up = self.z < levels - 1
        self.has_down = self.z > 0
        self.across_a = (self.a_near, c)
        self.across_b = (self.b_near, c)
        self.sibling = (d, 1 - c)

    def levels_at(self, distance):
        if distance == 0:
            return [(self.z, None, 0)]
        return [
            (self.z - distance, self.z >= distance, -1),
            (self.z + distance, self.z + distance < self.levels, 1),
        ]

    def at(self, column, level):
        return column + 4 * (level - self.z)

    def turn(self, distance):
        return self.at(self.d, (self.z + distance) % self.levels)

    def along(self, step):
        return (self.up, self.has_up) if step > 0 else (self.down, self.has_down)

    def meet(self):
        barrier = pltpu.get_barrier_semaphore()

        def greet(device):
            pl.semaphore_signal(barrier, inc=1, device_id=device, device_id_type=MESH_ID)

        for device in (self.across_a, self.across_b, self.sibling):
            greet(device)
        count = 3
        for distance in range(1, self.levels):
            greet((self.turn(distance), self.c))
            count += 1
        edges = [((self.d + 1, self.c), self.d < 4 * self.levels - 1), ((self.d - 1, self.c), self.d > 0)]
        for device, there in edges:
            pl.when(there)(functools.partial(greet, device))
            count = count + there.astype(jnp.int32)
        pl.semaphore_wait(barrier, count)


def both(first, second):
    if first is None:
        return second
    return first if second is None else first & second


class Sends:
    def __init__(self):
        self.steps, self.closing = [], False

    def go(self, step):
        if not any(step is other for other in self.steps):
            self.steps.append(step)
        step()

    def later(self, step):
        return lambda: self.go(step)

    def start(self, cond, make):
        when(cond, lambda: make().wait_send() if self.closing else make().start())

    def wait(self, cond, make):
        if not self.closing:
            when(cond, lambda: make().wait_recv())

    def finish(self):
        self.closing = True
        for step in self.steps:
            step()


def remote(src, dst, send_sem, recv_sem, device):
    return pltpu.make_async_remote_copy(
        src_ref=src,
        dst_ref=dst,
        send_sem=send_sem,
        recv_sem=recv_sem,
        device_id=device,
        device_id_type=MESH_ID,
    )


class Gather:
    def __init__(self, place, ref, parts, lanes, send_sem, recv_sem, sib_sem):
        self.place, self.ref, self.parts, self.lanes = place, ref, parts, lanes
        self.send_sem, self.recv_sem, self.sib_sem = send_sem, recv_sem, sib_sem
        self.half = ref.shape[2] // 2
        levels = place.levels
        self.leave = {2: levels, 3: 2 * levels, 4: 4 * levels - 1}
        self.together = 1

    def rows(self, core):
        return pl.ds(pl.multiple_of(core * self.half, self.half), self.half)

    def piece(self, chip, core):
        return self.ref.at[chip, self.parts, self.rows(core), self.lanes]

    def several(self, count):
        return self.ref.at[pl.ds(0, count), self.parts, pl.ds(0, self.half), self.lanes]

    def send(self, cond, chip, way, device):
        own = self.piece(chip, self.place.c)
        recv = self.sib_sem if way == 4 else self.recv_sem.at[chip]
        when(cond, lambda: remote(own, own, self.send_sem.at[way], recv, device).start())

    def wait(self, cond, part, sem):
        when(cond, lambda: remote(part, part, self.send_sem.at[0], sem, self.place.sibling).wait_recv())

    def arrived(self, cond, chip):
        self.wait(cond, self.piece(chip, self.place.c), self.recv_sem.at[chip])

    def own(self):
        p = self.place
        self.send(p.has_up, p.d, 0, p.up)
        self.send(p.has_down, p.d, 1, p.down)
        self.send(None, p.d, 3, p.across_b)
        self.send(None, p.d, 2, p.across_a)

    def line(self, distance):
        p = self.place
        for level, there, step in p.levels_at(distance):
            chip = p.at(p.d, level)
            self.arrived(there, chip)
            onward, more = p.along(-step)
            self.send(both(there, more), chip, 0 if step < 0 else 1, onward)
            self.send(there, chip, 3, p.across_b)
            self.send(there, chip, 2, p.across_a)
            self.send(there, chip, 4, p.sibling)

    def over_a(self, distance):
        p = self.place
        for level, there, _ in p.levels_at(distance):
            chip = p.at(p.a_near, level)
            self.arrived(there, chip)
            self.send(there, chip, 3, p.across_b)
            self.send(there, chip, 4, p.sibling)

    def over_b(self, distance):
        p = self.place
        for column in (p.b_near, p.far):
            for level, there, _ in p.levels_at(distance):
                chip = p.at(column, level)
                self.arrived(there, chip)
                self.send(there, chip, 4, p.sibling)

    def from_sibling(self):
        self.wait(None, self.several(4 * self.place.levels - 1), self.sib_sem)

    def left(self, cond, way, count):
        part = self.several(count)
        sem = self.send_sem.at[way]
        when(cond, lambda: remote(part, part, sem, self.sib_sem, self.place.sibling).wait_send())

    def finish(self):
        p = self.place
        for way, count in self.leave.items():
            self.left(None, way, count)
        for level in range(p.levels):
            if level < p.levels - 1:
                self.left(p.z == level, 0, self.together * (level + 1))
            if level > 0:
                self.left(p.z == level, 1, self.together * (p.levels - level))


class Plane(Gather):
    def __init__(self, place, ref, parts, lanes, send_sem, recv_sem, sib_sem):
        super().__init__(place, ref, parts, lanes, send_sem, recv_sem, sib_sem)
        self.leave = {2: 1, 3: 2, 4: 4 * place.levels - 1}
        self.together = 4
        self.from_a, self.from_b = place.levels, place.levels + 1

    def send(self, cond, chip, way, device):
        own = self.piece(chip, self.place.c)
        recv = self.sib_sem if way == 4 else self.recv_sem.at[self.from_a if way == 2 else self.from_b]
        when(cond, lambda: remote(own, own, self.send_sem.at[way], recv, device).start())

    def own(self):
        p = self.place
        self.send(None, p.d, 2, p.across_a)
        self.send(None, p.d, 3, p.across_b)

    def near(self):
        p = self.place
        self.wait(None, self.piece(p.a_near, p.c), self.recv_sem.at[self.from_a])
        self.send(None, p.a_near, 3, p.across_b)
        self.send(None, p.a_near, 4, p.sibling)

    def sheet(self, level):
        return self.ref.at[pl.ds(4 * level, 4), self.parts, self.rows(self.place.c), self.lanes]

    def send_sheet(self, cond, level, way, device):
        own = self.sheet(level)
        recv = self.sib_sem if way == 4 else self.recv_sem.at[level]
        when(cond, lambda: remote(own, own, self.send_sem.at[way], recv, device).start())

    def complete(self):
        p = self.place
        self.wait(None, self.several(2), self.recv_sem.at[self.from_b])
        self.send_sheet(p.has_up, p.z, 0, p.up)
        self.send_sheet(p.has_down, p.z, 1, p.down)
        for chip in (p.b_near, p.far):
            self.send(None, chip, 4, p.sibling)

    def line(self, distance):
        p = self.place
        for level, there, step in p.levels_at(distance):
            self.wait(there, self.sheet(level), self.recv_sem.at[level])
            onward, more = p.along(-step)
            self.send_sheet(both(there, more), level, 0 if step < 0 else 1, onward)
            self.send_sheet(there, level, 4, p.sibling)


class Spread:
    def __init__(self, place, sends, ref, send_sem, recv_sem):
        self.place, self.sends, self.ref = place, sends, ref
        self.send_sem, self.recv_sem = send_sem, recv_sem

    def copy(self, way, device):
        return remote(self.ref, self.ref, self.send_sem.at[way], self.recv_sem, device)

    def wait(self, cond):
        self.sends.wait(cond, lambda: self.copy(0, self.place.sibling))

    def run(self):
        p = self.place
        home = (p.a_at == 1) & (p.b_at == 1)
        self.wait(home & p.has_up)
        self.sends.start(home & p.has_down, lambda: self.copy(0, p.down))
        self.wait((p.a_at == 0) & (p.b_at == 1))
        self.sends.start(home, lambda: self.copy(1, p.across_a))
        self.wait(p.b_at == 0)
        self.sends.start(p.b_at == 1, lambda: self.copy(2, p.across_b))


def shifted(ref, start, rows):
    first, turn = start // 128, start % 128
    here = pltpu.roll(ref[pl.ds(first, rows), :], (128 - turn) % 128, 1)
    after = pltpu.roll(ref[pl.ds(first + 1, rows), :], (128 - turn) % 128, 1)
    lane = lax.broadcasted_iota(jnp.int32, (rows, 128), 1)
    return jnp.where(lane < 128 - turn, here, after)


class Flat:
    def __init__(self, length, chips, parts, split, turned):
        self.length, self.chips, self.parts, self.turned = length, chips, parts, turned
        self.rows = length // D // parts * parts
        self.slip = length - self.rows * D
        self.deep = self.rows // parts
        self.split = split
        self.lines = self.rows * (D // 128)
        self.most = self.slip * chips
        self.halo = -(-self.most // 1024) * 8
        self.held = -(-length // 1024) * 8
        self.tail_from = (length - self.most) // 1024 * 8
        self.tail = self.held - self.tail_from

    def place_of(self, part, block, split):
        if split:
            return 6 * part + block, 6 * self.parts
        return 6 * self.deep * part + block, 6


class Lead:
    def __init__(self, place, sends, flat, long_ref, halo_ref, line_ref, send_sem, recv_sem):
        self.place, self.sends, self.flat = place, sends, flat
        self.long_ref, self.halo_ref, self.line_ref = long_ref, halo_ref, line_ref
        self.send_sem, self.recv_sem = send_sem, recv_sem

    def copy(self):
        f, p = self.flat, self.place
        return remote(
            self.long_ref.at[pl.ds(f.halo + f.tail_from, f.tail), :],
            self.halo_ref.at[pl.ds(0, f.tail), :],
            self.send_sem,
            self.recv_sem,
            (p.d + 1, p.c),
        )

    def begin(self):
        self.sends.start(self.place.d < self.flat.chips - 1, self.copy)

    def lines(self):
        p, f = self.place, self.flat
        slip = f.slip * p.d
        self.line_ref[pl.ds(0, f.lines), :] = shifted(self.long_ref, f.halo * 128 - slip, f.lines)

        def mend():
            self.copy().wait_recv()
            before = shifted(self.halo_ref, f.length - f.tail_from * 128 - slip, f.halo)
            at = lax.broadcasted_iota(jnp.int32, (f.halo, 128), 0) * 128
            at = at + lax.broadcasted_iota(jnp.int32, (f.halo, 128), 1)
            self.line_ref[pl.ds(0, f.halo), :] = jnp.where(at < slip, before, self.line_ref[pl.ds(0, f.halo), :])

        pl.when(p.d > 0)(mend)

    def store(self, out_ref):
        p, f = self.place, self.flat

        def put(split):
            for part in range(f.parts):
                for block in range(D // 128):
                    first, stride = f.place_of(part, block, split)
                    out_ref[p.d, part, :, pl.ds(128 * block, 128)] = self.line_ref[
                        pl.ds(first, f.deep, stride=stride), :
                    ].astype(jnp.bfloat16)

        pl.when(p.d < f.split)(lambda: put(True))
        pl.when(p.d >= f.split)(lambda: put(False))

    def last_rows(self, count):
        f = self.flat
        lines = -(-count * 6 // 8) * 8
        return shifted(self.long_ref, f.halo * 128 + f.length - count * D, lines)


class Reduce:
    def __init__(self, place, parts, chips, batches, view, slots, kept, send_sem, recv_sem, whole=None):
        self.place, self.parts, self.batches = place, parts, batches
        self.view, self.slots, self.kept = view, slots, kept
        self.send_sem, self.recv_sem, self.whole = send_sem, recv_sem, whole
        self.levels = [level for batch in batches for level in batch]
        self.from_b, self.from_a = chips, chips + 2 * place.levels
        self.from_z = chips + 3 * place.levels

    def arrival(self, kind, batch):
        return self.recv_sem.at[batch, kind]

    def wait(self, part, sem):
        remote(part, part, self.send_sem.at[0], sem, self.place.sibling).wait_recv()

    def send(self, cond, chip, way, dst, recv, device):
        p = self.place
        src = self.view(chip, 1 - p.c if way == 4 else p.c)
        when(cond, lambda: remote(src, dst, self.send_sem.at[way], recv, device).start())

    def add(self, chip, src):
        here = self.view(chip, self.place.c)
        for part in range(self.parts):
            here[part] = here[part] + src[part]

    def share(self, batch):
        p = self.place
        recv = self.arrival(0, batch)
        if self.whole is not None:
            src, dst = self.whole
            remote(src, dst, self.send_sem.at[4], recv, p.sibling).start()
            return
        for level in self.batches[batch]:
            for column in (p.far, p.b_near, p.a_near, p.d):
                chip = p.at(column, level)
                self.send(None, chip, 4, self.slots(chip, 1), recv, p.sibling)

    def over_b(self, batch):
        p = self.place
        levels = self.batches[batch]
        self.wait(self.slots(4 * levels[0], 4 * len(levels)), self.arrival(0, batch))
        for kind, column in ((1, p.far), (0, p.b_near)):
            for level in levels:
                chip = p.at(column, level)
                self.add(chip, self.slots(chip, 1))
                dst = self.slots(self.from_b + p.levels * kind + level, 1)
                self.send(None, chip, 3, dst, self.arrival(1 + kind, batch), p.across_b)

    def over_a(self, batch):
        p = self.place
        levels = self.batches[batch]
        first = self.from_b + p.levels
        self.wait(self.slots(first + levels[0], len(levels)), self.arrival(2, batch))
        for level in levels:
            chip = p.at(p.a_near, level)
            self.add(chip, self.slots(chip, 1))
            self.add(chip, self.slots(first + level, 1))
            self.send(None, chip, 2, self.slots(self.from_a + level, 1), self.arrival(3, batch), p.across_a)

    def collect(self, batch):
        p = self.place
        levels = self.batches[batch]
        self.wait(self.slots(self.from_b + levels[0], len(levels)), self.arrival(1, batch))
        self.wait(self.slots(self.from_a + levels[0], len(levels)), self.arrival(3, batch))
        for level in levels:
            chip = p.at(p.d, level)
            for first in (0, self.from_b, self.from_a):
                self.add(chip, self.slots(first + level if first else chip, 1))

    def line(self, batch):
        p = self.place
        dst = self.slots(self.from_z + p.z, 1)
        for level in self.batches[batch]:
            chip = p.at(p.d, level)
            self.send(p.z != level, chip, 0, dst, self.arrival(4, batch), (chip, p.c))

    def keep(self):
        p = self.place
        own = self.kept(p.c)

        def total(batch):
            self.wait(self.slots(self.from_z, p.levels - 1), self.arrival(4, batch))
            here = self.view(p.d, p.c)
            others = [self.slots(self.from_z + (p.z + i) % p.levels, 1) for i in range(1, p.levels)]
            for part in range(self.parts):
                sum_now = here[part].astype(jnp.float32)
                for other in others:
                    sum_now = sum_now + other[part].astype(jnp.float32)
                own[part] = sum_now

        for batch, levels in enumerate(self.batches):
            pl.when((p.z >= levels[0]) & (p.z <= levels[-1]))(functools.partial(total, batch))

    def left(self, cond, way, count):
        part = self.slots(0, count)
        sem = self.send_sem.at[way]
        when(cond, lambda: remote(part, part, sem, self.recv_sem.at[0, 0], self.place.sibling).wait_send())

    def finish(self):
        p = self.place
        count = len(self.levels)
        for way, pieces in ((4, 4 * count), (3, 2 * count), (2, count)):
            self.left(None, way, pieces)
        for z in range(p.levels):
            self.left(p.z == z, 0, count - (z in self.levels))


class Chain(Reduce):
    def __init__(self, extra, line_sem, *rest):
        super().__init__(*rest)
        self.extra, self.line_sem = extra, line_sem

    def pass_on(self, here, level, way, waits, dst, device):
        p = self.place
        chip = p.at(p.d, level)
        slot = self.slots(self.from_z + level, 1)

        def act():
            if waits:
                self.wait(slot, self.line_sem.at[way, level])
                self.add(chip, slot)
            self.send(None, chip, way, dst, self.line_sem.at[way, level], device)

        pl.when(here)(act)

    def line(self, distance, batch):
        p = self.place
        for level in self.batches[batch]:
            slot = self.slots(self.from_z + level, 1)
            if level >= distance:
                self.pass_on(p.z == level - distance, level, 0, level > distance, slot, p.up)
            if level + distance < p.levels:
                dst = slot if distance > 1 else self.extra
                self.pass_on(p.z == level + distance, level, 1, level + distance < p.levels - 1, dst, p.down)

    def keep(self):
        p = self.place
        own = self.kept(p.c)

        def at(level):
            here = self.view(p.d, p.c)
            for part in range(self.parts):
                own[part] = here[part].astype(jnp.float32)
            sources = [(0, self.slots(self.from_z + level, 1))] if level > 0 else []
            sources += [(1, self.extra)] if level < p.levels - 1 else []
            for way, src in sources:
                self.wait(src, self.line_sem.at[way, level])
                for part in range(self.parts):
                    own[part] = own[part] + src[part].astype(jnp.float32)

        for level in self.levels:
            pl.when(p.z == level)(functools.partial(at, level))

    def finish(self):
        p = self.place
        count = len(self.levels)
        for way, pieces in ((4, 4 * count), (3, 2 * count), (2, count)):
            self.left(None, way, pieces)
        for z in range(p.levels):
            for way, pieces in enumerate((sum(n > z for n in self.levels), sum(n < z for n in self.levels))):
                if pieces:
                    self.left(p.z == z, way, pieces)


def handed(place, own_ref, core, send_sem, recv_sem):
    own = own_ref.at[core]
    return remote(own, own, send_sem, recv_sem, place.sibling)


class Terms:
    def __init__(self, place, sends, ref, got_ref, all_ref, send_sem, recv_sem):
        self.place, self.sends, self.ref, self.got_ref, self.all_ref = place, sends, ref, got_ref, all_ref
        self.send_sem, self.recv_sem = send_sem, recv_sem

    def copy(self, way, core, device):
        return remote(self.ref.at[core], self.got_ref.at[way], self.send_sem.at[way], self.recv_sem.at[way], device)

    def add(self, cond, way):
        if self.sends.closing:
            return

        def act():
            self.copy(way, 0, self.place.sibling).wait_recv()
            self.ref[self.place.c] = self.ref[self.place.c] + self.got_ref[way]

        when(cond, act)

    def share(self):
        self.sends.start(None, lambda: self.copy(0, 1 - self.place.c, self.place.sibling))

    def over_b(self):
        p = self.place
        self.add(None, 0)
        self.sends.start(p.b_at == 0, lambda: self.copy(1, p.c, p.across_b))

    def over_a(self):
        p = self.place
        self.add(p.b_at == 1, 1)
        self.sends.start((p.b_at == 1) & (p.a_at == 0), lambda: self.copy(2, p.c, p.across_a))

    def line(self):
        p = self.place
        home = (p.b_at == 1) & (p.a_at == 1)
        self.add(home, 2)
        here, top = self.ref.at[p.c], p.at(p.d, p.levels - 1)
        self.sends.start(
            home & p.has_up,
            lambda: remote(here, self.got_ref.at[3 + p.z], self.send_sem.at[3], self.recv_sem.at[3], (top, p.c)),
        )

    def keep(self):
        p = self.place
        got = self.got_ref.at[pl.ds(3, p.levels - 1)]
        remote(got, got, self.send_sem.at[3], self.recv_sem.at[3], p.sibling).wait_recv()
        for level in range(p.levels - 1):
            self.ref[p.c] = self.ref[p.c] + self.got_ref[3 + level]

    def final(self):
        return remote(
            self.ref.at[self.place.c],
            self.all_ref.at[self.place.c],
            self.send_sem.at[4],
            self.recv_sem.at[4],
            self.place.sibling,
        )

    def hand_over(self):
        p = self.place
        last = p.d == 4 * p.levels - 1
        if not self.sends.closing:
            pl.when(last)(self.keep)
        self.sends.start(last, self.final)

    def take_over(self):
        self.final().wait_recv()
        self.all_ref[self.place.c] = self.ref[self.place.c]


class Trail:
    def __init__(self, place, sends, flat, own_ref, line_ref, out_ref, send_sem, recv_sem):
        self.place, self.sends, self.flat = place, sends, flat
        self.own_ref, self.line_ref, self.out_ref = own_ref, line_ref, out_ref
        self.send_sem, self.recv_sem = send_sem, recv_sem

    def copy(self):
        f, p = self.flat, self.place
        return remote(
            self.line_ref.at[pl.ds(0, f.halo), :],
            self.line_ref.at[pl.ds(f.lines, f.halo), :],
            self.send_sem,
            self.recv_sem,
            (p.d - 1, p.c),
        )

    def lines(self):
        p, f = self.place, self.flat
        half = f.deep // 2

        def put(split):
            for core in range(2):
                for part in range(f.parts):
                    for block in range(D // 128):
                        first, stride = f.place_of(part, block, split)
                        first = first + stride * half * core
                        self.line_ref[pl.ds(first, half, stride=stride), :] = self.own_ref[
                            core, part, :, pl.ds(128 * block, 128)
                        ]

        def put_turned():
            for j in range(f.rows // 128):
                blocks = []
                for i in range(D // f.deep):
                    lanes = pl.ds(128 * (3 * (i % 2) + j), 128)
                    blocks += [self.own_ref[core, i // 2, :, lanes] for core in range(2)]
                turned = jnp.concatenate(blocks, 0).T
                for block in range(D // 128):
                    first = 6 * 128 * j + block
                    self.line_ref[pl.ds(first, 128, stride=6), :] = turned[:, 128 * block : 128 * (block + 1)]

        pl.when(p.d < f.split)(lambda: put(True))
        pl.when(p.d >= f.split)(put_turned if f.turned else lambda: put(False))

    def pass_back(self):
        self.sends.start(self.place.d > 0, self.copy)

    def last_rows(self, terms_ref, at, count):
        f = self.flat
        for core in range(2):
            for block in range(3):
                self.line_ref[pl.ds(f.lines + 3 * core + block, count, stride=6), :] = terms_ref[
                    core, pl.ds(at, count), pl.ds(128 * block, 128)
                ]

    def out(self):
        p, f = self.place, self.flat
        pl.when(p.d < f.chips - 1)(lambda: self.copy().wait_recv())
        self.out_ref[pl.ds(0, f.held), :] = shifted(self.line_ref, f.slip * p.d, f.held)


def dot(a, b):
    return jnp.dot(a, b, preferred_element_type=jnp.float32)


def dot_nt(a, b):
    return lax.dot_general(a, b, (((1,), (1,)), ((), ())), preferred_element_type=jnp.float32)


def square(values):
    return values.reshape(D, D)


def tile(index, size):
    return pl.ds(pl.multiple_of(index * size, size), size)


def loop(count, step, beside=()):
    def body(i, _):
        step(i)
        for at, act in beside:
            pl.when(i == at)(act)
        return 0

    lax.fori_loop(0, count, body, 0)


TILE, WIDE = 256, 512


class Layer:
    def __init__(self, refs, att_split, ffn_split, seqs, length):
        self.__dict__.update(refs)
        self.att_split, self.ffn_split = att_split, ffn_split
        self.seqs, self.length = seqs, length
        self.tiles = seqs * length // TILE

    def whole(self, blocks, part):
        count = blocks.shape[0] // 4
        return blocks[pl.ds(count * part, count)].reshape(self.seqs * self.length, D)

    def some(self, blocks, part, r, size=TILE):
        count = size // blocks.shape[1]
        return pl.ds(blocks.shape[0] // 4 * part + count * r, count)

    def qkv_weight(self, part):
        return square(self.att_w[pl.ds(0, self.att_split), part])

    def out_weight(self):
        return square(self.att_w[pl.ds(self.att_split, self.att_w.shape[0] - self.att_split)])

    def in_weight(self, part):
        return square(self.ffn_w[pl.ds(0, self.ffn_split), part])

    def down_weight(self, part):
        return square(self.ffn_w[pl.ds(self.ffn_split + 2 * part, 2)])

    def term(self, row):
        return self.terms[pl.ds(row, 1), :]

    def add_term(self, row, values):
        self.term_grads[pl.ds(row, 1), :] += jnp.sum(values, 0, keepdims=True)


    def qkv(self, beside=()):
        def step(r):
            rows = tile(r, TILE)
            x = self.tok[rows, :]
            queries = (dot(x, self.qkv_weight(0)) + self.term(0)).astype(jnp.bfloat16)
            self.heads[0, rows, :] = queries * HEAD_DIM ** (-0.5)
            self.heads[1, rows, :] = dot(x, self.qkv_weight(1)).astype(jnp.bfloat16)
            self.heads[2, rows, :] = (dot(x, self.qkv_weight(2)) + self.term(1)).astype(jnp.bfloat16)

        loop(self.tiles, step, beside)

    def make_bias(self):
        segs = self.segs[...].astype(jnp.float32)
        columns = jnp.concatenate([segs, jnp.zeros((8 - self.seqs, self.length), jnp.float32)], 0).T
        for seq in range(self.seqs):
            same = columns[:, seq : seq + 1] == segs[seq : seq + 1, :]
            self.bias[pl.ds(seq * self.length, self.length), :] = jnp.where(same, 0.0, masked)

    def lane_half(self, half):
        lane = lax.broadcasted_iota(jnp.int32, (self.length, 2 * HEAD_DIM), 1)
        return (lane // HEAD_DIM) == half

    def attend(self, beside=()):
        self.make_bias()

        def step(i):
            seq, pair = i // (HEADS // 2), i % (HEADS // 2)
            lanes = tile(pair, 2 * HEAD_DIM)
            rows = tile(seq, self.length)
            queries, keys, values = (self.heads[j, rows, lanes] for j in range(3))
            values_t = values.T
            parts = []
            for half in range(2):
                own = jnp.where(self.lane_half(half), queries, jnp.zeros_like(queries))
                scores = dot_nt(keys, own) + self.bias[rows, :]
                top = jnp.max(scores, 0, keepdims=True)
                raised = jnp.exp(scores - top)
                total = jnp.sum(raised, 0, keepdims=True)
                probs = (raised * (1.0 / total)).astype(jnp.bfloat16)
                self.totals[pl.ds(HEADS * seq + 2 * pair + half, 1), :] = top + jnp.log(total)
                parts.append(dot(values_t[HEAD_DIM * half : HEAD_DIM * (half + 1)], probs))
            both_t = jnp.concatenate(parts, 0).astype(jnp.bfloat16)
            self.ctx_t[lanes, rows] = both_t
            self.ctx[rows, lanes] = both_t.T

        loop(self.seqs * HEADS // 2, step, beside)

    def first_norm(self, beside=()):
        def step(r):
            rows = tile(r, TILE)
            residual = self.tok[rows, :].astype(jnp.float32) + dot(self.ctx[rows, :], self.out_weight()) + self.term(2)
            first, normed, rstd = normalize(residual, self.term(3), self.term(4))
            self.hat[rows, :] = normed
            self.rstd[rows, :] = rstd
            self.low_t[:, rows] = first.astype(jnp.bfloat16).T

        loop(self.tiles, step, beside)

    def feed(self, beside=()):
        def step(r):
            rows = tile(r, TILE)
            first = self.hat[rows, :] * self.term(3) + self.term(4)
            low = first.astype(jnp.bfloat16)
            second = first + self.term(12)
            for part in range(4):
                inner = dot(low, self.in_weight(part)) + self.term(8 + part)
                cdf, slope = gelu_parts(inner)
                act = (inner * cdf).astype(jnp.bfloat16)
                self.act[self.some(self.act, part, r)] = act.reshape(-1, self.act.shape[1], D)
                slope = slope.astype(jnp.bfloat16).reshape(-1, self.slope.shape[1], D)
                self.slope[self.some(self.slope, part, r)] = slope
                second = second + dot(act, self.down_weight(part))
            out, normed, rstd = normalize(second, self.term(13), self.term(14))
            seq = r // (self.length // TILE)
            live = jnp.clip(self.live_count[0] - seq, 0, 1).astype(jnp.float32)
            grad_out = self.cot[rows, :].astype(jnp.float32) * live
            self.out[rows, :] = out.astype(jnp.bfloat16)
            scaled = grad_out * self.term(13)
            grad = rstd * (
                scaled
                - jnp.mean(scaled, -1, keepdims=True)
                - normed * jnp.mean(scaled * normed, -1, keepdims=True)
            )
            self.add_term(13, grad_out * normed)
            self.add_term(14, grad_out)
            grad_down = grad.astype(jnp.bfloat16)
            self.add_term(12, grad_down.astype(jnp.float32))
            self.grad[rows, :] = grad
            self.down[rows, :] = grad_down
            self.down_t[:, rows] = grad_down.T

        loop(self.tiles, step, beside)


    def hidden_back(self, part, beside=()):
        def step(r):
            rows = tile(r, WIDE)
            grad_act = dot_nt(self.down[rows, :], self.down_weight(part))
            at = self.some(self.slope, part, r, WIDE)
            slope = self.slope[at].reshape(WIDE, D).astype(jnp.float32)
            inner = (grad_act * slope).astype(jnp.bfloat16)
            self.slope[at] = inner.reshape(-1, self.slope.shape[1], D)
            self.add_term(8 + part, inner.astype(jnp.float32))

        loop(self.seqs * self.length // WIDE, step, beside)

    def down_grads(self, part, beside=()):
        deep = self.ffn_w.shape[2]
        first = self.ffn_split + 2 * part
        count = self.act.shape[0] // 4

        def step(n):
            acts = self.act[pl.ds(count * part, count), :, tile(n, 256)].reshape(self.seqs * self.length, 256)
            grads = dot(self.down_t[...], acts).astype(jnp.bfloat16)
            for k in range(2):
                block = 2 * n + k
                for i in range(D // deep):
                    lanes = tile(3 * (i % 2) + block % 3, 128)
                    self.ffn_w[first + block // 3, i // 2, :, lanes] = grads[
                        deep * i : deep * (i + 1), 128 * k : 128 * (k + 1)
                    ]

        loop(3, step, beside)

    def in_back(self, part, beside=()):
        def step(r):
            rows = tile(r, WIDE)
            self.grad[rows, :] += dot_nt(
                self.slope[self.some(self.slope, part, r, WIDE)].reshape(WIDE, D), self.in_weight(part)
            )

        loop(self.seqs * self.length // WIDE, step, beside)

    def in_grads(self, part, beside=()):
        deep = self.ffn_w.shape[2]
        count = self.slope.shape[0] // 4

        def step(n):
            lanes = tile(n, 256)
            inner = self.slope[pl.ds(count * part, count), :, lanes].reshape(self.seqs * self.length, 256)
            grads = dot(self.low_t[...], inner).astype(jnp.bfloat16)
            self.ffn_w[pl.ds(0, self.ffn_split), part, :, lanes] = grads.reshape(self.ffn_split, deep, 256)

        loop(3, step, beside)

    def first_back(self, beside=()):
        def step(r):
            rows = tile(r, TILE)
            grad_first, normed = self.grad[rows, :], self.hat[rows, :]
            scaled = grad_first * self.term(3)
            grad = self.rstd[rows, :] * (
                scaled
                - jnp.mean(scaled, -1, keepdims=True)
                - normed * jnp.mean(scaled * normed, -1, keepdims=True)
            )
            self.add_term(3, grad_first * normed)
            self.add_term(4, grad_first)
            proj = grad.astype(jnp.bfloat16)
            self.add_term(2, proj.astype(jnp.float32))
            self.grad[rows, :] = grad
            shape = (-1, self.act.shape[1], D)
            self.act[self.some(self.act, 3, r)] = proj.reshape(shape)
            grad_context = dot_nt(proj, self.out_weight()).astype(jnp.bfloat16)
            self.act[self.some(self.act, 0, r)] = grad_context.reshape(shape)
            self.tok_t[:, rows] = self.tok[rows, :].T

        loop(self.tiles, step, beside)

    def out_grads(self, beside=()):
        count = self.act.shape[0] // 4

        def step(n):
            lanes = tile(n, 256)
            proj = self.act[pl.ds(3 * count, count), :, lanes].reshape(self.seqs * self.length, 256)
            grads = dot(self.ctx_t[...], proj).astype(jnp.bfloat16)
            owners = self.att_w.shape[0] - self.att_split
            shape = (owners, *self.att_w.shape[1:3], 256)
            self.att_w[pl.ds(self.att_split, owners), :, :, lanes] = grads.reshape(shape)

        loop(3, step, beside)

    def attend_back(self, group, beside=()):
        def step(i):
            seq, pair = i % self.seqs, 2 * group + i // self.seqs
            lanes = tile(pair, 2 * HEAD_DIM)
            rows = tile(seq, self.length)
            count = self.length // self.act.shape[1]
            queries, keys, values = (self.heads[j, rows, lanes] for j in range(3))
            grads = self.act[pl.ds(count * seq, count), :, lanes].reshape(self.length, 2 * HEAD_DIM)
            keys_t = keys.T
            parts = []
            grad_keys = grad_values = 0.0
            for half in range(2):
                here = self.lane_half(half)
                own = jnp.where(here, queries, jnp.zeros_like(queries))
                own_grads = jnp.where(here, grads, jnp.zeros_like(grads))
                total = self.totals[pl.ds(HEADS * seq + 2 * pair + half, 1), :]
                probs = jnp.exp(dot_nt(keys, own) + self.bias[rows, :] - total)
                grad_values = grad_values + dot(probs.astype(jnp.bfloat16), own_grads)
                grad_probs = dot_nt(values, own_grads)
                row_sum = jnp.sum(probs * grad_probs, 0, keepdims=True)
                grad_scores = (probs * (grad_probs - row_sum)).astype(jnp.bfloat16)
                grad_keys = grad_keys + dot(grad_scores, own)
                parts.append(dot(keys_t[HEAD_DIM * half : HEAD_DIM * (half + 1)], grad_scores))
            grad_queries = (jnp.concatenate(parts, 0) * HEAD_DIM ** (-0.5)).astype(jnp.bfloat16).T
            grad_values = grad_values.astype(jnp.bfloat16)
            self.heads[0, rows, lanes] = grad_queries
            self.heads[1, rows, lanes] = grad_keys.astype(jnp.bfloat16)
            self.heads[2, rows, lanes] = grad_values
            for row, grad in ((0, grad_queries), (1, grad_values)):
                self.term_grads[pl.ds(row, 1), lanes] += jnp.sum(grad.astype(jnp.float32), 0, keepdims=True)

        loop(2 * self.seqs, step, beside)

    def qkv_grads(self, group):
        lanes = pl.ds(4 * HEAD_DIM * group, 4 * HEAD_DIM)
        deep = self.att_w.shape[2]

        def step(part):
            grads = dot(self.tok_t[...], self.heads[part, :, lanes]).astype(jnp.bfloat16)
            for chip in range(self.att_split):
                self.act[self.act_first + 3 * chip + part, :, lanes] = grads[deep * chip : deep * (chip + 1)]

        loop(3, step)

    def input_back(self, beside=()):
        def step(r):
            rows = tile(r, TILE)
            total = self.grad[rows, :]
            for part in range(3):
                total = total + dot_nt(self.heads[part, rows, :], self.qkv_weight(part))
            self.gin[rows, :] = total.astype(jnp.bfloat16)

        loop(self.tiles, step, beside)


def gelu_parts(values):
    cdf = 0.5 * (1.0 + lax.erf(values * 0.5**0.5))
    return cdf, cdf + values * jnp.exp(-0.5 * values * values) * (2.0 * math.pi) ** (-0.5)


def batches(levels):
    half = levels // 2
    return [(level,) for level in range(half, levels)], [tuple(range(half))], [(levels - 1,)], [tuple(range(levels - 1))]


def scratch_shapes(levels, att, ffn, rows, seqs, length):
    bf16, f32 = jnp.bfloat16, jnp.float32
    vmem, dma = pltpu.VMEM, pltpu.SemaphoreType.DMA
    chips = att.chips
    turned = vmem((D, rows), bf16)
    f_batches, i_batches, o_batches, q_batches = batches(levels)
    shapes = dict(
        att_w=vmem((chips, att.parts, att.deep, D), bf16),
        ffn_w=vmem((chips, ffn.parts, ffn.deep, D), bf16),
        tok=vmem((rows, D), bf16),
        heads=vmem((3, rows, D), bf16),
        totals=vmem((seqs * HEADS, length), f32),
        ctx=vmem((rows, D), bf16),
        ctx_t=turned,
        hat=vmem((rows, D), f32),
        rstd=vmem((rows, 1), f32),
        low_t=turned,
        act=vmem((4 * rows // att.deep, att.deep, D), bf16),
        slope=vmem((8 * rows // att.deep, att.deep // 2, D), bf16),
        grad=vmem((rows, D), f32),
        down_t=turned,
        terms=vmem((16, D), f32),
        term_grads=vmem((16, D), f32),
        spare=vmem((48, 128), f32),
        terms_sum=vmem((2, 16, D // 2), f32),
        terms_got=vmem((2 + levels, 16, D // 2), f32),
        terms_all=vmem((2, 16, D // 2), f32),
        ffn_slots=vmem((chips + 4 * levels, ffn.parts, ffn.deep // 2, D), bf16),
        local_sem=dma((8,)),
        term_send=dma((3,)),
        term_recv=dma,
        sum_send=dma((5,)),
        sum_recv=dma((5,)),
        free=pltpu.SemaphoreType.REGULAR,
        ffn_extra=vmem((ffn.parts, ffn.deep // 2, D), bf16),
        f_send=dma((5,)),
        f_line=dma((2, levels)),
        i_send=dma((2, 5)),
        i_recv=dma((2, len(i_batches), 5)),
        i_line=dma((2, 2, levels)),
        f_recv=dma((len(f_batches), 5)),
        o_send=dma((5,)),
        o_recv=dma((len(o_batches), 5)),
        q_send=dma((3, 5)),
        q_recv=dma((3, len(q_batches), 5)),
    )
    for name, flat in (("att_", att), ("ffn_", ffn)):
        half = (flat.parts, flat.deep // 2, D)
        own = dict(
            long=vmem((flat.halo + flat.held + 8, 128), f32),
            halo=vmem((flat.tail + flat.halo + 8, 128), f32),
            line=vmem((flat.lines + flat.halo + 8, 128), f32),
            own=vmem((2, *half), f32),
            send=dma((5,)),
            recv=dma((chips,)),
            sib=dma,
            plane_send=dma((5,)),
            plane_recv=dma((levels + 2,)),
            plane_sib=dma,
            halo_send=dma,
            halo_recv=dma,
            own_send=dma,
            own_recv=dma,
            back_send=dma,
            back_recv=dma,
        )
        shapes.update({name + key: shape for key, shape in own.items()})
    return shapes


def layer_kernel(names, levels, att, ffn, seqs, length, masters_in, tok_in, cot_in, segs, live_count,
                 out_out, gin_out, att_out, ffn_out, *scratch):
    s = types.SimpleNamespace(**dict(zip(names, scratch)))
    act_first = s.act.shape[0] // 4
    refs = dict(vars(s), segs=segs, live_count=live_count)
    refs.update(cot=s.tok, out=s.tok, down=s.ctx, tok_t=s.low_t)
    refs.update(bias=s.hat.at[:, pl.ds(0, length)], gin=s.tok, act_first=act_first)
    work = Layer(refs, att.split, ffn.split, seqs, length)

    def local(src, dst, at):
        copy = pltpu.make_async_copy(src, dst, s.local_sem.at[at])
        copy.start()
        return copy

    p = Place(levels)
    get_a = local(masters_in.at[pl.ds(0, att.held), :], s.att_long.at[pl.ds(att.halo, att.held), :], 0)
    get_f = local(masters_in.at[pl.ds(att.held, ffn.held), :], s.ffn_long.at[pl.ds(ffn.halo, ffn.held), :], 1)
    get_t = local(tok_in, s.tok, 2)
    p.meet()
    sends = Sends()
    lead_a = Lead(p, sends, att, s.att_long, s.att_halo, s.att_line, s.att_halo_send, s.att_halo_recv)
    lead_f = Lead(p, sends, ffn, s.ffn_long, s.ffn_halo, s.ffn_line, s.ffn_halo_send, s.ffn_halo_recv)
    get_a.wait()
    sends.go(lead_a.begin)
    get_f.wait()
    sends.go(lead_f.begin)
    lead_a.lines()
    lead_a.store(s.att_w)
    def gathers(ref, cut, *sems):
        parts, lanes = ref.shape[1], pl.ds(0, D)
        if cut[0]:
            first, last = (pl.ds(0, parts - cut[0]), lanes), (pl.ds(parts - cut[0], cut[0]), lanes)
        else:
            first = (pl.ds(0, parts), pl.ds(0, D - cut[1]))
            last = (pl.ds(0, parts), pl.ds(D - cut[1], cut[1]))
        go, plane = Gather(p, ref, *first, *sems[:3]), Plane(p, ref, *last, *sems[3:])
        return go, plane

    go_a = gathers(
        s.att_w, (0, 128), s.att_send, s.att_recv, s.att_sib, s.att_plane_send, s.att_plane_recv, s.att_plane_sib
    )
    go_f = gathers(
        s.ffn_w, (1, 0), s.ffn_send, s.ffn_recv, s.ffn_sib, s.ffn_plane_send, s.ffn_plane_recv, s.ffn_plane_sib
    )
    (a, a_plane), (f, f_plane) = go_a, go_f
    a.own()
    a_plane.own()

    def last():
        terms, spare = s.terms, s.spare
        terms[...] = jnp.zeros(terms.shape, terms.dtype)
        for lead, at, count in ((lead_a, 0, 5), (lead_f, 8, 7)):
            rows = lead.last_rows(count)
            spare[pl.ds(0, rows.shape[0]), :] = rows
            for block in range(D // 128):
                terms[pl.ds(at, count), pl.ds(128 * block, 128)] = spare[pl.ds(block, count, stride=6), :]

    pl.when(p.d == att.chips - 1)(last)
    lead_f.lines()
    lead_f.store(s.ffn_w)
    s.term_grads[...] = jnp.zeros(s.term_grads.shape, jnp.float32)
    a.line(1)
    a.over_a(0)
    a_plane.near()
    a.line(2)
    a.over_b(0)
    a_plane.complete()
    a.over_a(1)
    a.line(3)
    f_plane.own()
    a.over_a(2)
    f.own()
    a_plane.line(1)
    a.over_b(1)
    a.over_b(2)
    a.over_a(3)
    f_plane.near()
    a_plane.line(2)
    f.line(1)
    a.over_b(3)
    a_plane.line(3)
    sends.go(Spread(p, sends, s.terms, s.term_send, s.term_recv).run)
    for go in go_a:
        go.from_sibling()
    get_t.wait()

    on = functools.partial
    work.qkv(((2, on(f.over_a, 0)), (2, on(f.line, 2)), (2, f_plane.complete),))
    work.attend(
        (
            (3, on(f.over_a, 1)),
            (3, on(f.line, 3)),
            (6, on(f_plane.line, 1)),
            (8, on(f.over_a, 2)),
            (9, on(f.over_b, 0)),
            (10, on(f_plane.line, 2)),
            (10, on(f.over_b, 1)),
            (10, on(f.over_a, 3)),
        )
    )
    work.first_norm()
    f.over_b(2)
    f_plane.line(3)
    f.over_b(3)

    get_c = local(cot_in, s.tok, 2)
    for go in go_f:
        go.from_sibling()
    get_c.wait()
    work.feed()
    put_o = local(s.tok, out_out, 3)
    sends.finish()
    for go in (*go_a, *go_f):
        go.finish()

    sums = Sends()
    slots, slope, act = s.ffn_slots, s.slope, s.act
    half_a, half_f = att.deep // 2, ffn.deep // 2

    def of(ref, half):
        return lambda chip, core: ref.at[chip, :, tile(core, half), :]

    def att_slots(lanes):
        return lambda i, count: slope.at[pl.ds(3 * i, 3 * count), :, lanes]

    f_batches, i_batches, o_batches, q_batches = batches(levels)
    everything = pl.ds(0, D)
    ffn_slots = lambda i, count: slots.at[i] if count == 1 else slots.at[pl.ds(i, count)]
    add_f = Chain(
        s.ffn_extra, s.f_line, p, 4, ffn.chips, f_batches, of(s.ffn_w, half_f), ffn_slots,
        lambda core: s.ffn_own.at[core], s.f_send, s.f_recv,
    )
    add_i = []
    for group in range(2):
        parts = pl.ds(2 * group, 2)
        own_chips = pl.ds(0, ffn.split)
        whole = (s.ffn_w.at[own_chips, parts, tile(1 - p.c, half_f), :], slots.at[own_chips, parts])
        add_i.append(
            Chain(
                s.ffn_extra.at[parts], s.i_line.at[group], p, 2, ffn.chips, i_batches,
                lambda chip, core, parts=parts: s.ffn_w.at[chip, parts, tile(core, half_f), :],
                lambda i, count, parts=parts: slots.at[i, parts] if count == 1 else slots.at[pl.ds(i, count), parts],
                lambda core, parts=parts: s.ffn_own.at[core, parts], s.i_send.at[group], s.i_recv.at[group], whole,
            )
        )
    add_o = Reduce(
        p, 3, att.chips, o_batches, of(s.att_w, half_a), att_slots(everything),
        lambda core: s.att_own.at[core], s.o_send, s.o_recv,
    )
    add_q = []
    for group in range(3):
        lanes = pl.ds(256 * group, 256)
        blocks = pl.ds(act_first, 3 * att.split)
        view = lambda chip, core, lanes=lanes: act.at[pl.ds(act_first + 3 * chip, 3), tile(core, half_a), lanes]
        whole = (act.at[blocks, tile(1 - p.c, half_a), lanes], slope.at[pl.ds(0, 3 * att.split), :, lanes])
        add_q.append(
            Reduce(
                p, 3, att.chips, q_batches, view, att_slots(lanes),
                lambda core, lanes=lanes: s.att_own.at[core, :, :, lanes], s.q_send.at[group], s.q_recv.at[group], whole,
            )
        )
    add_t = Terms(p, sums, s.terms_sum, s.terms_got, s.terms_all, s.sum_send, s.sum_recv)

    def do(act, *at):
        return sums.later(functools.partial(act, *at))

    work.hidden_back(0)
    work.down_grads(0)
    work.hidden_back(1)
    work.down_grads(1)
    add_f.share(0)
    put_o.wait()
    get_t = local(tok_in, s.tok, 2)
    work.hidden_back(2)
    work.down_grads(2, ((0, on(add_f.over_b, 0)),))
    work.hidden_back(3)
    work.down_grads(3)
    add_f.share(1)
    work.in_back(0, ((1, on(add_f.over_b, 1)),))
    work.in_grads(0)
    work.in_back(1)
    work.in_grads(1, ((0, on(add_f.over_a, 0)),))
    add_i[0].share(0)
    work.in_back(2, ((1, on(add_i[0].over_b, 0)),))
    work.in_grads(2)
    work.in_back(3)
    work.in_grads(3, ((0, on(add_f.collect, 0)), (0, on(add_f.line, 2, 0)), (2, on(add_f.over_a, 1))))
    add_i[1].share(0)

    line = [(p.turn(distance), p.c) for distance in range(1, levels)]
    for device in (p.sibling, p.across_a, p.across_b, *line):
        pl.semaphore_signal(s.free, inc=1, device_id=device, device_id_type=MESH_ID)
    get_t.wait()
    work.first_back(((1, on(add_i[1].over_b, 0)),))
    work.out_grads()
    pl.semaphore_wait(s.free, 2 + levels)
    add_o.share(0)
    work.make_bias()
    work.attend_back(
        0,
        (
            (0, on(add_f.collect, 1)),
            (0, on(add_f.line, 3, 1)),
            (1, on(add_f.line, 1, 0)),
            (1, on(add_i[0].over_a, 0)),
            (3, on(add_o.over_b, 0)),
        ),
    )
    work.qkv_grads(0)
    q = add_q
    q[0].share(0)
    work.attend_back(
        1,
        (
            (0, on(q[0].over_b, 0)),
            (0, on(add_f.line, 2, 1)),
            (0, on(add_i[0].collect, 0)),
            (0, on(add_i[0].line, 3, 0)),
            (2, on(add_i[1].over_a, 0)),
            (3, on(add_i[0].line, 2, 0)),
            (3, on(q[0].over_a, 0)),
            (3, on(add_o.over_a, 0)),
        ),
    )
    work.qkv_grads(1)
    q[1].share(0)
    work.attend_back(
        2,
        (
            (0, on(add_f.line, 1, 1)),
            (0, on(q[1].over_b, 0)),
            (0, on(add_i[1].collect, 0)),
            (0, on(add_i[1].line, 3, 0)),
            (1, on(q[0].collect, 0)),
            (1, on(q[0].line, 0)),
            (1, on(add_o.collect, 0)),
            (1, on(add_o.line, 0)),
            (1, on(add_i[0].line, 1, 0)),
            (3, on(add_i[1].line, 2, 0)),
            (3, on(q[1].over_a, 0)),
        ),
    )
    work.qkv_grads(2)
    q[2].share(0)
    for core in range(2):
        s.terms_sum[core] = s.term_grads[:, pl.ds(D // 2 * core, D // 2)]
    do(add_t.share)()
    trail_f = Trail(p, sums, ffn, s.ffn_own, s.ffn_line, s.ffn_long, s.ffn_back_send, s.ffn_back_recv)
    trail_a = Trail(p, sums, att, s.att_own, s.att_line, s.att_long, s.att_back_send, s.att_back_recv)
    given_f = lambda core: handed(p, s.ffn_own, core, s.ffn_own_send, s.ffn_own_recv)
    given_a = lambda core: handed(p, s.att_own, core, s.att_own_send, s.att_own_recv)
    work.input_back(
        (
            (0, on(q[2].over_b, 0)),
            (0, on(add_i[1].line, 1, 0)),
            (0, do(add_t.over_b)),
            (1, on(q[1].collect, 0)),
            (1, on(q[1].line, 0)),
            (2, do(add_t.over_a)),
            (3, on(q[2].over_a, 0)),
            (3, do(add_t.line)),
        )
    )
    put_g = local(work.gin, gin_out, 4)
    for who in (add_f, *add_i):
        who.keep()
    sums.go(lambda: sums.start(None, lambda: given_f(p.c)))
    add_o.keep()
    q[0].keep()
    q[2].collect(0)
    q[2].line(0)
    given_f(1 - p.c).wait_recv()
    trail_f.lines()
    sums.go(trail_f.pass_back)
    q[1].keep()
    do(add_t.hand_over)()
    final = p.d == att.chips - 1

    def terms_here():
        add_t.take_over()
        trail_f.last_rows(s.terms_all, 8, 7)
        trail_a.last_rows(s.terms_all, 0, 5)

    pl.when(final)(terms_here)
    trail_f.out()
    put_f = local(s.ffn_long.at[pl.ds(0, ffn.held), :], ffn_out, 1)
    q[2].keep()
    sums.go(lambda: sums.start(None, lambda: given_a(p.c)))
    given_a(1 - p.c).wait_recv()
    trail_a.lines()
    sums.go(trail_a.pass_back)
    trail_a.out()
    put_a = local(s.att_long.at[pl.ds(0, att.held), :], att_out, 0)
    sums.finish()
    for who in (add_f, *add_i, add_o, *q):
        who.finish()
    for copy in (put_g, put_f, put_a):
        copy.wait()


def run_layer(levels, att, ffn, masters, tokens, cotangent, segments, live_count):
    vmem = pl.BlockSpec(memory_space=pltpu.VMEM)
    anywhere = pl.BlockSpec(memory_space=pl.ANY)
    seqs, length = segments.shape
    rows = tokens.shape[0]
    bf16, f32 = jnp.bfloat16, jnp.float32
    shape = jax.ShapeDtypeStruct
    scratch = scratch_shapes(levels, att, ffn, rows, seqs, length)
    return pl.pallas_call(
        functools.partial(layer_kernel, tuple(scratch), levels, att, ffn, seqs, length),
        out_shape=(
            shape(tokens.shape, bf16),
            shape(tokens.shape, bf16),
            shape((att.held, 128), f32),
            shape((ffn.held, 128), f32),
        ),
        in_specs=[anywhere, anywhere, anywhere, vmem, pl.BlockSpec(memory_space=pltpu.SMEM)],
        out_specs=(anywhere, anywhere, anywhere, anywhere),
        scratch_shapes=list(scratch.values()),
        compiler_params=pltpu.CompilerParams(
            collective_id=1, has_side_effects=True, vmem_limit_bytes=64 * 2**20
        ),
        name="layer",
    )(masters, tokens, cotangent, segments, live_count)


def as_lines(flat, vector):
    return jnp.pad(vector, (0, flat.held * 128 - flat.length)).reshape(flat.held, 128)


def fast_body(
    levels,
    tokens,
    cotangent,
    segments,
    live_count,
    att_master,
    att_first,
    att_second,
    ffn_master,
    ffn_first,
    ffn_second,
):
    chips = lax.axis_size("dp")
    att = Flat(att_master.shape[0], chips, 3, 3 * chips // 4, False)
    ffn = Flat(ffn_master.shape[0], chips, 4, chips // 2, True)
    output, input_grad, att_sum, ffn_sum = run_layer(
        levels,
        att,
        ffn,
        jnp.concatenate([as_lines(att, att_master), as_lines(ffn, ffn_master)]),
        tokens,
        cotangent,
        segments,
        live_count,
    )
    att_grad = att_sum.reshape(-1)[: att.length]
    ffn_grad = ffn_sum.reshape(-1)[: ffn.length]
    att_new = adam_update(att_master, att_first, att_second, att_grad)
    ffn_new = adam_update(ffn_master, ffn_first, ffn_second, ffn_grad)
    return (output, input_grad, att_grad, *att_new, ffn_grad, *ffn_new)


def body_for(mesh):
    chips, cores = mesh.shape["dp"], mesh.shape["rep"]
    if chips == 16 and cores == 2:
        return functools.partial(fast_body, chips // 4)
    return general_body


def solution(mesh):
    placed = (
        P(("dp", "rep"), None),
        P(("dp", "rep"), None),
        P(("dp", "rep"), None),
        P(("dp", "rep")),
        P("dp"),
        P("dp"),
        P("dp"),
        P("dp"),
        P("dp"),
        P("dp"),
    )
    return jax.shard_map(
        body_for(mesh),
        mesh=mesh,
        in_specs=placed,
        out_specs=(
            P(("dp", "rep"), None),
            P(("dp", "rep"), None),
            P("dp"),
            P("dp"),
            P("dp"),
            P("dp"),
            P("dp"),
            P("dp"),
            P("dp"),
            P("dp"),
        ),
        check_vma=False,
    )
```

```python
import functools
import math
import types

import jax
import jax.numpy as jnp
from jax import lax
from jax.experimental import pallas as pl
from jax.experimental.pallas import tpu as pltpu
from jax.sharding import PartitionSpec as P

D = 768
HEADS = 12
HEAD_DIM = 64
FF = 3072
STEP = 10


norm_eps = 1e-05
beta_one = 0.9
beta_two = 0.98
decay = 0.01
adam_eps = 1e-08
masked = -1e30


def split_attention(flat_params):
    qkv_weight = flat_params[: 3 * D * D].reshape(D, 3 * D)
    offset = 3 * D * D
    out_weight = flat_params[offset : offset + D * D].reshape(D, D)
    offset = offset + D * D
    att_terms = flat_params[offset : offset + 5 * D].reshape(5, D).astype(jnp.float32)
    return (qkv_weight, out_weight, att_terms)


def split_ffn(flat_params):
    in_weight = flat_params[: D * FF].reshape(D, FF)
    offset = D * FF
    down_weight = flat_params[offset : offset + FF * D].reshape(FF, D)
    offset = offset + FF * D
    in_bias = flat_params[offset : offset + FF].astype(jnp.float32)
    offset = offset + FF
    ffn_terms = flat_params[offset : offset + 3 * D].reshape(3, D).astype(jnp.float32)
    return (in_weight, down_weight, in_bias, ffn_terms)


def normalize(values, gain, shift):
    row_mean = jnp.mean(values, -1, keepdims=True)
    centred = values - row_mean
    rstd_rows = lax.rsqrt(jnp.mean(centred * centred, -1, keepdims=True) + norm_eps)
    normed = centred * rstd_rows
    return (normed * gain + shift, normed, rstd_rows)


def norm_back(grad_in, normed, rstd_rows, gain):
    scaled = grad_in * gain
    grad_rows = rstd_rows * (
        scaled
        - jnp.mean(scaled, -1, keepdims=True)
        - normed * jnp.mean(scaled * normed, -1, keepdims=True)
    )
    return (grad_rows, jnp.sum(grad_in * normed, 0), jnp.sum(grad_in, 0))


def gelu_slope(values):
    normal_cdf = 0.5 * (1.0 + lax.erf(values * 0.5**0.5))
    return normal_cdf + values * jnp.exp(-0.5 * values * values) * (2.0 * math.pi) ** (-0.5)


def masked_scores(query_rows, key_rows, seg_ids):
    scores = jnp.einsum(
        "qhd,khd->hqk", query_rows, key_rows, preferred_element_type=jnp.float32
    ) * HEAD_DIM ** (-0.5)
    same_doc = seg_ids[:, None] == seg_ids[None, :]
    return jnp.where(same_doc[None], scores, masked)


def attend_forward(block):
    query_rows, key_rows, value_rows, seg_ids = block
    scores = masked_scores(query_rows, key_rows, seg_ids)
    row_top = jnp.max(scores, -1, keepdims=True)
    raised = jnp.exp(scores - row_top)
    row_total = jnp.sum(raised, -1, keepdims=True)
    soft_probs = (raised / row_total).astype(jnp.bfloat16)
    context = jnp.einsum("hqk,khd->qhd", soft_probs, value_rows, preferred_element_type=jnp.float32)
    return (
        context.astype(jnp.bfloat16).reshape(context.shape[0], -1),
        row_top + jnp.log(row_total),
    )


def attend_backward(query_rows, key_rows, value_rows, seg_ids, log_total, grad_context):
    soft_probs = jnp.exp(masked_scores(query_rows, key_rows, seg_ids) - log_total)
    grad_probs = jnp.einsum(
        "qhd,khd->hqk", grad_context, value_rows, preferred_element_type=jnp.float32
    )
    grad_values = jnp.einsum(
        "hqk,qhd->khd",
        soft_probs.astype(jnp.bfloat16),
        grad_context,
        preferred_element_type=jnp.float32,
    )
    grad_scores = soft_probs * (grad_probs - jnp.sum(soft_probs * grad_probs, -1, keepdims=True))
    grad_scores = grad_scores.astype(jnp.bfloat16)
    grad_queries = jnp.einsum(
        "hqk,khd->qhd", grad_scores, key_rows, preferred_element_type=jnp.float32
    ) * HEAD_DIM ** (-0.5)
    grad_keys = jnp.einsum(
        "hqk,qhd->khd", grad_scores, query_rows, preferred_element_type=jnp.float32
    ) * HEAD_DIM ** (-0.5)
    length_here = query_rows.shape[0]
    return jnp.concatenate(
        [
            grad_queries.reshape(length_here, -1),
            grad_keys.reshape(length_here, -1),
            grad_values.reshape(length_here, -1),
        ],
        -1,
    )


def adam_update(master, first, second, grad):
    first_new = beta_one * first + (1.0 - beta_one) * grad
    second_new = beta_two * second + (1.0 - beta_two) * grad * grad
    fix_one = 1.0 - beta_one**STEP
    fix_two = 1.0 - beta_two**STEP
    update = first_new / fix_one / (jnp.sqrt(second_new / fix_two) + adam_eps)
    return (first_new, second_new, update + decay * master)


def general_body(
    tokens,
    cotangent,
    segments,
    live_count,
    att_master,
    att_first,
    att_second,
    ffn_master,
    ffn_first,
    ffn_second,
):
    seq_count = segments.shape[0]
    length = segments.shape[1]
    att_full = lax.all_gather(att_master.astype(jnp.bfloat16), "dp", axis=0, tiled=True)
    qkv_weight, out_weight, att_terms = split_attention(att_full)
    bias_qkv = jnp.concatenate([att_terms[0], jnp.zeros_like(att_terms[0]), att_terms[1]])
    qkv = (jnp.dot(tokens, qkv_weight, preferred_element_type=jnp.float32) + bias_qkv).astype(
        jnp.bfloat16
    )
    head_split = qkv.reshape(seq_count, length, 3, HEADS, HEAD_DIM)
    context, log_total = lax.map(
        attend_forward, (head_split[:, :, 0], head_split[:, :, 1], head_split[:, :, 2], segments)
    )
    context = context.reshape(-1, D)
    residual = (
        tokens.astype(jnp.float32)
        + jnp.dot(context, out_weight, preferred_element_type=jnp.float32)
        + att_terms[2]
    )
    first_out, first_hat, first_rstd = normalize(residual, att_terms[3], att_terms[4])
    ffn_full = lax.all_gather(ffn_master.astype(jnp.bfloat16), "dp", axis=0, tiled=True)
    in_weight, down_weight, in_bias, ffn_terms = split_ffn(ffn_full)
    first_low = first_out.astype(jnp.bfloat16)
    ffn_inner = jnp.dot(first_low, in_weight, preferred_element_type=jnp.float32) + in_bias
    ffn_act = jax.nn.gelu(ffn_inner, approximate=False).astype(jnp.bfloat16)
    second_in = (
        first_out + jnp.dot(ffn_act, down_weight, preferred_element_type=jnp.float32) + ffn_terms[0]
    )
    output, second_hat, second_rstd = normalize(second_in, ffn_terms[1], ffn_terms[2])
    att_back = lax.all_gather(att_master.astype(jnp.bfloat16), "dp", axis=0, tiled=True)
    qkv_weight, out_weight, att_terms = split_attention(att_back)
    ffn_back = lax.all_gather(ffn_master.astype(jnp.bfloat16), "dp", axis=0, tiled=True)
    in_weight, down_weight, in_bias, ffn_terms = split_ffn(ffn_back)

    def microbatch(micro_index, state_now):
        grad_sums, input_grads = state_now

        def take_rows(array_in):
            return lax.dynamic_slice_in_dim(array_in, micro_index * length, length, 0)

        grad_out = take_rows(cotangent).astype(jnp.float32)
        grad_second, grad_gain_two, grad_shift_two = norm_back(
            grad_out, take_rows(second_hat), take_rows(second_rstd), ffn_terms[1]
        )
        grad_down = grad_second.astype(jnp.bfloat16)
        grad_down_bias = jnp.sum(grad_down.astype(jnp.float32), 0)
        grad_down_weight = jnp.dot(
            take_rows(ffn_act).T, grad_down, preferred_element_type=jnp.float32
        )
        grad_act = jnp.dot(grad_down, down_weight.T, preferred_element_type=jnp.float32)
        grad_inner = (grad_act * gelu_slope(take_rows(ffn_inner))).astype(jnp.bfloat16)
        grad_in_bias = jnp.sum(grad_inner.astype(jnp.float32), 0)
        grad_in_weight = jnp.dot(
            take_rows(first_low).T, grad_inner, preferred_element_type=jnp.float32
        )
        grad_first = grad_second + jnp.dot(
            grad_inner, in_weight.T, preferred_element_type=jnp.float32
        )
        grad_residual, grad_gain_one, grad_shift_one = norm_back(
            grad_first, take_rows(first_hat), take_rows(first_rstd), att_terms[3]
        )
        grad_proj = grad_residual.astype(jnp.bfloat16)
        grad_out_bias = jnp.sum(grad_proj.astype(jnp.float32), 0)
        grad_out_weight = jnp.dot(
            take_rows(context).T, grad_proj, preferred_element_type=jnp.float32
        )
        grad_context = jnp.dot(grad_proj, out_weight.T, preferred_element_type=jnp.float32).astype(
            jnp.bfloat16
        )
        this_seq = lax.dynamic_index_in_dim(head_split, micro_index, 0, keepdims=False)
        this_segs = lax.dynamic_index_in_dim(segments, micro_index, 0, keepdims=False)
        this_total = lax.dynamic_index_in_dim(log_total, micro_index, 0, keepdims=False)
        grad_qkv = attend_backward(
            this_seq[:, 0],
            this_seq[:, 1],
            this_seq[:, 2],
            this_segs,
            this_total,
            grad_context.reshape(length, HEADS, HEAD_DIM),
        )
        grad_qkv = grad_qkv.astype(jnp.bfloat16)
        grad_wide = grad_qkv.astype(jnp.float32)
        grad_query_bias = jnp.sum(grad_wide[:, :D], 0)
        grad_value_bias = jnp.sum(grad_wide[:, 2 * D :], 0)
        grad_qkv_weight = jnp.dot(take_rows(tokens).T, grad_qkv, preferred_element_type=jnp.float32)
        grad_tokens = (
            jnp.dot(grad_qkv, qkv_weight.T, preferred_element_type=jnp.float32) + grad_residual
        )
        input_grads = lax.dynamic_update_slice_in_dim(
            input_grads, grad_tokens.astype(jnp.bfloat16), micro_index * length, 0
        )
        terms_now = (
            grad_qkv_weight,
            grad_out_weight,
            grad_query_bias,
            grad_value_bias,
            grad_out_bias,
            grad_gain_one,
            grad_shift_one,
            grad_in_weight,
            grad_down_weight,
            grad_in_bias,
            grad_down_bias,
            grad_gain_two,
            grad_shift_two,
        )
        grad_sums = tuple((running + fresh for running, fresh in zip(grad_sums, terms_now)))
        return (grad_sums, input_grads)

    zero_sums = (
        jnp.zeros((D, 3 * D), jnp.float32),
        jnp.zeros((D, D), jnp.float32),
        jnp.zeros((D,), jnp.float32),
        jnp.zeros((D,), jnp.float32),
        jnp.zeros((D,), jnp.float32),
        jnp.zeros((D,), jnp.float32),
        jnp.zeros((D,), jnp.float32),
        jnp.zeros((D, FF), jnp.float32),
        jnp.zeros((FF, D), jnp.float32),
        jnp.zeros((FF,), jnp.float32),
        jnp.zeros((D,), jnp.float32),
        jnp.zeros((D,), jnp.float32),
        jnp.zeros((D,), jnp.float32),
    )
    zero_inputs = jnp.zeros(tokens.shape, jnp.bfloat16)
    grad_sums, input_grad = lax.fori_loop(0, live_count[0], microbatch, (zero_sums, zero_inputs))
    dp_count = lax.axis_size("dp")
    att_pad = att_master.shape[0] * dp_count - 4 * D * D - 5 * D
    ffn_pad = ffn_master.shape[0] * dp_count - 2 * D * FF - FF - 3 * D
    att_local = jnp.concatenate(
        [
            grad_sums[0].reshape(-1),
            grad_sums[1].reshape(-1),
            grad_sums[2],
            grad_sums[3],
            grad_sums[4],
            grad_sums[5],
            grad_sums[6],
            jnp.zeros((att_pad,), jnp.float32),
        ]
    )
    ffn_local = jnp.concatenate(
        [
            grad_sums[7].reshape(-1),
            grad_sums[8].reshape(-1),
            grad_sums[9],
            grad_sums[10],
            grad_sums[11],
            grad_sums[12],
            jnp.zeros((ffn_pad,), jnp.float32),
        ]
    )
    att_rows, ffn_rows = (
        lax.all_to_all(
            att_local.reshape(dp_count, -1).astype(jnp.bfloat16),
            "dp",
            split_axis=0,
            concat_axis=0,
            tiled=True,
        ).astype(jnp.float32),
        lax.all_to_all(
            ffn_local.reshape(dp_count, -1).astype(jnp.bfloat16),
            "dp",
            split_axis=0,
            concat_axis=0,
            tiled=True,
        ).astype(jnp.float32),
    )
    att_share = jnp.sum(att_rows, 0)
    ffn_share = jnp.sum(ffn_rows, 0)
    att_grad, ffn_grad = (
        lax.psum(att_share.astype(jnp.bfloat16), "rep").astype(jnp.float32),
        lax.psum(ffn_share.astype(jnp.bfloat16), "rep").astype(jnp.float32),
    )
    att_new = adam_update(att_master, att_first, att_second, att_grad)
    ffn_new = adam_update(ffn_master, ffn_first, ffn_second, ffn_grad)
    return (
        output.astype(jnp.bfloat16),
        input_grad,
        att_grad,
        att_new[0],
        att_new[1],
        att_new[2],
        ffn_grad,
        ffn_new[0],
        ffn_new[1],
        ffn_new[2],
    )


MESH_ID = pl.DeviceIdType.MESH


def when(cond, act):
    if cond is None:
        act()
    else:
        pl.when(cond)(act)


class Place:
    def __init__(self, levels):
        self.levels = levels
        d = lax.axis_index("dp")
        c = lax.axis_index("rep")
        self.d, self.c = d, c
        self.z, y, x = d // 4, (d // 2) % 2, d % 2
        x_near, y_near = d + 1 - 2 * x, d + 2 - 4 * y
        self.a_near = x_near + c * (y_near - x_near)
        self.b_near = y_near + c * (x_near - y_near)
        self.far = x_near + y_near - d
        self.a_at = x + c * (y - x)
        self.b_at = y + c * (x - y)
        self.up = (d + 4, c)
        self.down = (d - 4, c)
        self.has_up = self.z < levels - 1
        self.has_down = self.z > 0
        self.across_a = (self.a_near, c)
        self.across_b = (self.b_near, c)
        self.sibling = (d, 1 - c)

    def levels_at(self, distance):
        if distance == 0:
            return [(self.z, None, 0)]
        return [
            (self.z - distance, self.z >= distance, -1),
            (self.z + distance, self.z + distance < self.levels, 1),
        ]

    def at(self, column, level):
        return column + 4 * (level - self.z)

    def turn(self, distance):
        return self.at(self.d, (self.z + distance) % self.levels)

    def along(self, step):
        return (self.up, self.has_up) if step > 0 else (self.down, self.has_down)

    def meet(self):
        barrier = pltpu.get_barrier_semaphore()

        def greet(device):
            pl.semaphore_signal(barrier, inc=1, device_id=device, device_id_type=MESH_ID)

        for device in (self.across_a, self.across_b, self.sibling):
            greet(device)
        count = 3
        for distance in range(1, self.levels):
            greet((self.turn(distance), self.c))
            count += 1
        after, before = self.d < 4 * self.levels - 1, self.d > 0
        edges = [((self.d + 1, self.c), after), ((self.d - 1, self.c), before)]
        edges += [((self.d + 1, 0), after & (self.c == 1)), ((self.d - 1, 1), before & (self.c == 0))]
        for device, there in edges:
            pl.when(there)(functools.partial(greet, device))
            count = count + there.astype(jnp.int32)
        pl.semaphore_wait(barrier, count)


def both(first, second):
    if first is None:
        return second
    return first if second is None else first & second


class Sends:
    def __init__(self):
        self.steps, self.closing = [], False

    def go(self, step):
        if not any(step is other for other in self.steps):
            self.steps.append(step)
        step()

    def later(self, step):
        return lambda: self.go(step)

    def start(self, cond, make):
        when(cond, lambda: make().wait_send() if self.closing else make().start())

    def wait(self, cond, make):
        if not self.closing:
            when(cond, lambda: make().wait_recv())

    def finish(self):
        self.closing = True
        for step in self.steps:
            step()


def remote(src, dst, send_sem, recv_sem, device):
    return pltpu.make_async_remote_copy(
        src_ref=src,
        dst_ref=dst,
        send_sem=send_sem,
        recv_sem=recv_sem,
        device_id=device,
        device_id_type=MESH_ID,
    )


class Gather:
    def __init__(self, place, ref, parts, lanes, send_sem, recv_sem, sib_sem):
        self.place, self.ref, self.parts, self.lanes = place, ref, parts, lanes
        self.send_sem, self.recv_sem, self.sib_sem = send_sem, recv_sem, sib_sem
        self.half = ref.shape[2] // 2
        levels = place.levels
        self.leave = {2: levels, 3: 2 * levels, 4: 4 * levels - 1}
        self.together = 1

    def rows(self, core):
        return pl.ds(pl.multiple_of(core * self.half, self.half), self.half)

    def piece(self, chip, core):
        return self.ref.at[chip, self.parts, self.rows(core), self.lanes]

    def several(self, count):
        return self.ref.at[pl.ds(0, count), self.parts, pl.ds(0, self.half), self.lanes]

    def send(self, cond, chip, way, device):
        own = self.piece(chip, self.place.c)
        recv = self.sib_sem if way == 4 else self.recv_sem.at[chip]
        when(cond, lambda: remote(own, own, self.send_sem.at[way], recv, device).start())

    def wait(self, cond, part, sem):
        when(cond, lambda: remote(part, part, self.send_sem.at[0], sem, self.place.sibling).wait_recv())

    def arrived(self, cond, chip):
        self.wait(cond, self.piece(chip, self.place.c), self.recv_sem.at[chip])

    def own(self):
        p = self.place
        self.send(p.has_up, p.d, 0, p.up)
        self.send(p.has_down, p.d, 1, p.down)
        self.send(None, p.d, 3, p.across_b)
        self.send(None, p.d, 2, p.across_a)

    def line(self, distance):
        p = self.place
        for level, there, step in p.levels_at(distance):
            chip = p.at(p.d, level)
            self.arrived(there, chip)
            onward, more = p.along(-step)
            self.send(both(there, more), chip, 0 if step < 0 else 1, onward)
            self.send(there, chip, 3, p.across_b)
            self.send(there, chip, 2, p.across_a)
            self.send(there, chip, 4, p.sibling)

    def over_a(self, distance):
        p = self.place
        for level, there, _ in p.levels_at(distance):
            chip = p.at(p.a_near, level)
            self.arrived(there, chip)
            self.send(there, chip, 3, p.across_b)
            self.send(there, chip, 4, p.sibling)

    def over_b(self, distance):
        p = self.place
        for column in (p.b_near, p.far):
            for level, there, _ in p.levels_at(distance):
                chip = p.at(column, level)
                self.arrived(there, chip)
                self.send(there, chip, 4, p.sibling)

    def from_sibling(self):
        self.wait(None, self.several(4 * self.place.levels - 1), self.sib_sem)

    def left(self, cond, way, count):
        part = self.several(count)
        sem = self.send_sem.at[way]
        when(cond, lambda: remote(part, part, sem, self.sib_sem, self.place.sibling).wait_send())

    def finish(self):
        p = self.place
        for way, count in self.leave.items():
            self.left(None, way, count)
        for level in range(p.levels):
            if level < p.levels - 1:
                self.left(p.z == level, 0, self.together * (level + 1))
            if level > 0:
                self.left(p.z == level, 1, self.together * (p.levels - level))


class Plane(Gather):
    def __init__(self, place, ref, parts, lanes, send_sem, recv_sem, sib_sem):
        super().__init__(place, ref, parts, lanes, send_sem, recv_sem, sib_sem)
        self.leave = {2: 1, 3: 2, 4: 4 * place.levels - 1}
        self.together = 4
        self.from_a, self.from_b = place.levels, place.levels + 1

    def send(self, cond, chip, way, device):
        own = self.piece(chip, self.place.c)
        recv = self.sib_sem if way == 4 else self.recv_sem.at[self.from_a if way == 2 else self.from_b]
        when(cond, lambda: remote(own, own, self.send_sem.at[way], recv, device).start())

    def own(self):
        p = self.place
        self.send(None, p.d, 2, p.across_a)
        self.send(None, p.d, 3, p.across_b)

    def near(self):
        p = self.place
        self.wait(None, self.piece(p.a_near, p.c), self.recv_sem.at[self.from_a])
        self.send(None, p.a_near, 3, p.across_b)
        self.send(None, p.a_near, 4, p.sibling)

    def sheet(self, level):
        return self.ref.at[pl.ds(4 * level, 4), self.parts, self.rows(self.place.c), self.lanes]

    def send_sheet(self, cond, level, way, device):
        own = self.sheet(level)
        recv = self.sib_sem if way == 4 else self.recv_sem.at[level]
        when(cond, lambda: remote(own, own, self.send_sem.at[way], recv, device).start())

    def complete(self):
        p = self.place
        self.wait(None, self.several(2), self.recv_sem.at[self.from_b])
        self.send_sheet(p.has_up, p.z, 0, p.up)
        self.send_sheet(p.has_down, p.z, 1, p.down)
        for chip in (p.b_near, p.far):
            self.send(None, chip, 4, p.sibling)

    def line(self, distance):
        p = self.place
        for level, there, step in p.levels_at(distance):
            self.wait(there, self.sheet(level), self.recv_sem.at[level])
            onward, more = p.along(-step)
            self.send_sheet(both(there, more), level, 0 if step < 0 else 1, onward)
            self.send_sheet(there, level, 4, p.sibling)


class Spread:
    def __init__(self, place, sends, ref, send_sem, recv_sem):
        self.place, self.sends, self.ref = place, sends, ref
        self.send_sem, self.recv_sem = send_sem, recv_sem

    def copy(self, way, device):
        return remote(self.ref, self.ref, self.send_sem.at[way], self.recv_sem, device)

    def wait(self, cond):
        self.sends.wait(cond, lambda: self.copy(0, self.place.sibling))

    def run(self):
        p = self.place
        home = (p.a_at == 1) & (p.b_at == 1)
        self.wait(home & p.has_up)
        self.sends.start(home & p.has_down, lambda: self.copy(0, p.down))
        self.wait((p.a_at == 0) & (p.b_at == 1))
        self.sends.start(home, lambda: self.copy(1, p.across_a))
        self.wait(p.b_at == 0)
        self.sends.start(p.b_at == 1, lambda: self.copy(2, p.across_b))


def shifted(ref, start, rows):
    first, turn = start // 128, start % 128
    here = pltpu.roll(ref[pl.ds(first, rows), :], (128 - turn) % 128, 1)
    after = pltpu.roll(ref[pl.ds(first + 1, rows), :], (128 - turn) % 128, 1)
    lane = lax.broadcasted_iota(jnp.int32, (rows, 128), 1)
    return jnp.where(lane < 128 - turn, here, after)


class Flat:
    def __init__(self, length, chips, parts, split, turned):
        self.length, self.chips, self.parts, self.turned = length, chips, parts, turned
        self.rows = length // D // parts * parts
        self.slip = length - self.rows * D
        self.deep = self.rows // parts
        self.split = split
        self.lines = self.rows * (D // 128)
        self.most = self.slip * chips
        self.halo = -(-self.most // 1024) * 8
        self.held = -(-length // 1024) * 8
        self.tail_from = (length - self.most) // 1024 * 8
        self.tail = self.held - self.tail_from

    def place_of(self, part, block, split):
        if split:
            return 6 * part + block, 6 * self.parts
        return 6 * self.deep * part + block, 6


class Lead:
    def __init__(self, place, sends, flat, long_ref, halo_ref, line_ref, send_sem, recv_sem):
        self.place, self.sends, self.flat = place, sends, flat
        self.long_ref, self.halo_ref, self.line_ref = long_ref, halo_ref, line_ref
        self.send_sem, self.recv_sem = send_sem, recv_sem

    def copy(self):
        f, p = self.flat, self.place
        return remote(
            self.long_ref.at[pl.ds(f.halo + f.tail_from, f.tail), :],
            self.halo_ref.at[pl.ds(0, f.tail), :],
            self.send_sem,
            self.recv_sem,
            (p.d + 1, p.c),
        )

    def begin(self):
        self.sends.start(self.place.d < self.flat.chips - 1, self.copy)

    def lines(self):
        p, f = self.place, self.flat
        slip = f.slip * p.d
        self.line_ref[pl.ds(0, f.lines), :] = shifted(self.long_ref, f.halo * 128 - slip, f.lines)

        def mend():
            self.copy().wait_recv()
            before = shifted(self.halo_ref, f.length - f.tail_from * 128 - slip, f.halo)
            at = lax.broadcasted_iota(jnp.int32, (f.halo, 128), 0) * 128
            at = at + lax.broadcasted_iota(jnp.int32, (f.halo, 128), 1)
            self.line_ref[pl.ds(0, f.halo), :] = jnp.where(at < slip, before, self.line_ref[pl.ds(0, f.halo), :])

        pl.when(p.d > 0)(mend)

    def store(self, out_ref):
        p, f = self.place, self.flat

        def put(split):
            for part in range(f.parts):
                for block in range(D // 128):
                    first, stride = f.place_of(part, block, split)
                    out_ref[p.d, part, :, pl.ds(128 * block, 128)] = self.line_ref[
                        pl.ds(first, f.deep, stride=stride), :
                    ].astype(jnp.bfloat16)

        pl.when(p.d < f.split)(lambda: put(True))
        pl.when(p.d >= f.split)(lambda: put(False))

    def last_rows(self, count):
        f = self.flat
        lines = -(-count * 6 // 8) * 8
        return shifted(self.long_ref, f.halo * 128 + f.length - count * D, lines)


class Reduce:
    def __init__(self, place, parts, chips, batches, view, slots, kept, send_sem, recv_sem, whole=None):
        self.place, self.parts, self.batches = place, parts, batches
        self.view, self.slots, self.kept = view, slots, kept
        self.send_sem, self.recv_sem, self.whole = send_sem, recv_sem, whole
        self.levels = [level for batch in batches for level in batch]
        self.from_b, self.from_a = chips, chips + 2 * place.levels
        self.from_z = chips + 3 * place.levels

    def arrival(self, kind, batch):
        return self.recv_sem.at[batch, kind]

    def wait(self, part, sem):
        remote(part, part, self.send_sem.at[0], sem, self.place.sibling).wait_recv()

    def send(self, cond, chip, way, dst, recv, device):
        p = self.place
        src = self.view(chip, 1 - p.c if way == 4 else p.c)
        when(cond, lambda: remote(src, dst, self.send_sem.at[way], recv, device).start())

    def add(self, chip, src):
        here = self.view(chip, self.place.c)
        for part in range(self.parts):
            here[part] = here[part] + src[part]

    def share(self, batch):
        p = self.place
        recv = self.arrival(0, batch)
        if self.whole is not None:
            src, dst = self.whole
            remote(src, dst, self.send_sem.at[4], recv, p.sibling).start()
            return
        for level in self.batches[batch]:
            for column in (p.far, p.b_near, p.a_near, p.d):
                chip = p.at(column, level)
                self.send(None, chip, 4, self.slots(chip, 1), recv, p.sibling)

    def over_b(self, batch):
        p = self.place
        levels = self.batches[batch]
        self.wait(self.slots(4 * levels[0], 4 * len(levels)), self.arrival(0, batch))
        for kind, column in ((1, p.far), (0, p.b_near)):
            for level in levels:
                chip = p.at(column, level)
                self.add(chip, self.slots(chip, 1))
                dst = self.slots(self.from_b + p.levels * kind + level, 1)
                self.send(None, chip, 3, dst, self.arrival(1 + kind, batch), p.across_b)

    def over_a(self, batch):
        p = self.place
        levels = self.batches[batch]
        first = self.from_b + p.levels
        self.wait(self.slots(first + levels[0], len(levels)), self.arrival(2, batch))
        for level in levels:
            chip = p.at(p.a_near, level)
            self.add(chip, self.slots(chip, 1))
            self.add(chip, self.slots(first + level, 1))
            self.send(None, chip, 2, self.slots(self.from_a + level, 1), self.arrival(3, batch), p.across_a)

    def collect(self, batch):
        p = self.place
        levels = self.batches[batch]
        self.wait(self.slots(self.from_b + levels[0], len(levels)), self.arrival(1, batch))
        self.wait(self.slots(self.from_a + levels[0], len(levels)), self.arrival(3, batch))
        for level in levels:
            chip = p.at(p.d, level)
            for first in (0, self.from_b, self.from_a):
                self.add(chip, self.slots(first + level if first else chip, 1))

    def line(self, batch):
        p = self.place
        dst = self.slots(self.from_z + p.z, 1)
        for level in self.batches[batch]:
            chip = p.at(p.d, level)
            self.send(p.z != level, chip, 0, dst, self.arrival(4, batch), (chip, p.c))

    def keep(self):
        p = self.place
        own = self.kept(p.c)

        def total(batch):
            self.wait(self.slots(self.from_z, p.levels - 1), self.arrival(4, batch))
            here = self.view(p.d, p.c)
            others = [self.slots(self.from_z + (p.z + i) % p.levels, 1) for i in range(1, p.levels)]
            for part in range(self.parts):
                sum_now = here[part].astype(jnp.float32)
                for other in others:
                    sum_now = sum_now + other[part].astype(jnp.float32)
                own[part] = sum_now

        for batch, levels in enumerate(self.batches):
            pl.when((p.z >= levels[0]) & (p.z <= levels[-1]))(functools.partial(total, batch))

    def left(self, cond, way, count):
        part = self.slots(0, count)
        sem = self.send_sem.at[way]
        when(cond, lambda: remote(part, part, sem, self.recv_sem.at[0, 0], self.place.sibling).wait_send())

    def finish(self):
        p = self.place
        count = len(self.levels)
        for way, pieces in ((4, 4 * count), (3, 2 * count), (2, count)):
            self.left(None, way, pieces)
        for z in range(p.levels):
            self.left(p.z == z, 0, count - (z in self.levels))


class Chain(Reduce):
    def __init__(self, extra, line_sem, *rest):
        super().__init__(*rest)
        self.extra, self.line_sem = extra, line_sem

    def pass_on(self, here, level, way, waits, dst, device):
        p = self.place
        chip = p.at(p.d, level)
        slot = self.slots(self.from_z + level, 1)

        def act():
            if waits:
                self.wait(slot, self.line_sem.at[way, level])
                self.add(chip, slot)
            self.send(None, chip, way, dst, self.line_sem.at[way, level], device)

        pl.when(here)(act)

    def line(self, distance, batch):
        p = self.place
        for level in self.batches[batch]:
            slot = self.slots(self.from_z + level, 1)
            if level >= distance:
                self.pass_on(p.z == level - distance, level, 0, level > distance, slot, p.up)
            if level + distance < p.levels:
                dst = slot if distance > 1 else self.extra
                self.pass_on(p.z == level + distance, level, 1, level + distance < p.levels - 1, dst, p.down)

    def keep(self):
        p = self.place
        own = self.kept(p.c)

        def at(level):
            here = self.view(p.d, p.c)
            for part in range(self.parts):
                own[part] = here[part].astype(jnp.float32)
            sources = [(0, self.slots(self.from_z + level, 1))] if level > 0 else []
            sources += [(1, self.extra)] if level < p.levels - 1 else []
            for way, src in sources:
                self.wait(src, self.line_sem.at[way, level])
                for part in range(self.parts):
                    own[part] = own[part] + src[part].astype(jnp.float32)

        for level in self.levels:
            pl.when(p.z == level)(functools.partial(at, level))

    def finish(self):
        p = self.place
        count = len(self.levels)
        for way, pieces in ((4, 4 * count), (3, 2 * count), (2, count)):
            self.left(None, way, pieces)
        for z in range(p.levels):
            for way, pieces in enumerate((sum(n > z for n in self.levels), sum(n < z for n in self.levels))):
                if pieces:
                    self.left(p.z == z, way, pieces)


def handed(place, own_ref, core, send_sem, recv_sem):
    own = own_ref.at[core]
    return remote(own, own, send_sem, recv_sem, place.sibling)


class Terms:
    def __init__(self, place, sends, ref, got_ref, all_ref, send_sem, recv_sem):
        self.place, self.sends, self.ref, self.got_ref, self.all_ref = place, sends, ref, got_ref, all_ref
        self.send_sem, self.recv_sem = send_sem, recv_sem

    def copy(self, way, core, device):
        return remote(self.ref.at[core], self.got_ref.at[way], self.send_sem.at[way], self.recv_sem.at[way], device)

    def add(self, cond, way):
        if self.sends.closing:
            return

        def act():
            self.copy(way, 0, self.place.sibling).wait_recv()
            self.ref[self.place.c] = self.ref[self.place.c] + self.got_ref[way]

        when(cond, act)

    def share(self):
        self.sends.start(None, lambda: self.copy(0, 1 - self.place.c, self.place.sibling))

    def over_b(self):
        p = self.place
        self.add(None, 0)
        self.sends.start(p.b_at == 0, lambda: self.copy(1, p.c, p.across_b))

    def over_a(self):
        p = self.place
        self.add(p.b_at == 1, 1)
        self.sends.start((p.b_at == 1) & (p.a_at == 0), lambda: self.copy(2, p.c, p.across_a))

    def line(self):
        p = self.place
        home = (p.b_at == 1) & (p.a_at == 1)
        self.add(home, 2)
        here, top = self.ref.at[p.c], p.at(p.d, p.levels - 1)
        self.sends.start(
            home & p.has_up,
            lambda: remote(here, self.got_ref.at[3 + p.z], self.send_sem.at[3], self.recv_sem.at[3], (top, p.c)),
        )

    def keep(self):
        p = self.place
        got = self.got_ref.at[pl.ds(3, p.levels - 1)]
        remote(got, got, self.send_sem.at[3], self.recv_sem.at[3], p.sibling).wait_recv()
        for level in range(p.levels - 1):
            self.ref[p.c] = self.ref[p.c] + self.got_ref[3 + level]

    def final(self):
        return remote(
            self.ref.at[self.place.c],
            self.all_ref.at[self.place.c],
            self.send_sem.at[4],
            self.recv_sem.at[4],
            self.place.sibling,
        )

    def hand_over(self):
        p = self.place
        last = p.d == 4 * p.levels - 1
        if not self.sends.closing:
            pl.when(last)(self.keep)
        self.sends.start(last, self.final)

    def take_over(self):
        self.final().wait_recv()
        self.all_ref[self.place.c] = self.ref[self.place.c]


class Trail:
    def __init__(self, place, sends, flat, own_ref, line_ref, out_ref, send_sem, recv_sem, more_sem=None):
        self.place, self.sends, self.flat = place, sends, flat
        self.own_ref, self.line_ref, self.out_ref = own_ref, line_ref, out_ref
        self.send_sem, self.recv_sem, self.more_sem = send_sem, recv_sem, more_sem

    def copy(self, send_sem=None, device=None):
        f, p = self.flat, self.place
        return remote(
            self.line_ref.at[pl.ds(0, f.halo), :],
            self.line_ref.at[pl.ds(f.lines, f.halo), :],
            self.send_sem if send_sem is None else send_sem,
            self.recv_sem,
            (p.d - 1, p.c) if device is None else device,
        )

    def put(self, split, core):
        f = self.flat
        half = f.deep // 2
        for part in range(f.parts):
            for block in range(D // 128):
                first, stride = f.place_of(part, block, split)
                first = first + stride * half * core
                self.line_ref[pl.ds(first, half, stride=stride), :] = self.own_ref[
                    core, part, :, pl.ds(128 * block, 128)
                ]

    def half_lines(self, core, cond):
        p, f = self.place, self.flat
        pl.when(cond & (p.d < f.split))(lambda: self.put(True, core))
        pl.when(cond & (p.d >= f.split))(lambda: self.put(False, core))

    def early_back(self):
        p, f = self.place, self.flat
        for core, send_sem in ((0, self.send_sem), (1, self.more_sem)):
            make = lambda core=core, send_sem=send_sem: self.copy(send_sem, (p.d - 1, core))
            self.sends.start((p.c == 0) & (p.d > 0), make)

    def lines(self):
        p, f = self.place, self.flat

        def put(split):
            for core in range(2):
                self.put(split, core)

        def put_turned():
            for j in range(f.rows // 128):
                blocks = []
                for i in range(D // f.deep):
                    lanes = pl.ds(128 * (3 * (i % 2) + j), 128)
                    blocks += [self.own_ref[core, i // 2, :, lanes] for core in range(2)]
                turned = jnp.concatenate(blocks, 0).T
                for block in range(D // 128):
                    first = 6 * 128 * j + block
                    self.line_ref[pl.ds(first, 128, stride=6), :] = turned[:, 128 * block : 128 * (block + 1)]

        pl.when(p.d < f.split)(lambda: put(True))
        pl.when(p.d >= f.split)(put_turned if f.turned else lambda: put(False))

    def pass_back(self):
        self.sends.start(self.place.d > 0, self.copy)

    def last_rows(self, terms_ref, at, count):
        f = self.flat
        for core in range(2):
            for block in range(3):
                self.line_ref[pl.ds(f.lines + 3 * core + block, count, stride=6), :] = terms_ref[
                    core, pl.ds(at, count), pl.ds(128 * block, 128)
                ]

    def out(self):
        p, f = self.place, self.flat
        pl.when(p.d < f.chips - 1)(lambda: self.copy().wait_recv())
        self.out_ref[pl.ds(0, f.held), :] = shifted(self.line_ref, f.slip * p.d, f.held)


def dot(a, b):
    return jnp.dot(a, b, preferred_element_type=jnp.float32)


def dot_nt(a, b):
    return lax.dot_general(a, b, (((1,), (1,)), ((), ())), preferred_element_type=jnp.float32)


def square(values):
    return values.reshape(D, D)


def tile(index, size):
    return pl.ds(pl.multiple_of(index * size, size), size)


def loop(count, step, beside=()):
    def body(i, _):
        step(i)
        for at, act in beside:
            pl.when(i == at)(act)
        return 0

    lax.fori_loop(0, count, body, 0)


TILE, WIDE = 256, 512


class Layer:
    def __init__(self, refs, att_split, ffn_split, seqs, length):
        self.__dict__.update(refs)
        self.att_split, self.ffn_split = att_split, ffn_split
        self.seqs, self.length = seqs, length
        self.tiles = seqs * length // TILE

    def whole(self, blocks, part):
        count = blocks.shape[0] // 4
        return blocks[pl.ds(count * part, count)].reshape(self.seqs * self.length, D)

    def some(self, blocks, part, r, size=TILE):
        count = size // blocks.shape[1]
        return pl.ds(blocks.shape[0] // 4 * part + count * r, count)

    def qkv_weight(self, part):
        return square(self.att_w[pl.ds(0, self.att_split), part])

    def out_weight(self):
        return square(self.att_w[pl.ds(self.att_split, self.att_w.shape[0] - self.att_split)])

    def in_weight(self, part):
        return square(self.ffn_w[pl.ds(0, self.ffn_split), part])

    def down_weight(self, part):
        return square(self.ffn_w[pl.ds(self.ffn_split + 2 * part, 2)])

    def term(self, row):
        return self.terms[pl.ds(row, 1), :]

    def add_term(self, row, values):
        self.term_grads[pl.ds(row, 1), :] += jnp.sum(values, 0, keepdims=True)


    def qkv(self, beside=()):
        def step(r):
            rows = tile(r, TILE)
            x = self.tok[rows, :]
            queries = (dot(x, self.qkv_weight(0)) + self.term(0)).astype(jnp.bfloat16)
            self.heads[0, rows, :] = queries * HEAD_DIM ** (-0.5)
            self.heads[1, rows, :] = dot(x, self.qkv_weight(1)).astype(jnp.bfloat16)
            self.heads[2, rows, :] = (dot(x, self.qkv_weight(2)) + self.term(1)).astype(jnp.bfloat16)

        loop(self.tiles, step, beside)

    def make_bias(self):
        segs = self.segs[...].astype(jnp.float32)
        columns = jnp.concatenate([segs, jnp.zeros((8 - self.seqs, self.length), jnp.float32)], 0).T
        for seq in range(self.seqs):
            same = columns[:, seq : seq + 1] == segs[seq : seq + 1, :]
            self.bias[pl.ds(seq * self.length, self.length), :] = jnp.where(same, 0.0, masked)

    def lane_half(self, half):
        lane = lax.broadcasted_iota(jnp.int32, (self.length, 2 * HEAD_DIM), 1)
        return (lane // HEAD_DIM) == half

    def attend(self, beside=()):
        self.make_bias()

        def step(i):
            seq, pair = i // (HEADS // 2), i % (HEADS // 2)
            lanes = tile(pair, 2 * HEAD_DIM)
            rows = tile(seq, self.length)
            queries, keys, values = (self.heads[j, rows, lanes] for j in range(3))
            values_t = values.T
            parts = []
            for half in range(2):
                own = jnp.where(self.lane_half(half), queries, jnp.zeros_like(queries))
                scores = dot_nt(keys, own) + self.bias[rows, :]
                top = jnp.max(scores, 0, keepdims=True)
                raised = jnp.exp(scores - top)
                total = jnp.sum(raised, 0, keepdims=True)
                probs = (raised * (1.0 / total)).astype(jnp.bfloat16)
                self.totals[pl.ds(HEADS * seq + 2 * pair + half, 1), :] = top + jnp.log(total)
                parts.append(dot(values_t[HEAD_DIM * half : HEAD_DIM * (half + 1)], probs))
            both_t = jnp.concatenate(parts, 0).astype(jnp.bfloat16)
            self.ctx_t[lanes, rows] = both_t
            self.ctx[rows, lanes] = both_t.T

        loop(self.seqs * HEADS // 2, step, beside)

    def first_norm(self, beside=()):
        def step(r):
            rows = tile(r, TILE)
            residual = self.tok[rows, :].astype(jnp.float32) + dot(self.ctx[rows, :], self.out_weight()) + self.term(2)
            first, normed, rstd = normalize(residual, self.term(3), self.term(4))
            self.hat[rows, :] = normed
            self.rstd[rows, :] = rstd
            self.low_t[:, rows] = first.astype(jnp.bfloat16).T

        loop(self.tiles, step, beside)

    def feed(self, beside=()):
        def step(r):
            rows = tile(r, TILE)
            first = self.hat[rows, :] * self.term(3) + self.term(4)
            low = first.astype(jnp.bfloat16)
            second = first + self.term(12)
            for part in range(4):
                inner = dot(low, self.in_weight(part)) + self.term(8 + part)
                cdf, slope = gelu_parts(inner)
                act = (inner * cdf).astype(jnp.bfloat16)
                self.act[self.some(self.act, part, r)] = act.reshape(-1, self.act.shape[1], D)
                slope = slope.astype(jnp.bfloat16).reshape(-1, self.slope.shape[1], D)
                self.slope[self.some(self.slope, part, r)] = slope
                second = second + dot(act, self.down_weight(part))
            out, normed, rstd = normalize(second, self.term(13), self.term(14))
            seq = r // (self.length // TILE)
            live = jnp.clip(self.live_count[0] - seq, 0, 1).astype(jnp.float32)
            grad_out = self.cot[rows, :].astype(jnp.float32) * live
            self.out[rows, :] = out.astype(jnp.bfloat16)
            scaled = grad_out * self.term(13)
            grad = rstd * (
                scaled
                - jnp.mean(scaled, -1, keepdims=True)
                - normed * jnp.mean(scaled * normed, -1, keepdims=True)
            )
            self.add_term(13, grad_out * normed)
            self.add_term(14, grad_out)
            grad_down = grad.astype(jnp.bfloat16)
            self.add_term(12, grad_down.astype(jnp.float32))
            self.grad[rows, :] = grad
            self.down[rows, :] = grad_down
            self.down_t[:, rows] = grad_down.T

        loop(self.tiles, step, beside)


    def hidden_back(self, part, beside=()):
        def step(r):
            rows = tile(r, WIDE)
            grad_act = dot_nt(self.down[rows, :], self.down_weight(part))
            at = self.some(self.slope, part, r, WIDE)
            slope = self.slope[at].reshape(WIDE, D).astype(jnp.float32)
            inner = (grad_act * slope).astype(jnp.bfloat16)
            self.slope[at] = inner.reshape(-1, self.slope.shape[1], D)
            self.add_term(8 + part, inner.astype(jnp.float32))

        loop(self.seqs * self.length // WIDE, step, beside)

    def down_grads(self, part, beside=()):
        deep = self.ffn_w.shape[2]
        first = self.ffn_split + 2 * part
        count = self.act.shape[0] // 4

        def step(n):
            acts = self.act[pl.ds(count * part, count), :, tile(n, 256)].reshape(self.seqs * self.length, 256)
            grads = dot(self.down_t[...], acts).astype(jnp.bfloat16)
            for k in range(2):
                block = 2 * n + k
                for i in range(D // deep):
                    lanes = tile(3 * (i % 2) + block % 3, 128)
                    self.ffn_w[first + block // 3, i // 2, :, lanes] = grads[
                        deep * i : deep * (i + 1), 128 * k : 128 * (k + 1)
                    ]

        loop(3, step, beside)

    def in_back(self, part, beside=()):
        def step(r):
            rows = tile(r, WIDE)
            self.grad[rows, :] += dot_nt(
                self.slope[self.some(self.slope, part, r, WIDE)].reshape(WIDE, D), self.in_weight(part)
            )

        loop(self.seqs * self.length // WIDE, step, beside)

    def in_grads(self, part, beside=()):
        deep = self.ffn_w.shape[2]
        count = self.slope.shape[0] // 4

        def step(n):
            lanes = tile(n, 256)
            inner = self.slope[pl.ds(count * part, count), :, lanes].reshape(self.seqs * self.length, 256)
            grads = dot(self.low_t[...], inner).astype(jnp.bfloat16)
            self.ffn_w[pl.ds(0, self.ffn_split), part, :, lanes] = grads.reshape(self.ffn_split, deep, 256)

        loop(3, step, beside)

    def first_back(self, beside=()):
        def step(r):
            rows = tile(r, TILE)
            grad_first, normed = self.grad[rows, :], self.hat[rows, :]
            scaled = grad_first * self.term(3)
            grad = self.rstd[rows, :] * (
                scaled
                - jnp.mean(scaled, -1, keepdims=True)
                - normed * jnp.mean(scaled * normed, -1, keepdims=True)
            )
            self.add_term(3, grad_first * normed)
            self.add_term(4, grad_first)
            proj = grad.astype(jnp.bfloat16)
            self.add_term(2, proj.astype(jnp.float32))
            self.grad[rows, :] = grad
            shape = (-1, self.act.shape[1], D)
            self.act[self.some(self.act, 3, r)] = proj.reshape(shape)
            grad_context = dot_nt(proj, self.out_weight()).astype(jnp.bfloat16)
            self.act[self.some(self.act, 0, r)] = grad_context.reshape(shape)
            self.tok_t[:, rows] = self.tok[rows, :].T

        loop(self.tiles, step, beside)

    def out_grads(self, beside=()):
        count = self.act.shape[0] // 4

        def step(n):
            lanes = tile(n, 256)
            proj = self.act[pl.ds(3 * count, count), :, lanes].reshape(self.seqs * self.length, 256)
            grads = dot(self.ctx_t[...], proj).astype(jnp.bfloat16)
            owners = self.att_w.shape[0] - self.att_split
            shape = (owners, *self.att_w.shape[1:3], 256)
            self.att_w[pl.ds(self.att_split, owners), :, :, lanes] = grads.reshape(shape)

        loop(3, step, beside)

    def attend_back(self, group, beside=()):
        def step(i):
            seq, pair = i % self.seqs, 2 * group + i // self.seqs
            lanes = tile(pair, 2 * HEAD_DIM)
            rows = tile(seq, self.length)
            count = self.length // self.act.shape[1]
            queries, keys, values = (self.heads[j, rows, lanes] for j in range(3))
            grads = self.act[pl.ds(count * seq, count), :, lanes].reshape(self.length, 2 * HEAD_DIM)
            keys_t = keys.T
            parts = []
            grad_keys = grad_values = 0.0
            for half in range(2):
                here = self.lane_half(half)
                own = jnp.where(here, queries, jnp.zeros_like(queries))
                own_grads = jnp.where(here, grads, jnp.zeros_like(grads))
                total = self.totals[pl.ds(HEADS * seq + 2 * pair + half, 1), :]
                probs = jnp.exp(dot_nt(keys, own) + self.bias[rows, :] - total)
                grad_values = grad_values + dot(probs.astype(jnp.bfloat16), own_grads)
                grad_probs = dot_nt(values, own_grads)
                row_sum = jnp.sum(probs * grad_probs, 0, keepdims=True)
                grad_scores = (probs * (grad_probs - row_sum)).astype(jnp.bfloat16)
                grad_keys = grad_keys + dot(grad_scores, own)
                parts.append(dot(keys_t[HEAD_DIM * half : HEAD_DIM * (half + 1)], grad_scores))
            grad_queries = (jnp.concatenate(parts, 0) * HEAD_DIM ** (-0.5)).astype(jnp.bfloat16).T
            grad_values = grad_values.astype(jnp.bfloat16)
            self.heads[0, rows, lanes] = grad_queries
            self.heads[1, rows, lanes] = grad_keys.astype(jnp.bfloat16)
            self.heads[2, rows, lanes] = grad_values
            for row, grad in ((0, grad_queries), (1, grad_values)):
                self.term_grads[pl.ds(row, 1), lanes] += jnp.sum(grad.astype(jnp.float32), 0, keepdims=True)

        loop(2 * self.seqs, step, beside)

    def qkv_grads(self, group):
        lanes = pl.ds(4 * HEAD_DIM * group, 4 * HEAD_DIM)
        deep = self.att_w.shape[2]

        def step(part):
            grads = dot(self.tok_t[...], self.heads[part, :, lanes]).astype(jnp.bfloat16)
            for chip in range(self.att_split):
                self.act[self.act_first + 3 * chip + part, :, lanes] = grads[deep * chip : deep * (chip + 1)]

        loop(3, step)

    def input_back(self, beside=()):
        def step(r):
            rows = tile(r, TILE)
            total = self.grad[rows, :]
            for part in range(3):
                total = total + dot_nt(self.heads[part, rows, :], self.qkv_weight(part))
            self.gin[rows, :] = total.astype(jnp.bfloat16)

        loop(self.tiles, step, beside)


def gelu_parts(values):
    cdf = 0.5 * (1.0 + lax.erf(values * 0.5**0.5))
    return cdf, cdf + values * jnp.exp(-0.5 * values * values) * (2.0 * math.pi) ** (-0.5)


def batches(levels):
    half = levels // 2
    return [(level,) for level in range(half, levels)], [tuple(range(half))], [(levels - 1,)], [tuple(range(levels - 1))]


def scratch_shapes(levels, att, ffn, rows, seqs, length):
    bf16, f32 = jnp.bfloat16, jnp.float32
    vmem, dma = pltpu.VMEM, pltpu.SemaphoreType.DMA
    chips = att.chips
    turned = vmem((D, rows), bf16)
    f_batches, i_batches, o_batches, q_batches = batches(levels)
    shapes = dict(
        att_w=vmem((chips, att.parts, att.deep, D), bf16),
        ffn_w=vmem((chips, ffn.parts, ffn.deep, D), bf16),
        tok=vmem((rows, D), bf16),
        heads=vmem((3, rows, D), bf16),
        totals=vmem((seqs * HEADS, length), f32),
        ctx=vmem((rows, D), bf16),
        ctx_t=turned,
        hat=vmem((rows, D), f32),
        rstd=vmem((rows, 1), f32),
        low_t=turned,
        act=vmem((4 * rows // att.deep, att.deep, D), bf16),
        slope=vmem((8 * rows // att.deep, att.deep // 2, D), bf16),
        grad=vmem((rows, D), f32),
        down_t=turned,
        terms=vmem((16, D), f32),
        term_grads=vmem((16, D), f32),
        spare=vmem((48, 128), f32),
        terms_sum=vmem((2, 16, D // 2), f32),
        terms_got=vmem((2 + levels, 16, D // 2), f32),
        terms_all=vmem((2, 16, D // 2), f32),
        ffn_slots=vmem((chips + 4 * levels, ffn.parts, ffn.deep // 2, D), bf16),
        local_sem=dma((8,)),
        term_send=dma((3,)),
        term_recv=dma,
        sum_send=dma((5,)),
        sum_recv=dma((5,)),
        more_send=dma,
        free=pltpu.SemaphoreType.REGULAR,
        ffn_extra=vmem((ffn.parts, ffn.deep // 2, D), bf16),
        f_send=dma((5,)),
        f_line=dma((2, levels)),
        i_send=dma((2, 5)),
        i_recv=dma((2, len(i_batches), 5)),
        i_line=dma((2, 2, levels)),
        f_recv=dma((len(f_batches), 5)),
        o_send=dma((5,)),
        o_recv=dma((len(o_batches), 5)),
        q_send=dma((3, 5)),
        q_recv=dma((3, len(q_batches), 5)),
    )
    for name, flat in (("att_", att), ("ffn_", ffn)):
        half = (flat.parts, flat.deep // 2, D)
        own = dict(
            long=vmem((flat.halo + flat.held + 8, 128), f32),
            halo=vmem((flat.tail + flat.halo + 8, 128), f32),
            line=vmem((flat.lines + flat.halo + 8, 128), f32),
            own=vmem((2, *half), f32),
            send=dma((5,)),
            recv=dma((chips,)),
            sib=dma,
            plane_send=dma((5,)),
            plane_recv=dma((levels + 2,)),
            plane_sib=dma,
            halo_send=dma,
            halo_recv=dma,
            own_send=dma,
            own_recv=dma,
            back_send=dma,
            back_recv=dma,
        )
        shapes.update({name + key: shape for key, shape in own.items()})
    return shapes


def layer_kernel(names, levels, att, ffn, seqs, length, masters_in, tok_in, cot_in, segs, live_count,
                 out_out, gin_out, att_out, ffn_out, *scratch):
    s = types.SimpleNamespace(**dict(zip(names, scratch)))
    act_first = s.act.shape[0] // 4
    refs = dict(vars(s), segs=segs, live_count=live_count)
    refs.update(cot=s.tok, out=s.tok, down=s.ctx, tok_t=s.low_t)
    refs.update(bias=s.hat.at[:, pl.ds(0, length)], gin=s.tok, act_first=act_first)
    work = Layer(refs, att.split, ffn.split, seqs, length)

    def local(src, dst, at):
        copy = pltpu.make_async_copy(src, dst, s.local_sem.at[at])
        copy.start()
        return copy

    p = Place(levels)
    get_a = local(masters_in.at[pl.ds(0, att.held), :], s.att_long.at[pl.ds(att.halo, att.held), :], 0)
    get_f = local(masters_in.at[pl.ds(att.held, ffn.held), :], s.ffn_long.at[pl.ds(ffn.halo, ffn.held), :], 1)
    get_t = local(tok_in, s.tok, 2)
    p.meet()
    sends = Sends()
    lead_a = Lead(p, sends, att, s.att_long, s.att_halo, s.att_line, s.att_halo_send, s.att_halo_recv)
    lead_f = Lead(p, sends, ffn, s.ffn_long, s.ffn_halo, s.ffn_line, s.ffn_halo_send, s.ffn_halo_recv)
    get_a.wait()
    sends.go(lead_a.begin)
    get_f.wait()
    sends.go(lead_f.begin)
    lead_a.lines()
    lead_a.store(s.att_w)
    def gathers(ref, cut, *sems):
        parts, lanes = ref.shape[1], pl.ds(0, D)
        if cut[0]:
            first, last = (pl.ds(0, parts - cut[0]), lanes), (pl.ds(parts - cut[0], cut[0]), lanes)
        else:
            first = (pl.ds(0, parts), pl.ds(0, D - cut[1]))
            last = (pl.ds(0, parts), pl.ds(D - cut[1], cut[1]))
        go, plane = Gather(p, ref, *first, *sems[:3]), Plane(p, ref, *last, *sems[3:])
        return go, plane

    go_a = gathers(
        s.att_w, (0, 128), s.att_send, s.att_recv, s.att_sib, s.att_plane_send, s.att_plane_recv, s.att_plane_sib
    )
    go_f = gathers(
        s.ffn_w, (1, 0), s.ffn_send, s.ffn_recv, s.ffn_sib, s.ffn_plane_send, s.ffn_plane_recv, s.ffn_plane_sib
    )
    (a, a_plane), (f, f_plane) = go_a, go_f
    a.own()
    a_plane.own()

    def last():
        terms, spare = s.terms, s.spare
        terms[...] = jnp.zeros(terms.shape, terms.dtype)
        for lead, at, count in ((lead_a, 0, 5), (lead_f, 8, 7)):
            rows = lead.last_rows(count)
            spare[pl.ds(0, rows.shape[0]), :] = rows
            for block in range(D // 128):
                terms[pl.ds(at, count), pl.ds(128 * block, 128)] = spare[pl.ds(block, count, stride=6), :]

    pl.when(p.d == att.chips - 1)(last)
    lead_f.lines()
    lead_f.store(s.ffn_w)
    s.term_grads[...] = jnp.zeros(s.term_grads.shape, jnp.float32)
    a.line(1)
    a.over_a(0)
    a_plane.near()
    a.line(2)
    a.over_b(0)
    a_plane.complete()
    a.over_a(1)
    a.line(3)
    f_plane.own()
    a.over_a(2)
    f.own()
    a_plane.line(1)
    a.over_b(1)
    a.over_b(2)
    a.over_a(3)
    f_plane.near()
    a_plane.line(2)
    f.line(1)
    a.over_b(3)
    a_plane.line(3)
    sends.go(Spread(p, sends, s.terms, s.term_send, s.term_recv).run)
    for go in go_a:
        go.from_sibling()
    get_t.wait()

    on = functools.partial
    work.qkv(((2, on(f.over_a, 0)), (2, on(f.line, 2)), (2, f_plane.complete),))
    work.attend(
        (
            (3, on(f.over_a, 1)),
            (3, on(f.line, 3)),
            (6, on(f_plane.line, 1)),
            (8, on(f.over_a, 2)),
            (9, on(f.over_b, 0)),
            (10, on(f_plane.line, 2)),
            (10, on(f.over_b, 1)),
            (10, on(f.over_a, 3)),
        )
    )
    work.first_norm()
    f.over_b(2)
    f_plane.line(3)
    f.over_b(3)

    get_c = local(cot_in, s.tok, 2)
    for go in go_f:
        go.from_sibling()
    get_c.wait()
    work.feed()
    put_o = local(s.tok, out_out, 3)
    sends.finish()
    for go in (*go_a, *go_f):
        go.finish()

    sums = Sends()
    slots, slope, act = s.ffn_slots, s.slope, s.act
    half_a, half_f = att.deep // 2, ffn.deep // 2

    def of(ref, half):
        return lambda chip, core: ref.at[chip, :, tile(core, half), :]

    def att_slots(lanes):
        return lambda i, count: slope.at[pl.ds(3 * i, 3 * count), :, lanes]

    f_batches, i_batches, o_batches, q_batches = batches(levels)
    everything = pl.ds(0, D)
    ffn_slots = lambda i, count: slots.at[i] if count == 1 else slots.at[pl.ds(i, count)]
    add_f = Chain(
        s.ffn_extra, s.f_line, p, 4, ffn.chips, f_batches, of(s.ffn_w, half_f), ffn_slots,
        lambda core: s.ffn_own.at[core], s.f_send, s.f_recv,
    )
    add_i = []
    for group in range(2):
        parts = pl.ds(2 * group, 2)
        own_chips = pl.ds(0, ffn.split)
        whole = (s.ffn_w.at[own_chips, parts, tile(1 - p.c, half_f), :], slots.at[own_chips, parts])
        add_i.append(
            Chain(
                s.ffn_extra.at[parts], s.i_line.at[group], p, 2, ffn.chips, i_batches,
                lambda chip, core, parts=parts: s.ffn_w.at[chip, parts, tile(core, half_f), :],
                lambda i, count, parts=parts: slots.at[i, parts] if count == 1 else slots.at[pl.ds(i, count), parts],
                lambda core, parts=parts: s.ffn_own.at[core, parts], s.i_send.at[group], s.i_recv.at[group], whole,
            )
        )
    add_o = Reduce(
        p, 3, att.chips, o_batches, of(s.att_w, half_a), att_slots(everything),
        lambda core: s.att_own.at[core], s.o_send, s.o_recv,
    )
    add_q = []
    for group in range(3):
        lanes = pl.ds(256 * group, 256)
        blocks = pl.ds(act_first, 3 * att.split)
        view = lambda chip, core, lanes=lanes: act.at[pl.ds(act_first + 3 * chip, 3), tile(core, half_a), lanes]
        whole = (act.at[blocks, tile(1 - p.c, half_a), lanes], slope.at[pl.ds(0, 3 * att.split), :, lanes])
        add_q.append(
            Reduce(
                p, 3, att.chips, q_batches, view, att_slots(lanes),
                lambda core, lanes=lanes: s.att_own.at[core, :, :, lanes], s.q_send.at[group], s.q_recv.at[group], whole,
            )
        )
    add_t = Terms(p, sums, s.terms_sum, s.terms_got, s.terms_all, s.sum_send, s.sum_recv)

    def do(act, *at):
        return sums.later(functools.partial(act, *at))

    q = add_q
    work.hidden_back(0)
    work.down_grads(0)
    work.hidden_back(1)
    work.down_grads(1)
    add_f.share(0)
    put_o.wait()
    get_t = local(tok_in, s.tok, 2)
    work.hidden_back(2)
    work.down_grads(2, (
            (2, on(add_f.over_b, 0)),
        ))
    work.hidden_back(3)
    work.down_grads(3)
    add_f.share(1)
    work.in_back(0)
    work.in_grads(0, (
            (2, on(add_f.over_b, 1)),
        ))
    work.in_back(1)
    work.in_grads(1)
    add_i[0].share(0)
    work.in_back(2)
    work.in_grads(2, (
            (1, on(add_f.over_a, 0)),
        ))
    work.in_back(3, (
            (0, on(add_f.over_a, 1)),
        ))
    work.in_grads(3)
    add_i[1].share(0)

    line = [(p.turn(distance), p.c) for distance in range(1, levels)]
    for device in (p.sibling, p.across_a, p.across_b, *line):
        pl.semaphore_signal(s.free, inc=1, device_id=device, device_id_type=MESH_ID)
    get_t.wait()
    work.first_back((
            (0, on(add_i[0].over_b, 0)),
            (3, on(add_f.collect, 1)),
        ))
    work.out_grads((
            (1, on(add_i[1].over_b, 0)),
            (2, on(add_f.line, 3, 1)),
        ))
    pl.semaphore_wait(s.free, 2 + levels)
    add_o.share(0)
    work.make_bias()
    work.attend_back(0, (
            (1, on(add_f.collect, 0)),
            (2, on(add_f.line, 2, 0)),
            (2, on(add_i[0].over_a, 0)),
        ))
    work.qkv_grads(0)
    q[0].share(0)
    work.attend_back(1, (
            (0, on(add_f.line, 2, 1)),
            (0, on(add_f.line, 1, 0)),
            (0, on(add_i[1].over_a, 0)),
            (2, on(q[0].over_b, 0)),
            (3, on(add_i[0].collect, 0)),
            (3, on(add_o.over_b, 0)),
            (3, on(add_i[0].line, 3, 0)),
        ))
    work.qkv_grads(1)
    q[1].share(0)
    q[1].over_b(0)
    add_i[1].collect(0)
    add_i[0].line(2, 0)
    q[0].over_a(0)
    work.attend_back(2, (
            (1, on(add_o.over_a, 0)),
            (1, on(add_i[1].line, 3, 0)),
            (1, on(add_i[0].line, 1, 0)),
            (2, on(q[0].collect, 0)),
            (2, on(q[0].line, 0)),
            (3, on(add_f.line, 1, 1)),
        ))
    work.qkv_grads(2)
    q[2].share(0)
    for core in range(2):
        s.terms_sum[core] = s.term_grads[:, pl.ds(D // 2 * core, D // 2)]
    do(add_t.share)()
    trail_f = Trail(p, sums, ffn, s.ffn_own, s.ffn_line, s.ffn_long, s.ffn_back_send, s.ffn_back_recv)
    trail_a = Trail(p, sums, att, s.att_own, s.att_line, s.att_long, s.att_back_send, s.att_back_recv, s.more_send)
    given_f = lambda core: handed(p, s.ffn_own, core, s.ffn_own_send, s.ffn_own_recv)
    given_a = lambda core: handed(p, s.att_own, core, s.att_own_send, s.att_own_recv)
    add_o.collect(0)
    add_i[1].line(2, 0)
    add_o.line(0)
    q[1].over_a(0)
    work.input_back((
            (0, on(q[2].over_b, 0)),
            (0, on(add_i[1].line, 1, 0)),
            (0, on(q[1].collect, 0)),
            (0, do(add_t.over_b)),
            (2, on(q[2].over_a, 0)),
            (2, on(q[1].line, 0)),
            (2, do(add_t.over_a)),
            (3, on(q[2].collect, 0)),
            (3, do(add_t.line)),
        ))
    put_g = local(work.gin, gin_out, 4)
    add_f.keep()
    q[0].keep()
    add_i[0].keep()
    q[2].line(0)
    add_i[1].keep()
    sums.go(lambda: sums.start(None, lambda: given_f(p.c)))
    add_o.keep()
    q[1].keep()
    given_f(1 - p.c).wait_recv()
    trail_f.lines()
    sums.go(trail_f.pass_back)
    q[2].keep()
    sums.go(lambda: sums.start(None, lambda: given_a(p.c)))
    trail_a.half_lines(0, p.c == 0)
    sums.go(trail_a.early_back)
    trail_a.half_lines(1, p.c == 1)
    do(add_t.hand_over)()
    given_a(1 - p.c).wait_recv()
    trail_a.half_lines(1, p.c == 0)
    trail_a.half_lines(0, p.c == 1)
    final = p.d == att.chips - 1

    def terms_here():
        add_t.take_over()
        trail_f.last_rows(s.terms_all, 8, 7)
        trail_a.last_rows(s.terms_all, 0, 5)

    pl.when(final)(terms_here)
    trail_f.out()
    put_f = local(s.ffn_long.at[pl.ds(0, ffn.held), :], ffn_out, 1)
    trail_a.out()
    put_a = local(s.att_long.at[pl.ds(0, att.held), :], att_out, 0)
    sums.finish()
    for who in (add_f, *add_i, add_o, *q):
        who.finish()
    for copy in (put_g, put_f, put_a):
        copy.wait()


def run_layer(levels, att, ffn, masters, tokens, cotangent, segments, live_count):
    vmem = pl.BlockSpec(memory_space=pltpu.VMEM)
    anywhere = pl.BlockSpec(memory_space=pl.ANY)
    seqs, length = segments.shape
    rows = tokens.shape[0]
    bf16, f32 = jnp.bfloat16, jnp.float32
    shape = jax.ShapeDtypeStruct
    scratch = scratch_shapes(levels, att, ffn, rows, seqs, length)
    return pl.pallas_call(
        functools.partial(layer_kernel, tuple(scratch), levels, att, ffn, seqs, length),
        out_shape=(
            shape(tokens.shape, bf16),
            shape(tokens.shape, bf16),
            shape((att.held, 128), f32),
            shape((ffn.held, 128), f32),
        ),
        in_specs=[anywhere, anywhere, anywhere, vmem, pl.BlockSpec(memory_space=pltpu.SMEM)],
        out_specs=(anywhere, anywhere, anywhere, anywhere),
        scratch_shapes=list(scratch.values()),
        compiler_params=pltpu.CompilerParams(
            collective_id=1, has_side_effects=True, vmem_limit_bytes=64 * 2**20
        ),
        name="layer",
    )(masters, tokens, cotangent, segments, live_count)


def as_lines(flat, vector):
    return jnp.pad(vector, (0, flat.held * 128 - flat.length)).reshape(flat.held, 128)


def fast_body(
    levels,
    tokens,
    cotangent,
    segments,
    live_count,
    att_master,
    att_first,
    att_second,
    ffn_master,
    ffn_first,
    ffn_second,
):
    chips = lax.axis_size("dp")
    att = Flat(att_master.shape[0], chips, 3, 3 * chips // 4, False)
    ffn = Flat(ffn_master.shape[0], chips, 4, chips // 2, True)
    output, input_grad, att_sum, ffn_sum = run_layer(
        levels,
        att,
        ffn,
        jnp.concatenate([as_lines(att, att_master), as_lines(ffn, ffn_master)]),
        tokens,
        cotangent,
        segments,
        live_count,
    )
    att_grad = att_sum.reshape(-1)[: att.length]
    ffn_grad = ffn_sum.reshape(-1)[: ffn.length]
    att_new = adam_update(att_master, att_first, att_second, att_grad)
    ffn_new = adam_update(ffn_master, ffn_first, ffn_second, ffn_grad)
    return (output, input_grad, att_grad, *att_new, ffn_grad, *ffn_new)


def body_for(mesh):
    chips, cores = mesh.shape["dp"], mesh.shape["rep"]
    if chips == 16 and cores == 2:
        return functools.partial(fast_body, chips // 4)
    return general_body


def solution(mesh):
    placed = (
        P(("dp", "rep"), None),
        P(("dp", "rep"), None),
        P(("dp", "rep"), None),
        P(("dp", "rep")),
        P("dp"),
        P("dp"),
        P("dp"),
        P("dp"),
        P("dp"),
        P("dp"),
    )
    return jax.shard_map(
        body_for(mesh),
        mesh=mesh,
        in_specs=placed,
        out_specs=(
            P(("dp", "rep"), None),
            P(("dp", "rep"), None),
            P("dp"),
            P("dp"),
            P("dp"),
            P("dp"),
            P("dp"),
            P("dp"),
            P("dp"),
            P("dp"),
        ),
        check_vma=False,
    )
```

```python
import functools
import math
import types

import jax
import jax.numpy as jnp
from jax import lax
from jax.experimental import pallas as pl
from jax.experimental.pallas import tpu as pltpu
from jax.sharding import PartitionSpec as P

D = 768
HEADS = 12
HEAD_DIM = 64
FF = 3072
STEP = 10


norm_eps = 1e-05
beta_one = 0.9
beta_two = 0.98
decay = 0.01
adam_eps = 1e-08
masked = -1e30


def split_attention(flat_params):
    qkv_weight = flat_params[: 3 * D * D].reshape(D, 3 * D)
    offset = 3 * D * D
    out_weight = flat_params[offset : offset + D * D].reshape(D, D)
    offset = offset + D * D
    att_terms = flat_params[offset : offset + 5 * D].reshape(5, D).astype(jnp.float32)
    return (qkv_weight, out_weight, att_terms)


def split_ffn(flat_params):
    in_weight = flat_params[: D * FF].reshape(D, FF)
    offset = D * FF
    down_weight = flat_params[offset : offset + FF * D].reshape(FF, D)
    offset = offset + FF * D
    in_bias = flat_params[offset : offset + FF].astype(jnp.float32)
    offset = offset + FF
    ffn_terms = flat_params[offset : offset + 3 * D].reshape(3, D).astype(jnp.float32)
    return (in_weight, down_weight, in_bias, ffn_terms)


def normalize(values, gain, shift):
    row_mean = jnp.mean(values, -1, keepdims=True)
    centred = values - row_mean
    rstd_rows = lax.rsqrt(jnp.mean(centred * centred, -1, keepdims=True) + norm_eps)
    normed = centred * rstd_rows
    return (normed * gain + shift, normed, rstd_rows)


def norm_back(grad_in, normed, rstd_rows, gain):
    scaled = grad_in * gain
    grad_rows = rstd_rows * (
        scaled
        - jnp.mean(scaled, -1, keepdims=True)
        - normed * jnp.mean(scaled * normed, -1, keepdims=True)
    )
    return (grad_rows, jnp.sum(grad_in * normed, 0), jnp.sum(grad_in, 0))


def gelu_slope(values):
    normal_cdf = 0.5 * (1.0 + lax.erf(values * 0.5**0.5))
    return normal_cdf + values * jnp.exp(-0.5 * values * values) * (2.0 * math.pi) ** (-0.5)


def masked_scores(query_rows, key_rows, seg_ids):
    scores = jnp.einsum(
        "qhd,khd->hqk", query_rows, key_rows, preferred_element_type=jnp.float32
    ) * HEAD_DIM ** (-0.5)
    same_doc = seg_ids[:, None] == seg_ids[None, :]
    return jnp.where(same_doc[None], scores, masked)


def attend_forward(block):
    query_rows, key_rows, value_rows, seg_ids = block
    scores = masked_scores(query_rows, key_rows, seg_ids)
    row_top = jnp.max(scores, -1, keepdims=True)
    raised = jnp.exp(scores - row_top)
    row_total = jnp.sum(raised, -1, keepdims=True)
    soft_probs = (raised / row_total).astype(jnp.bfloat16)
    context = jnp.einsum("hqk,khd->qhd", soft_probs, value_rows, preferred_element_type=jnp.float32)
    return (
        context.astype(jnp.bfloat16).reshape(context.shape[0], -1),
        row_top + jnp.log(row_total),
    )


def attend_backward(query_rows, key_rows, value_rows, seg_ids, log_total, grad_context):
    soft_probs = jnp.exp(masked_scores(query_rows, key_rows, seg_ids) - log_total)
    grad_probs = jnp.einsum(
        "qhd,khd->hqk", grad_context, value_rows, preferred_element_type=jnp.float32
    )
    grad_values = jnp.einsum(
        "hqk,qhd->khd",
        soft_probs.astype(jnp.bfloat16),
        grad_context,
        preferred_element_type=jnp.float32,
    )
    grad_scores = soft_probs * (grad_probs - jnp.sum(soft_probs * grad_probs, -1, keepdims=True))
    grad_scores = grad_scores.astype(jnp.bfloat16)
    grad_queries = jnp.einsum(
        "hqk,khd->qhd", grad_scores, key_rows, preferred_element_type=jnp.float32
    ) * HEAD_DIM ** (-0.5)
    grad_keys = jnp.einsum(
        "hqk,qhd->khd", grad_scores, query_rows, preferred_element_type=jnp.float32
    ) * HEAD_DIM ** (-0.5)
    length_here = query_rows.shape[0]
    return jnp.concatenate(
        [
            grad_queries.reshape(length_here, -1),
            grad_keys.reshape(length_here, -1),
            grad_values.reshape(length_here, -1),
        ],
        -1,
    )


def adam_update(master, first, second, grad):
    first_new = beta_one * first + (1.0 - beta_one) * grad
    second_new = beta_two * second + (1.0 - beta_two) * grad * grad
    fix_one = 1.0 - beta_one**STEP
    fix_two = 1.0 - beta_two**STEP
    update = first_new / fix_one / (jnp.sqrt(second_new / fix_two) + adam_eps)
    return (first_new, second_new, update + decay * master)


def general_body(
    tokens,
    cotangent,
    segments,
    live_count,
    att_master,
    att_first,
    att_second,
    ffn_master,
    ffn_first,
    ffn_second,
):
    seq_count = segments.shape[0]
    length = segments.shape[1]
    att_full = lax.all_gather(att_master.astype(jnp.bfloat16), "dp", axis=0, tiled=True)
    qkv_weight, out_weight, att_terms = split_attention(att_full)
    bias_qkv = jnp.concatenate([att_terms[0], jnp.zeros_like(att_terms[0]), att_terms[1]])
    qkv = (jnp.dot(tokens, qkv_weight, preferred_element_type=jnp.float32) + bias_qkv).astype(
        jnp.bfloat16
    )
    head_split = qkv.reshape(seq_count, length, 3, HEADS, HEAD_DIM)
    context, log_total = lax.map(
        attend_forward, (head_split[:, :, 0], head_split[:, :, 1], head_split[:, :, 2], segments)
    )
    context = context.reshape(-1, D)
    residual = (
        tokens.astype(jnp.float32)
        + jnp.dot(context, out_weight, preferred_element_type=jnp.float32)
        + att_terms[2]
    )
    first_out, first_hat, first_rstd = normalize(residual, att_terms[3], att_terms[4])
    ffn_full = lax.all_gather(ffn_master.astype(jnp.bfloat16), "dp", axis=0, tiled=True)
    in_weight, down_weight, in_bias, ffn_terms = split_ffn(ffn_full)
    first_low = first_out.astype(jnp.bfloat16)
    ffn_inner = jnp.dot(first_low, in_weight, preferred_element_type=jnp.float32) + in_bias
    ffn_act = jax.nn.gelu(ffn_inner, approximate=False).astype(jnp.bfloat16)
    second_in = (
        first_out + jnp.dot(ffn_act, down_weight, preferred_element_type=jnp.float32) + ffn_terms[0]
    )
    output, second_hat, second_rstd = normalize(second_in, ffn_terms[1], ffn_terms[2])
    att_back = lax.all_gather(att_master.astype(jnp.bfloat16), "dp", axis=0, tiled=True)
    qkv_weight, out_weight, att_terms = split_attention(att_back)
    ffn_back = lax.all_gather(ffn_master.astype(jnp.bfloat16), "dp", axis=0, tiled=True)
    in_weight, down_weight, in_bias, ffn_terms = split_ffn(ffn_back)

    def microbatch(micro_index, state_now):
        grad_sums, input_grads = state_now

        def take_rows(array_in):
            return lax.dynamic_slice_in_dim(array_in, micro_index * length, length, 0)

        grad_out = take_rows(cotangent).astype(jnp.float32)
        grad_second, grad_gain_two, grad_shift_two = norm_back(
            grad_out, take_rows(second_hat), take_rows(second_rstd), ffn_terms[1]
        )
        grad_down = grad_second.astype(jnp.bfloat16)
        grad_down_bias = jnp.sum(grad_down.astype(jnp.float32), 0)
        grad_down_weight = jnp.dot(
            take_rows(ffn_act).T, grad_down, preferred_element_type=jnp.float32
        )
        grad_act = jnp.dot(grad_down, down_weight.T, preferred_element_type=jnp.float32)
        grad_inner = (grad_act * gelu_slope(take_rows(ffn_inner))).astype(jnp.bfloat16)
        grad_in_bias = jnp.sum(grad_inner.astype(jnp.float32), 0)
        grad_in_weight = jnp.dot(
            take_rows(first_low).T, grad_inner, preferred_element_type=jnp.float32
        )
        grad_first = grad_second + jnp.dot(
            grad_inner, in_weight.T, preferred_element_type=jnp.float32
        )
        grad_residual, grad_gain_one, grad_shift_one = norm_back(
            grad_first, take_rows(first_hat), take_rows(first_rstd), att_terms[3]
        )
        grad_proj = grad_residual.astype(jnp.bfloat16)
        grad_out_bias = jnp.sum(grad_proj.astype(jnp.float32), 0)
        grad_out_weight = jnp.dot(
            take_rows(context).T, grad_proj, preferred_element_type=jnp.float32
        )
        grad_context = jnp.dot(grad_proj, out_weight.T, preferred_element_type=jnp.float32).astype(
            jnp.bfloat16
        )
        this_seq = lax.dynamic_index_in_dim(head_split, micro_index, 0, keepdims=False)
        this_segs = lax.dynamic_index_in_dim(segments, micro_index, 0, keepdims=False)
        this_total = lax.dynamic_index_in_dim(log_total, micro_index, 0, keepdims=False)
        grad_qkv = attend_backward(
            this_seq[:, 0],
            this_seq[:, 1],
            this_seq[:, 2],
            this_segs,
            this_total,
            grad_context.reshape(length, HEADS, HEAD_DIM),
        )
        grad_qkv = grad_qkv.astype(jnp.bfloat16)
        grad_wide = grad_qkv.astype(jnp.float32)
        grad_query_bias = jnp.sum(grad_wide[:, :D], 0)
        grad_value_bias = jnp.sum(grad_wide[:, 2 * D :], 0)
        grad_qkv_weight = jnp.dot(take_rows(tokens).T, grad_qkv, preferred_element_type=jnp.float32)
        grad_tokens = (
            jnp.dot(grad_qkv, qkv_weight.T, preferred_element_type=jnp.float32) + grad_residual
        )
        input_grads = lax.dynamic_update_slice_in_dim(
            input_grads, grad_tokens.astype(jnp.bfloat16), micro_index * length, 0
        )
        terms_now = (
            grad_qkv_weight,
            grad_out_weight,
            grad_query_bias,
            grad_value_bias,
            grad_out_bias,
            grad_gain_one,
            grad_shift_one,
            grad_in_weight,
            grad_down_weight,
            grad_in_bias,
            grad_down_bias,
            grad_gain_two,
            grad_shift_two,
        )
        grad_sums = tuple((running + fresh for running, fresh in zip(grad_sums, terms_now)))
        return (grad_sums, input_grads)

    zero_sums = (
        jnp.zeros((D, 3 * D), jnp.float32),
        jnp.zeros((D, D), jnp.float32),
        jnp.zeros((D,), jnp.float32),
        jnp.zeros((D,), jnp.float32),
        jnp.zeros((D,), jnp.float32),
        jnp.zeros((D,), jnp.float32),
        jnp.zeros((D,), jnp.float32),
        jnp.zeros((D, FF), jnp.float32),
        jnp.zeros((FF, D), jnp.float32),
        jnp.zeros((FF,), jnp.float32),
        jnp.zeros((D,), jnp.float32),
        jnp.zeros((D,), jnp.float32),
        jnp.zeros((D,), jnp.float32),
    )
    zero_inputs = jnp.zeros(tokens.shape, jnp.bfloat16)
    grad_sums, input_grad = lax.fori_loop(0, live_count[0], microbatch, (zero_sums, zero_inputs))
    dp_count = lax.axis_size("dp")
    att_pad = att_master.shape[0] * dp_count - 4 * D * D - 5 * D
    ffn_pad = ffn_master.shape[0] * dp_count - 2 * D * FF - FF - 3 * D
    att_local = jnp.concatenate(
        [
            grad_sums[0].reshape(-1),
            grad_sums[1].reshape(-1),
            grad_sums[2],
            grad_sums[3],
            grad_sums[4],
            grad_sums[5],
            grad_sums[6],
            jnp.zeros((att_pad,), jnp.float32),
        ]
    )
    ffn_local = jnp.concatenate(
        [
            grad_sums[7].reshape(-1),
            grad_sums[8].reshape(-1),
            grad_sums[9],
            grad_sums[10],
            grad_sums[11],
            grad_sums[12],
            jnp.zeros((ffn_pad,), jnp.float32),
        ]
    )
    att_rows, ffn_rows = (
        lax.all_to_all(
            att_local.reshape(dp_count, -1).astype(jnp.bfloat16),
            "dp",
            split_axis=0,
            concat_axis=0,
            tiled=True,
        ).astype(jnp.float32),
        lax.all_to_all(
            ffn_local.reshape(dp_count, -1).astype(jnp.bfloat16),
            "dp",
            split_axis=0,
            concat_axis=0,
            tiled=True,
        ).astype(jnp.float32),
    )
    att_share = jnp.sum(att_rows, 0)
    ffn_share = jnp.sum(ffn_rows, 0)
    att_grad, ffn_grad = (
        lax.psum(att_share.astype(jnp.bfloat16), "rep").astype(jnp.float32),
        lax.psum(ffn_share.astype(jnp.bfloat16), "rep").astype(jnp.float32),
    )
    att_new = adam_update(att_master, att_first, att_second, att_grad)
    ffn_new = adam_update(ffn_master, ffn_first, ffn_second, ffn_grad)
    return (
        output.astype(jnp.bfloat16),
        input_grad,
        att_grad,
        att_new[0],
        att_new[1],
        att_new[2],
        ffn_grad,
        ffn_new[0],
        ffn_new[1],
        ffn_new[2],
    )


MESH_ID = pl.DeviceIdType.MESH


def when(cond, act):
    if cond is None:
        act()
    else:
        pl.when(cond)(act)


class Place:
    def __init__(self, levels):
        self.levels = levels
        d = lax.axis_index("dp")
        c = lax.axis_index("rep")
        self.d, self.c = d, c
        self.z, y, x = d // 4, (d // 2) % 2, d % 2
        x_near, y_near = d + 1 - 2 * x, d + 2 - 4 * y
        self.a_near = x_near + c * (y_near - x_near)
        self.b_near = y_near + c * (x_near - y_near)
        self.far = x_near + y_near - d
        self.a_at = x + c * (y - x)
        self.b_at = y + c * (x - y)
        self.up = (d + 4, c)
        self.down = (d - 4, c)
        self.has_up = self.z < levels - 1
        self.has_down = self.z > 0
        self.across_a = (self.a_near, c)
        self.across_b = (self.b_near, c)
        self.sibling = (d, 1 - c)

    def levels_at(self, distance):
        if distance == 0:
            return [(self.z, None, 0)]
        return [
            (self.z - distance, self.z >= distance, -1),
            (self.z + distance, self.z + distance < self.levels, 1),
        ]

    def at(self, column, level):
        return column + 4 * (level - self.z)

    def turn(self, distance):
        return self.at(self.d, (self.z + distance) % self.levels)

    def along(self, step):
        return (self.up, self.has_up) if step > 0 else (self.down, self.has_down)

    def meet(self):
        barrier = pltpu.get_barrier_semaphore()

        def greet(device):
            pl.semaphore_signal(barrier, inc=1, device_id=device, device_id_type=MESH_ID)

        for device in (self.across_a, self.across_b, self.sibling):
            greet(device)
        count = 3
        for distance in range(1, self.levels):
            greet((self.turn(distance), self.c))
            count += 1
        after, before = self.d < 4 * self.levels - 1, self.d > 0
        edges = [((self.d + 1, self.c), after), ((self.d - 1, self.c), before)]
        edges += [((self.d + 1, 0), after & (self.c == 1)), ((self.d - 1, 1), before & (self.c == 0))]
        for device, there in edges:
            pl.when(there)(functools.partial(greet, device))
            count = count + there.astype(jnp.int32)
        pl.semaphore_wait(barrier, count)


def both(first, second):
    if first is None:
        return second
    return first if second is None else first & second


class Sends:
    def __init__(self):
        self.steps, self.closing = [], False

    def go(self, step):
        if not any(step is other for other in self.steps):
            self.steps.append(step)
        step()

    def later(self, step):
        return lambda: self.go(step)

    def start(self, cond, make):
        when(cond, lambda: make().wait_send() if self.closing else make().start())

    def wait(self, cond, make):
        if not self.closing:
            when(cond, lambda: make().wait_recv())

    def finish(self):
        self.closing = True
        for step in self.steps:
            step()


def remote(src, dst, send_sem, recv_sem, device):
    return pltpu.make_async_remote_copy(
        src_ref=src,
        dst_ref=dst,
        send_sem=send_sem,
        recv_sem=recv_sem,
        device_id=device,
        device_id_type=MESH_ID,
    )


class Gather:
    def __init__(self, place, ref, parts, lanes, send_sem, recv_sem, sib_sem):
        self.place, self.ref, self.parts, self.lanes = place, ref, parts, lanes
        self.send_sem, self.recv_sem, self.sib_sem = send_sem, recv_sem, sib_sem
        self.half = ref.shape[2] // 2
        levels = place.levels
        self.leave = {2: levels, 3: 2 * levels, 4: 4 * levels - 1}
        self.together = 1

    def rows(self, core):
        return pl.ds(pl.multiple_of(core * self.half, self.half), self.half)

    def piece(self, chip, core):
        return self.ref.at[chip, self.parts, self.rows(core), self.lanes]

    def several(self, count):
        return self.ref.at[pl.ds(0, count), self.parts, pl.ds(0, self.half), self.lanes]

    def send(self, cond, chip, way, device):
        own = self.piece(chip, self.place.c)
        recv = self.sib_sem if way == 4 else self.recv_sem.at[chip]
        when(cond, lambda: remote(own, own, self.send_sem.at[way], recv, device).start())

    def wait(self, cond, part, sem):
        when(cond, lambda: remote(part, part, self.send_sem.at[0], sem, self.place.sibling).wait_recv())

    def arrived(self, cond, chip):
        self.wait(cond, self.piece(chip, self.place.c), self.recv_sem.at[chip])

    def own(self):
        p = self.place
        self.send(p.has_up, p.d, 0, p.up)
        self.send(p.has_down, p.d, 1, p.down)
        self.send(None, p.d, 3, p.across_b)
        self.send(None, p.d, 2, p.across_a)

    def line(self, distance):
        p = self.place
        for level, there, step in p.levels_at(distance):
            chip = p.at(p.d, level)
            self.arrived(there, chip)
            onward, more = p.along(-step)
            self.send(both(there, more), chip, 0 if step < 0 else 1, onward)
            self.send(there, chip, 3, p.across_b)
            self.send(there, chip, 2, p.across_a)
            self.send(there, chip, 4, p.sibling)

    def over_a(self, distance):
        p = self.place
        for level, there, _ in p.levels_at(distance):
            chip = p.at(p.a_near, level)
            self.arrived(there, chip)
            self.send(there, chip, 3, p.across_b)
            self.send(there, chip, 4, p.sibling)

    def over_b(self, distance):
        p = self.place
        for column in (p.b_near, p.far):
            for level, there, _ in p.levels_at(distance):
                chip = p.at(column, level)
                self.arrived(there, chip)
                self.send(there, chip, 4, p.sibling)

    def from_sibling(self):
        self.wait(None, self.several(4 * self.place.levels - 1), self.sib_sem)

    def left(self, cond, way, count):
        part = self.several(count)
        sem = self.send_sem.at[way]
        when(cond, lambda: remote(part, part, sem, self.sib_sem, self.place.sibling).wait_send())

    def finish(self):
        p = self.place
        for way, count in self.leave.items():
            self.left(None, way, count)
        for level in range(p.levels):
            if level < p.levels - 1:
                self.left(p.z == level, 0, self.together * (level + 1))
            if level > 0:
                self.left(p.z == level, 1, self.together * (p.levels - level))


class Plane(Gather):
    def __init__(self, place, ref, parts, lanes, send_sem, recv_sem, sib_sem):
        super().__init__(place, ref, parts, lanes, send_sem, recv_sem, sib_sem)
        self.leave = {2: 1, 3: 2, 4: 4 * place.levels - 1}
        self.together = 4
        self.from_a, self.from_b = place.levels, place.levels + 1

    def send(self, cond, chip, way, device):
        own = self.piece(chip, self.place.c)
        recv = self.sib_sem if way == 4 else self.recv_sem.at[self.from_a if way == 2 else self.from_b]
        when(cond, lambda: remote(own, own, self.send_sem.at[way], recv, device).start())

    def own(self):
        p = self.place
        self.send(None, p.d, 2, p.across_a)
        self.send(None, p.d, 3, p.across_b)

    def near(self):
        p = self.place
        self.wait(None, self.piece(p.a_near, p.c), self.recv_sem.at[self.from_a])
        self.send(None, p.a_near, 3, p.across_b)
        self.send(None, p.a_near, 4, p.sibling)

    def sheet(self, level):
        return self.ref.at[pl.ds(4 * level, 4), self.parts, self.rows(self.place.c), self.lanes]

    def send_sheet(self, cond, level, way, device):
        own = self.sheet(level)
        recv = self.sib_sem if way == 4 else self.recv_sem.at[level]
        when(cond, lambda: remote(own, own, self.send_sem.at[way], recv, device).start())

    def complete(self):
        p = self.place
        self.wait(None, self.several(2), self.recv_sem.at[self.from_b])
        self.send_sheet(p.has_up, p.z, 0, p.up)
        self.send_sheet(p.has_down, p.z, 1, p.down)
        for chip in (p.b_near, p.far):
            self.send(None, chip, 4, p.sibling)

    def line(self, distance):
        p = self.place
        for level, there, step in p.levels_at(distance):
            self.wait(there, self.sheet(level), self.recv_sem.at[level])
            onward, more = p.along(-step)
            self.send_sheet(both(there, more), level, 0 if step < 0 else 1, onward)
            self.send_sheet(there, level, 4, p.sibling)


class Spread:
    def __init__(self, place, sends, ref, send_sem, recv_sem):
        self.place, self.sends, self.ref = place, sends, ref
        self.send_sem, self.recv_sem = send_sem, recv_sem

    def copy(self, way, device):
        return remote(self.ref, self.ref, self.send_sem.at[way], self.recv_sem, device)

    def wait(self, cond):
        self.sends.wait(cond, lambda: self.copy(0, self.place.sibling))

    def run(self):
        p = self.place
        home = (p.a_at == 1) & (p.b_at == 1)
        self.wait(home & p.has_up)
        self.sends.start(home & p.has_down, lambda: self.copy(0, p.down))
        self.wait((p.a_at == 0) & (p.b_at == 1))
        self.sends.start(home, lambda: self.copy(1, p.across_a))
        self.wait(p.b_at == 0)
        self.sends.start(p.b_at == 1, lambda: self.copy(2, p.across_b))


def shifted(ref, start, rows):
    first, turn = start // 128, start % 128
    here = pltpu.roll(ref[pl.ds(first, rows), :], (128 - turn) % 128, 1)
    after = pltpu.roll(ref[pl.ds(first + 1, rows), :], (128 - turn) % 128, 1)
    lane = lax.broadcasted_iota(jnp.int32, (rows, 128), 1)
    return jnp.where(lane < 128 - turn, here, after)


class Flat:
    def __init__(self, length, chips, parts, split, turned):
        self.length, self.chips, self.parts, self.turned = length, chips, parts, turned
        self.rows = length // D // parts * parts
        self.slip = length - self.rows * D
        self.deep = self.rows // parts
        self.split = split
        self.lines = self.rows * (D // 128)
        self.most = self.slip * chips
        self.halo = -(-self.most // 1024) * 8
        self.held = -(-length // 1024) * 8
        self.tail_from = (length - self.most) // 1024 * 8
        self.tail = self.held - self.tail_from

    def place_of(self, part, block, split):
        if split:
            return 6 * part + block, 6 * self.parts
        return 6 * self.deep * part + block, 6


class Lead:
    def __init__(self, place, sends, flat, long_ref, halo_ref, line_ref, send_sem, recv_sem):
        self.place, self.sends, self.flat = place, sends, flat
        self.long_ref, self.halo_ref, self.line_ref = long_ref, halo_ref, line_ref
        self.send_sem, self.recv_sem = send_sem, recv_sem

    def copy(self):
        f, p = self.flat, self.place
        return remote(
            self.long_ref.at[pl.ds(f.halo + f.tail_from, f.tail), :],
            self.halo_ref.at[pl.ds(0, f.tail), :],
            self.send_sem,
            self.recv_sem,
            (p.d + 1, p.c),
        )

    def begin(self):
        self.sends.start(self.place.d < self.flat.chips - 1, self.copy)

    def lines(self):
        p, f = self.place, self.flat
        slip = f.slip * p.d
        self.line_ref[pl.ds(0, f.lines), :] = shifted(self.long_ref, f.halo * 128 - slip, f.lines)

    def join(self):
        p, f = self.place, self.flat
        slip = f.slip * p.d

        def mend():
            self.copy().wait_recv()
            before = shifted(self.halo_ref, f.length - f.tail_from * 128 - slip, f.halo)
            at = lax.broadcasted_iota(jnp.int32, (f.halo, 128), 0) * 128
            at = at + lax.broadcasted_iota(jnp.int32, (f.halo, 128), 1)
            self.line_ref[pl.ds(0, f.halo), :] = jnp.where(at < slip, before, self.line_ref[pl.ds(0, f.halo), :])

        pl.when(p.d > 0)(mend)

    def store(self, out_ref):
        p, f = self.place, self.flat

        def put(split):
            for part in range(f.parts):
                for block in range(D // 128):
                    first, stride = f.place_of(part, block, split)
                    out_ref[p.d, part, :, pl.ds(128 * block, 128)] = self.line_ref[
                        pl.ds(first, f.deep, stride=stride), :
                    ].astype(jnp.bfloat16)

        pl.when(p.d < f.split)(lambda: put(True))
        pl.when(p.d >= f.split)(lambda: put(False))

    def last_rows(self, count):
        f = self.flat
        lines = -(-count * 6 // 8) * 8
        return shifted(self.long_ref, f.halo * 128 + f.length - count * D, lines)


class Reduce:
    def __init__(self, place, parts, chips, batches, view, slots, kept, send_sem, recv_sem, whole=None):
        self.place, self.parts, self.batches = place, parts, batches
        self.view, self.slots, self.kept = view, slots, kept
        self.send_sem, self.recv_sem, self.whole = send_sem, recv_sem, whole
        self.levels = [level for batch in batches for level in batch]
        self.from_b, self.from_a = chips, chips + 2 * place.levels
        self.from_z = chips + 3 * place.levels

    def arrival(self, kind, batch):
        return self.recv_sem.at[batch, kind]

    def wait(self, part, sem):
        remote(part, part, self.send_sem.at[0], sem, self.place.sibling).wait_recv()

    def send(self, cond, chip, way, dst, recv, device):
        p = self.place
        src = self.view(chip, 1 - p.c if way == 4 else p.c)
        when(cond, lambda: remote(src, dst, self.send_sem.at[way], recv, device).start())

    def add(self, chip, src):
        here = self.view(chip, self.place.c)
        for part in range(self.parts):
            here[part] = here[part] + src[part]

    def share(self, batch):
        p = self.place
        recv = self.arrival(0, batch)
        if self.whole is not None:
            src, dst = self.whole
            remote(src, dst, self.send_sem.at[4], recv, p.sibling).start()
            return
        for level in self.batches[batch]:
            for column in (p.far, p.b_near, p.a_near, p.d):
                chip = p.at(column, level)
                self.send(None, chip, 4, self.slots(chip, 1), recv, p.sibling)

    def over_b(self, batch):
        p = self.place
        levels = self.batches[batch]
        self.wait(self.slots(4 * levels[0], 4 * len(levels)), self.arrival(0, batch))
        for kind, column in ((1, p.far), (0, p.b_near)):
            for level in levels:
                chip = p.at(column, level)
                self.add(chip, self.slots(chip, 1))
                dst = self.slots(self.from_b + p.levels * kind + level, 1)
                self.send(None, chip, 3, dst, self.arrival(1 + kind, batch), p.across_b)

    def over_a(self, batch):
        p = self.place
        levels = self.batches[batch]
        first = self.from_b + p.levels
        self.wait(self.slots(first + levels[0], len(levels)), self.arrival(2, batch))
        for level in levels:
            chip = p.at(p.a_near, level)
            self.add(chip, self.slots(chip, 1))
            self.add(chip, self.slots(first + level, 1))
            self.send(None, chip, 2, self.slots(self.from_a + level, 1), self.arrival(3, batch), p.across_a)

    def collect(self, batch):
        p = self.place
        levels = self.batches[batch]
        self.wait(self.slots(self.from_b + levels[0], len(levels)), self.arrival(1, batch))
        self.wait(self.slots(self.from_a + levels[0], len(levels)), self.arrival(3, batch))
        for level in levels:
            chip = p.at(p.d, level)
            for first in (0, self.from_b, self.from_a):
                self.add(chip, self.slots(first + level if first else chip, 1))

    def line(self, batch):
        p = self.place
        dst = self.slots(self.from_z + p.z, 1)
        for level in self.batches[batch]:
            chip = p.at(p.d, level)
            self.send(p.z != level, chip, 0, dst, self.arrival(4, batch), (chip, p.c))

    def keep(self):
        p = self.place
        own = self.kept(p.c)

        def total(batch):
            self.wait(self.slots(self.from_z, p.levels - 1), self.arrival(4, batch))
            here = self.view(p.d, p.c)
            others = [self.slots(self.from_z + (p.z + i) % p.levels, 1) for i in range(1, p.levels)]
            for part in range(self.parts):
                sum_now = here[part].astype(jnp.float32)
                for other in others:
                    sum_now = sum_now + other[part].astype(jnp.float32)
                own[part] = sum_now

        for batch, levels in enumerate(self.batches):
            pl.when((p.z >= levels[0]) & (p.z <= levels[-1]))(functools.partial(total, batch))

    def left(self, cond, way, count):
        part = self.slots(0, count)
        sem = self.send_sem.at[way]
        when(cond, lambda: remote(part, part, sem, self.recv_sem.at[0, 0], self.place.sibling).wait_send())

    def finish(self):
        p = self.place
        count = len(self.levels)
        for way, pieces in ((4, 4 * count), (3, 2 * count), (2, count)):
            self.left(None, way, pieces)
        for z in range(p.levels):
            self.left(p.z == z, 0, count - (z in self.levels))


class Chain(Reduce):
    def __init__(self, extra, line_sem, *rest):
        super().__init__(*rest)
        self.extra, self.line_sem = extra, line_sem

    def pass_on(self, here, level, way, waits, dst, device):
        p = self.place
        chip = p.at(p.d, level)
        slot = self.slots(self.from_z + level, 1)

        def act():
            if waits:
                self.wait(slot, self.line_sem.at[way, level])
                self.add(chip, slot)
            self.send(None, chip, way, dst, self.line_sem.at[way, level], device)

        pl.when(here)(act)

    def line(self, distance, batch):
        p = self.place
        for level in self.batches[batch]:
            slot = self.slots(self.from_z + level, 1)
            if level >= distance:
                self.pass_on(p.z == level - distance, level, 0, level > distance, slot, p.up)
            if level + distance < p.levels:
                dst = slot if distance > 1 else self.extra
                self.pass_on(p.z == level + distance, level, 1, level + distance < p.levels - 1, dst, p.down)

    def keep(self):
        p = self.place
        own = self.kept(p.c)

        def at(level):
            here = self.view(p.d, p.c)
            for part in range(self.parts):
                own[part] = here[part].astype(jnp.float32)
            sources = [(0, self.slots(self.from_z + level, 1))] if level > 0 else []
            sources += [(1, self.extra)] if level < p.levels - 1 else []
            for way, src in sources:
                self.wait(src, self.line_sem.at[way, level])
                for part in range(self.parts):
                    own[part] = own[part] + src[part].astype(jnp.float32)

        for level in self.levels:
            pl.when(p.z == level)(functools.partial(at, level))

    def finish(self):
        p = self.place
        count = len(self.levels)
        for way, pieces in ((4, 4 * count), (3, 2 * count), (2, count)):
            self.left(None, way, pieces)
        for z in range(p.levels):
            for way, pieces in enumerate((sum(n > z for n in self.levels), sum(n < z for n in self.levels))):
                if pieces:
                    self.left(p.z == z, way, pieces)


def handed(place, own_ref, core, send_sem, recv_sem):
    own = own_ref.at[core]
    return remote(own, own, send_sem, recv_sem, place.sibling)


class Terms:
    def __init__(self, place, sends, ref, got_ref, all_ref, send_sem, recv_sem):
        self.place, self.sends, self.ref, self.got_ref, self.all_ref = place, sends, ref, got_ref, all_ref
        self.send_sem, self.recv_sem = send_sem, recv_sem

    def copy(self, way, core, device):
        return remote(self.ref.at[core], self.got_ref.at[way], self.send_sem.at[way], self.recv_sem.at[way], device)

    def add(self, cond, way):
        if self.sends.closing:
            return

        def act():
            self.copy(way, 0, self.place.sibling).wait_recv()
            self.ref[self.place.c] = self.ref[self.place.c] + self.got_ref[way]

        when(cond, act)

    def share(self):
        self.sends.start(None, lambda: self.copy(0, 1 - self.place.c, self.place.sibling))

    def over_b(self):
        p = self.place
        self.add(None, 0)
        self.sends.start(p.b_at == 0, lambda: self.copy(1, p.c, p.across_b))

    def over_a(self):
        p = self.place
        self.add(p.b_at == 1, 1)
        self.sends.start((p.b_at == 1) & (p.a_at == 0), lambda: self.copy(2, p.c, p.across_a))

    def line(self):
        p = self.place
        home = (p.b_at == 1) & (p.a_at == 1)
        self.add(home, 2)
        here, top = self.ref.at[p.c], p.at(p.d, p.levels - 1)
        self.sends.start(
            home & p.has_up,
            lambda: remote(here, self.got_ref.at[3 + p.z], self.send_sem.at[3], self.recv_sem.at[3], (top, p.c)),
        )

    def keep(self):
        p = self.place
        got = self.got_ref.at[pl.ds(3, p.levels - 1)]
        remote(got, got, self.send_sem.at[3], self.recv_sem.at[3], p.sibling).wait_recv()
        for level in range(p.levels - 1):
            self.ref[p.c] = self.ref[p.c] + self.got_ref[3 + level]

    def final(self):
        return remote(
            self.ref.at[self.place.c],
            self.all_ref.at[self.place.c],
            self.send_sem.at[4],
            self.recv_sem.at[4],
            self.place.sibling,
        )

    def hand_over(self):
        p = self.place
        last = p.d == 4 * p.levels - 1
        if not self.sends.closing:
            pl.when(last)(self.keep)
        self.sends.start(last, self.final)

    def take_over(self):
        self.final().wait_recv()
        self.all_ref[self.place.c] = self.ref[self.place.c]


class Trail:
    def __init__(self, place, sends, flat, own_ref, line_ref, out_ref, send_sem, recv_sem, more_sem=None):
        self.place, self.sends, self.flat = place, sends, flat
        self.own_ref, self.line_ref, self.out_ref = own_ref, line_ref, out_ref
        self.send_sem, self.recv_sem, self.more_sem = send_sem, recv_sem, more_sem

    def copy(self, send_sem=None, device=None):
        f, p = self.flat, self.place
        return remote(
            self.line_ref.at[pl.ds(0, f.halo), :],
            self.line_ref.at[pl.ds(f.lines, f.halo), :],
            self.send_sem if send_sem is None else send_sem,
            self.recv_sem,
            (p.d - 1, p.c) if device is None else device,
        )

    def put(self, split, core):
        f = self.flat
        half = f.deep // 2
        for part in range(f.parts):
            for block in range(D // 128):
                first, stride = f.place_of(part, block, split)
                first = first + stride * half * core
                self.line_ref[pl.ds(first, half, stride=stride), :] = self.own_ref[
                    core, part, :, pl.ds(128 * block, 128)
                ]

    def half_lines(self, core, cond):
        p, f = self.place, self.flat
        pl.when(cond & (p.d < f.split))(lambda: self.put(True, core))
        pl.when(cond & (p.d >= f.split))(lambda: self.put(False, core))

    def early_back(self):
        p, f = self.place, self.flat
        for core, send_sem in ((0, self.send_sem), (1, self.more_sem)):
            make = lambda core=core, send_sem=send_sem: self.copy(send_sem, (p.d - 1, core))
            self.sends.start((p.c == 0) & (p.d > 0), make)

    def lines(self):
        p, f = self.place, self.flat

        def put(split):
            for core in range(2):
                self.put(split, core)

        def put_turned():
            for j in range(f.rows // 128):
                blocks = []
                for i in range(D // f.deep):
                    lanes = pl.ds(128 * (3 * (i % 2) + j), 128)
                    blocks += [self.own_ref[core, i // 2, :, lanes] for core in range(2)]
                turned = jnp.concatenate(blocks, 0).T
                for block in range(D // 128):
                    first = 6 * 128 * j + block
                    self.line_ref[pl.ds(first, 128, stride=6), :] = turned[:, 128 * block : 128 * (block + 1)]

        pl.when(p.d < f.split)(lambda: put(True))
        pl.when(p.d >= f.split)(put_turned if f.turned else lambda: put(False))

    def pass_back(self):
        self.sends.start(self.place.d > 0, self.copy)

    def last_rows(self, terms_ref, at, count):
        f = self.flat
        for core in range(2):
            for block in range(3):
                self.line_ref[pl.ds(f.lines + 3 * core + block, count, stride=6), :] = terms_ref[
                    core, pl.ds(at, count), pl.ds(128 * block, 128)
                ]

    def out(self):
        p, f = self.place, self.flat
        pl.when(p.d < f.chips - 1)(lambda: self.copy().wait_recv())
        self.out_ref[pl.ds(0, f.held), :] = shifted(self.line_ref, f.slip * p.d, f.held)


def dot(a, b):
    return jnp.dot(a, b, preferred_element_type=jnp.float32)


def dot_nt(a, b):
    return lax.dot_general(a, b, (((1,), (1,)), ((), ())), preferred_element_type=jnp.float32)


def square(values):
    return values.reshape(D, D)


def tile(index, size):
    return pl.ds(pl.multiple_of(index * size, size), size)


def loop(count, step, beside=()):
    def body(i, _):
        step(i)
        for at, act in beside:
            pl.when(i == at)(act)
        return 0

    lax.fori_loop(0, count, body, 0)


TILE, WIDE = 256, 512


class Layer:
    def __init__(self, refs, att_split, ffn_split, seqs, length):
        self.__dict__.update(refs)
        self.att_split, self.ffn_split = att_split, ffn_split
        self.seqs, self.length = seqs, length
        self.tiles = seqs * length // TILE

    def whole(self, blocks, part):
        count = blocks.shape[0] // 4
        return blocks[pl.ds(count * part, count)].reshape(self.seqs * self.length, D)

    def some(self, blocks, part, r, size=TILE):
        count = size // blocks.shape[1]
        return pl.ds(blocks.shape[0] // 4 * part + count * r, count)

    def qkv_weight(self, part):
        return square(self.att_w[pl.ds(0, self.att_split), part])

    def out_weight(self):
        return square(self.att_w[pl.ds(self.att_split, self.att_w.shape[0] - self.att_split)])

    def in_weight(self, part):
        return square(self.ffn_w[pl.ds(0, self.ffn_split), part])

    def down_weight(self, part):
        return square(self.ffn_w[pl.ds(self.ffn_split + 2 * part, 2)])

    def term(self, row):
        return self.terms[pl.ds(row, 1), :]

    def add_term(self, row, values):
        self.term_grads[pl.ds(row, 1), :] += jnp.sum(values, 0, keepdims=True)


    def qkv(self, beside=()):
        def step(r):
            rows = tile(r, TILE)
            x = self.tok[rows, :]
            queries = (dot(x, self.qkv_weight(0)) + self.term(0)).astype(jnp.bfloat16)
            self.heads[0, rows, :] = queries * HEAD_DIM ** (-0.5)
            self.heads[1, rows, :] = dot(x, self.qkv_weight(1)).astype(jnp.bfloat16)
            self.heads[2, rows, :] = (dot(x, self.qkv_weight(2)) + self.term(1)).astype(jnp.bfloat16)

        loop(self.tiles, step, beside)

    def make_bias(self):
        segs = self.segs[...].astype(jnp.float32)
        columns = jnp.concatenate([segs, jnp.zeros((8 - self.seqs, self.length), jnp.float32)], 0).T
        for seq in range(self.seqs):
            same = columns[:, seq : seq + 1] == segs[seq : seq + 1, :]
            self.bias[pl.ds(seq * self.length, self.length), :] = jnp.where(same, 0.0, masked)

    def lane_half(self, half):
        lane = lax.broadcasted_iota(jnp.int32, (self.length, 2 * HEAD_DIM), 1)
        return (lane // HEAD_DIM) == half

    def attend(self, beside=()):
        self.make_bias()

        def step(i):
            seq, pair = i // (HEADS // 2), i % (HEADS // 2)
            lanes = tile(pair, 2 * HEAD_DIM)
            rows = tile(seq, self.length)
            queries, keys, values = (self.heads[j, rows, lanes] for j in range(3))
            values_t = values.T
            parts = []
            for half in range(2):
                own = jnp.where(self.lane_half(half), queries, jnp.zeros_like(queries))
                scores = dot_nt(keys, own) + self.bias[rows, :]
                top = jnp.max(scores, 0, keepdims=True)
                raised = jnp.exp(scores - top)
                total = jnp.sum(raised, 0, keepdims=True)
                probs = (raised * (1.0 / total)).astype(jnp.bfloat16)
                self.totals[pl.ds(HEADS * seq + 2 * pair + half, 1), :] = top + jnp.log(total)
                parts.append(dot(values_t[HEAD_DIM * half : HEAD_DIM * (half + 1)], probs))
            both_t = jnp.concatenate(parts, 0).astype(jnp.bfloat16)
            self.ctx_t[lanes, rows] = both_t
            self.ctx[rows, lanes] = both_t.T

        loop(self.seqs * HEADS // 2, step, beside)

    def first_norm(self, beside=()):
        def step(r):
            rows = tile(r, TILE)
            residual = self.tok[rows, :].astype(jnp.float32) + dot(self.ctx[rows, :], self.out_weight()) + self.term(2)
            first, normed, rstd = normalize(residual, self.term(3), self.term(4))
            self.hat[rows, :] = normed
            self.rstd[rows, :] = rstd
            self.low_t[:, rows] = first.astype(jnp.bfloat16).T

        loop(self.tiles, step, beside)

    def feed(self, beside=()):
        def step(r):
            rows = tile(r, TILE)
            first = self.hat[rows, :] * self.term(3) + self.term(4)
            low = first.astype(jnp.bfloat16)
            second = first + self.term(12)
            for part in range(4):
                inner = dot(low, self.in_weight(part)) + self.term(8 + part)
                cdf, slope = gelu_parts(inner)
                act = (inner * cdf).astype(jnp.bfloat16)
                self.act[self.some(self.act, part, r)] = act.reshape(-1, self.act.shape[1], D)
                slope = slope.astype(jnp.bfloat16).reshape(-1, self.slope.shape[1], D)
                self.slope[self.some(self.slope, part, r)] = slope
                second = second + dot(act, self.down_weight(part))
            out, normed, rstd = normalize(second, self.term(13), self.term(14))
            seq = r // (self.length // TILE)
            live = jnp.clip(self.live_count[0] - seq, 0, 1).astype(jnp.float32)
            grad_out = self.cot[rows, :].astype(jnp.float32) * live
            self.out[rows, :] = out.astype(jnp.bfloat16)
            scaled = grad_out * self.term(13)
            grad = rstd * (
                scaled
                - jnp.mean(scaled, -1, keepdims=True)
                - normed * jnp.mean(scaled * normed, -1, keepdims=True)
            )
            self.add_term(13, grad_out * normed)
            self.add_term(14, grad_out)
            grad_down = grad.astype(jnp.bfloat16)
            self.add_term(12, grad_down.astype(jnp.float32))
            self.grad[rows, :] = grad
            self.down[rows, :] = grad_down
            self.down_t[:, rows] = grad_down.T

        loop(self.tiles, step, beside)


    def hidden_back(self, part, beside=()):
        def step(r):
            rows = tile(r, WIDE)
            grad_act = dot_nt(self.down[rows, :], self.down_weight(part))
            at = self.some(self.slope, part, r, WIDE)
            slope = self.slope[at].reshape(WIDE, D).astype(jnp.float32)
            inner = (grad_act * slope).astype(jnp.bfloat16)
            self.slope[at] = inner.reshape(-1, self.slope.shape[1], D)
            self.add_term(8 + part, inner.astype(jnp.float32))

        loop(self.seqs * self.length // WIDE, step, beside)

    def down_grads(self, part, beside=()):
        deep = self.ffn_w.shape[2]
        first = self.ffn_split + 2 * part
        count = self.act.shape[0] // 4

        def step(n):
            acts = self.act[pl.ds(count * part, count), :, tile(n, 256)].reshape(self.seqs * self.length, 256)
            grads = dot(self.down_t[...], acts).astype(jnp.bfloat16)
            for k in range(2):
                block = 2 * n + k
                for i in range(D // deep):
                    lanes = tile(3 * (i % 2) + block % 3, 128)
                    self.ffn_w[first + block // 3, i // 2, :, lanes] = grads[
                        deep * i : deep * (i + 1), 128 * k : 128 * (k + 1)
                    ]

        loop(3, step, beside)

    def in_back(self, part, beside=()):
        def step(r):
            rows = tile(r, WIDE)
            self.grad[rows, :] += dot_nt(
                self.slope[self.some(self.slope, part, r, WIDE)].reshape(WIDE, D), self.in_weight(part)
            )

        loop(self.seqs * self.length // WIDE, step, beside)

    def in_grads(self, part, beside=()):
        deep = self.ffn_w.shape[2]
        count = self.slope.shape[0] // 4

        def step(n):
            lanes = tile(n, 256)
            inner = self.slope[pl.ds(count * part, count), :, lanes].reshape(self.seqs * self.length, 256)
            grads = dot(self.low_t[...], inner).astype(jnp.bfloat16)
            self.ffn_w[pl.ds(0, self.ffn_split), part, :, lanes] = grads.reshape(self.ffn_split, deep, 256)

        loop(3, step, beside)

    def first_back(self, beside=()):
        def step(r):
            rows = tile(r, TILE)
            grad_first, normed = self.grad[rows, :], self.hat[rows, :]
            scaled = grad_first * self.term(3)
            grad = self.rstd[rows, :] * (
                scaled
                - jnp.mean(scaled, -1, keepdims=True)
                - normed * jnp.mean(scaled * normed, -1, keepdims=True)
            )
            self.add_term(3, grad_first * normed)
            self.add_term(4, grad_first)
            proj = grad.astype(jnp.bfloat16)
            self.add_term(2, proj.astype(jnp.float32))
            self.grad[rows, :] = grad
            shape = (-1, self.act.shape[1], D)
            self.act[self.some(self.act, 3, r)] = proj.reshape(shape)
            grad_context = dot_nt(proj, self.out_weight()).astype(jnp.bfloat16)
            self.act[self.some(self.act, 0, r)] = grad_context.reshape(shape)
            self.tok_t[:, rows] = self.tok[rows, :].T

        loop(self.tiles, step, beside)

    def out_grads(self, beside=()):
        count = self.act.shape[0] // 4

        def step(n):
            lanes = tile(n, 256)
            proj = self.act[pl.ds(3 * count, count), :, lanes].reshape(self.seqs * self.length, 256)
            grads = dot(self.ctx_t[...], proj).astype(jnp.bfloat16)
            owners = self.att_w.shape[0] - self.att_split
            shape = (owners, *self.att_w.shape[1:3], 256)
            self.att_w[pl.ds(self.att_split, owners), :, :, lanes] = grads.reshape(shape)

        loop(3, step, beside)

    def attend_back(self, group, beside=()):
        def step(i):
            seq, pair = i % self.seqs, 2 * group + i // self.seqs
            lanes = tile(pair, 2 * HEAD_DIM)
            rows = tile(seq, self.length)
            count = self.length // self.act.shape[1]
            queries, keys, values = (self.heads[j, rows, lanes] for j in range(3))
            grads = self.act[pl.ds(count * seq, count), :, lanes].reshape(self.length, 2 * HEAD_DIM)
            keys_t = keys.T
            parts = []
            grad_keys = grad_values = 0.0
            for half in range(2):
                here = self.lane_half(half)
                own = jnp.where(here, queries, jnp.zeros_like(queries))
                own_grads = jnp.where(here, grads, jnp.zeros_like(grads))
                total = self.totals[pl.ds(HEADS * seq + 2 * pair + half, 1), :]
                probs = jnp.exp(dot_nt(keys, own) + self.bias[rows, :] - total)
                grad_values = grad_values + dot(probs.astype(jnp.bfloat16), own_grads)
                grad_probs = dot_nt(values, own_grads)
                row_sum = jnp.sum(probs * grad_probs, 0, keepdims=True)
                grad_scores = (probs * (grad_probs - row_sum)).astype(jnp.bfloat16)
                grad_keys = grad_keys + dot(grad_scores, own)
                parts.append(dot(keys_t[HEAD_DIM * half : HEAD_DIM * (half + 1)], grad_scores))
            grad_queries = (jnp.concatenate(parts, 0) * HEAD_DIM ** (-0.5)).astype(jnp.bfloat16).T
            grad_values = grad_values.astype(jnp.bfloat16)
            self.heads[0, rows, lanes] = grad_queries
            self.heads[1, rows, lanes] = grad_keys.astype(jnp.bfloat16)
            self.heads[2, rows, lanes] = grad_values
            for row, grad in ((0, grad_queries), (1, grad_values)):
                self.term_grads[pl.ds(row, 1), lanes] += jnp.sum(grad.astype(jnp.float32), 0, keepdims=True)

        loop(2 * self.seqs, step, beside)

    def qkv_grads(self, group):
        lanes = pl.ds(4 * HEAD_DIM * group, 4 * HEAD_DIM)
        deep = self.att_w.shape[2]

        def step(part):
            grads = dot(self.tok_t[...], self.heads[part, :, lanes]).astype(jnp.bfloat16)
            for chip in range(self.att_split):
                self.act[self.act_first + 3 * chip + part, :, lanes] = grads[deep * chip : deep * (chip + 1)]

        loop(3, step)

    def input_back(self, beside=()):
        def step(r):
            rows = tile(r, TILE)
            total = self.grad[rows, :]
            for part in range(3):
                total = total + dot_nt(self.heads[part, rows, :], self.qkv_weight(part))
            self.gin[rows, :] = total.astype(jnp.bfloat16)

        loop(self.tiles, step, beside)


def gelu_parts(values):
    cdf = 0.5 * (1.0 + lax.erf(values * 0.5**0.5))
    return cdf, cdf + values * jnp.exp(-0.5 * values * values) * (2.0 * math.pi) ** (-0.5)


def batches(levels):
    half = levels // 2
    return [(level,) for level in range(half, levels)], [tuple(range(half))], [(levels - 1,)], [tuple(range(levels - 1))]


def scratch_shapes(levels, att, ffn, rows, seqs, length):
    bf16, f32 = jnp.bfloat16, jnp.float32
    vmem, dma = pltpu.VMEM, pltpu.SemaphoreType.DMA
    chips = att.chips
    turned = vmem((D, rows), bf16)
    f_batches, i_batches, o_batches, q_batches = batches(levels)
    shapes = dict(
        att_w=vmem((chips, att.parts, att.deep, D), bf16),
        ffn_w=vmem((chips, ffn.parts, ffn.deep, D), bf16),
        tok=vmem((rows, D), bf16),
        heads=vmem((3, rows, D), bf16),
        totals=vmem((seqs * HEADS, length), f32),
        ctx=vmem((rows, D), bf16),
        ctx_t=turned,
        hat=vmem((rows, D), f32),
        rstd=vmem((rows, 1), f32),
        low_t=turned,
        act=vmem((4 * rows // att.deep, att.deep, D), bf16),
        slope=vmem((8 * rows // att.deep, att.deep // 2, D), bf16),
        grad=vmem((rows, D), f32),
        down_t=turned,
        terms=vmem((16, D), f32),
        term_grads=vmem((16, D), f32),
        spare=vmem((48, 128), f32),
        terms_sum=vmem((2, 16, D // 2), f32),
        terms_got=vmem((2 + levels, 16, D // 2), f32),
        terms_all=vmem((2, 16, D // 2), f32),
        ffn_slots=vmem((chips + 4 * levels, ffn.parts, ffn.deep // 2, D), bf16),
        local_sem=dma((8,)),
        term_send=dma((3,)),
        term_recv=dma,
        sum_send=dma((5,)),
        sum_recv=dma((5,)),
        more_send=dma,
        free=pltpu.SemaphoreType.REGULAR,
        ffn_extra=vmem((ffn.parts, ffn.deep // 2, D), bf16),
        f_send=dma((5,)),
        f_line=dma((2, levels)),
        i_send=dma((2, 5)),
        i_recv=dma((2, len(i_batches), 5)),
        i_line=dma((2, 2, levels)),
        f_recv=dma((len(f_batches), 5)),
        o_send=dma((5,)),
        o_recv=dma((len(o_batches), 5)),
        q_send=dma((3, 5)),
        q_recv=dma((3, len(q_batches), 5)),
    )
    for name, flat in (("att_", att), ("ffn_", ffn)):
        half = (flat.parts, flat.deep // 2, D)
        own = dict(
            long=vmem((flat.halo + flat.held + 8, 128), f32),
            halo=vmem((flat.tail + flat.halo + 8, 128), f32),
            line=vmem((flat.lines + flat.halo + 8, 128), f32),
            own=vmem((2, *half), f32),
            send=dma((5,)),
            recv=dma((chips,)),
            sib=dma,
            plane_send=dma((5,)),
            plane_recv=dma((levels + 2,)),
            plane_sib=dma,
            halo_send=dma,
            halo_recv=dma,
            own_send=dma,
            own_recv=dma,
            back_send=dma,
            back_recv=dma,
        )
        shapes.update({name + key: shape for key, shape in own.items()})
    return shapes


def layer_kernel(names, levels, att, ffn, seqs, length, masters_in, tok_in, cot_in, segs, live_count,
                 out_out, gin_out, att_out, ffn_out, *scratch):
    s = types.SimpleNamespace(**dict(zip(names, scratch)))
    act_first = s.act.shape[0] // 4
    refs = dict(vars(s), segs=segs, live_count=live_count)
    refs.update(cot=s.tok, out=s.tok, down=s.ctx, tok_t=s.low_t)
    refs.update(bias=s.hat.at[:, pl.ds(0, length)], gin=s.tok, act_first=act_first)
    work = Layer(refs, att.split, ffn.split, seqs, length)

    def local(src, dst, at):
        copy = pltpu.make_async_copy(src, dst, s.local_sem.at[at])
        copy.start()
        return copy

    p = Place(levels)
    get_a = local(masters_in.at[pl.ds(0, att.held), :], s.att_long.at[pl.ds(att.halo, att.held), :], 0)
    get_f = local(masters_in.at[pl.ds(att.held, ffn.held), :], s.ffn_long.at[pl.ds(ffn.halo, ffn.held), :], 1)
    get_t = local(tok_in, s.tok, 2)
    p.meet()
    sends = Sends()
    lead_a = Lead(p, sends, att, s.att_long, s.att_halo, s.att_line, s.att_halo_send, s.att_halo_recv)
    lead_f = Lead(p, sends, ffn, s.ffn_long, s.ffn_halo, s.ffn_line, s.ffn_halo_send, s.ffn_halo_recv)
    get_a.wait()
    sends.go(lead_a.begin)
    get_f.wait()
    sends.go(lead_f.begin)
    lead_a.lines()
    lead_f.lines()
    lead_a.join()
    lead_a.store(s.att_w)
    def gathers(ref, cut, *sems):
        parts, lanes = ref.shape[1], pl.ds(0, D)
        if cut[0]:
            first, last = (pl.ds(0, parts - cut[0]), lanes), (pl.ds(parts - cut[0], cut[0]), lanes)
        else:
            first = (pl.ds(0, parts), pl.ds(0, D - cut[1]))
            last = (pl.ds(0, parts), pl.ds(D - cut[1], cut[1]))
        go, plane = Gather(p, ref, *first, *sems[:3]), Plane(p, ref, *last, *sems[3:])
        return go, plane

    go_a = gathers(
        s.att_w, (0, 128), s.att_send, s.att_recv, s.att_sib, s.att_plane_send, s.att_plane_recv, s.att_plane_sib
    )
    go_f = gathers(
        s.ffn_w, (1, 0), s.ffn_send, s.ffn_recv, s.ffn_sib, s.ffn_plane_send, s.ffn_plane_recv, s.ffn_plane_sib
    )
    (a, a_plane), (f, f_plane) = go_a, go_f
    a.own()
    a_plane.own()

    def last():
        terms, spare = s.terms, s.spare
        terms[...] = jnp.zeros(terms.shape, terms.dtype)
        for lead, at, count in ((lead_a, 0, 5), (lead_f, 8, 7)):
            rows = lead.last_rows(count)
            spare[pl.ds(0, rows.shape[0]), :] = rows
            for block in range(D // 128):
                terms[pl.ds(at, count), pl.ds(128 * block, 128)] = spare[pl.ds(block, count, stride=6), :]

    pl.when(p.d == att.chips - 1)(last)
    lead_f.join()
    lead_f.store(s.ffn_w)
    s.term_grads[...] = jnp.zeros(s.term_grads.shape, jnp.float32)
    a.line(1)
    a.over_a(0)
    a_plane.near()
    a.line(2)
    a.over_b(0)
    a_plane.complete()
    a.over_a(1)
    a.line(3)
    f_plane.own()
    a.over_a(2)
    f.own()
    a_plane.line(1)
    a.over_b(1)
    a.over_b(2)
    a.over_a(3)
    f_plane.near()
    a_plane.line(2)
    f.line(1)
    a.over_b(3)
    a_plane.line(3)
    sends.go(Spread(p, sends, s.terms, s.term_send, s.term_recv).run)
    for go in go_a:
        go.from_sibling()
    get_t.wait()

    on = functools.partial
    work.qkv(((2, on(f.over_a, 0)), (2, on(f.line, 2)), (2, f_plane.complete),))
    work.attend(
        (
            (3, on(f.over_a, 1)),
            (3, on(f.line, 3)),
            (6, on(f_plane.line, 1)),
            (8, on(f.over_a, 2)),
            (9, on(f.over_b, 0)),
            (10, on(f_plane.line, 2)),
            (10, on(f.over_b, 1)),
            (10, on(f.over_a, 3)),
        )
    )
    work.first_norm()
    f.over_b(2)
    f_plane.line(3)
    f.over_b(3)

    get_c = local(cot_in, s.tok, 2)
    for go in go_f:
        go.from_sibling()
    get_c.wait()
    work.feed()
    put_o = local(s.tok, out_out, 3)
    sends.finish()
    for go in (*go_a, *go_f):
        go.finish()

    sums = Sends()
    slots, slope, act = s.ffn_slots, s.slope, s.act
    half_a, half_f = att.deep // 2, ffn.deep // 2

    def of(ref, half):
        return lambda chip, core: ref.at[chip, :, tile(core, half), :]

    def att_slots(lanes):
        return lambda i, count: slope.at[pl.ds(3 * i, 3 * count), :, lanes]

    f_batches, i_batches, o_batches, q_batches = batches(levels)
    everything = pl.ds(0, D)
    ffn_slots = lambda i, count: slots.at[i] if count == 1 else slots.at[pl.ds(i, count)]
    add_f = Chain(
        s.ffn_extra, s.f_line, p, 4, ffn.chips, f_batches, of(s.ffn_w, half_f), ffn_slots,
        lambda core: s.ffn_own.at[core], s.f_send, s.f_recv,
    )
    add_i = []
    for group in range(2):
        parts = pl.ds(2 * group, 2)
        own_chips = pl.ds(0, ffn.split)
        whole = (s.ffn_w.at[own_chips, parts, tile(1 - p.c, half_f), :], slots.at[own_chips, parts])
        add_i.append(
            Chain(
                s.ffn_extra.at[parts], s.i_line.at[group], p, 2, ffn.chips, i_batches,
                lambda chip, core, parts=parts: s.ffn_w.at[chip, parts, tile(core, half_f), :],
                lambda i, count, parts=parts: slots.at[i, parts] if count == 1 else slots.at[pl.ds(i, count), parts],
                lambda core, parts=parts: s.ffn_own.at[core, parts], s.i_send.at[group], s.i_recv.at[group], whole,
            )
        )
    add_o = Reduce(
        p, 3, att.chips, o_batches, of(s.att_w, half_a), att_slots(everything),
        lambda core: s.att_own.at[core], s.o_send, s.o_recv,
    )
    add_q = []
    for group in range(3):
        lanes = pl.ds(256 * group, 256)
        blocks = pl.ds(act_first, 3 * att.split)
        view = lambda chip, core, lanes=lanes: act.at[pl.ds(act_first + 3 * chip, 3), tile(core, half_a), lanes]
        whole = (act.at[blocks, tile(1 - p.c, half_a), lanes], slope.at[pl.ds(0, 3 * att.split), :, lanes])
        add_q.append(
            Reduce(
                p, 3, att.chips, q_batches, view, att_slots(lanes),
                lambda core, lanes=lanes: s.att_own.at[core, :, :, lanes], s.q_send.at[group], s.q_recv.at[group], whole,
            )
        )
    add_t = Terms(p, sums, s.terms_sum, s.terms_got, s.terms_all, s.sum_send, s.sum_recv)

    def do(act, *at):
        return sums.later(functools.partial(act, *at))

    q = add_q
    work.hidden_back(0)
    work.down_grads(0)
    work.hidden_back(1)
    work.down_grads(1)
    add_f.share(0)
    put_o.wait()
    get_t = local(tok_in, s.tok, 2)
    work.hidden_back(2)
    work.down_grads(2, (
            (2, on(add_f.over_b, 0)),
        ))
    work.hidden_back(3)
    work.down_grads(3)
    add_f.share(1)
    work.in_back(0)
    work.in_grads(0, (
            (2, on(add_f.over_b, 1)),
        ))
    work.in_back(1)
    work.in_grads(1)
    add_i[0].share(0)
    work.in_back(2)
    work.in_grads(2, (
            (1, on(add_f.over_a, 0)),
        ))
    work.in_back(3, (
            (0, on(add_f.over_a, 1)),
        ))
    work.in_grads(3)
    add_i[1].share(0)

    line = [(p.turn(distance), p.c) for distance in range(1, levels)]
    for device in (p.sibling, p.across_a, p.across_b, *line):
        pl.semaphore_signal(s.free, inc=1, device_id=device, device_id_type=MESH_ID)
    get_t.wait()
    work.first_back((
            (0, on(add_i[0].over_b, 0)),
            (3, on(add_f.collect, 1)),
        ))
    work.out_grads((
            (1, on(add_i[1].over_b, 0)),
            (2, on(add_f.line, 3, 1)),
        ))
    pl.semaphore_wait(s.free, 2 + levels)
    add_o.share(0)
    work.make_bias()
    work.attend_back(0, (
            (1, on(add_f.collect, 0)),
            (2, on(add_f.line, 2, 0)),
            (2, on(add_i[0].over_a, 0)),
        ))
    work.qkv_grads(0)
    q[0].share(0)
    work.attend_back(1, (
            (0, on(add_f.line, 2, 1)),
            (0, on(add_f.line, 1, 0)),
            (0, on(add_i[1].over_a, 0)),
            (2, on(q[0].over_b, 0)),
            (3, on(add_i[0].collect, 0)),
            (3, on(add_o.over_b, 0)),
            (3, on(add_i[0].line, 3, 0)),
        ))
    work.qkv_grads(1)
    q[1].share(0)
    q[1].over_b(0)
    add_i[1].collect(0)
    add_i[0].line(2, 0)
    q[0].over_a(0)
    work.attend_back(2, (
            (1, on(add_o.over_a, 0)),
            (1, on(add_i[1].line, 3, 0)),
            (1, on(add_i[0].line, 1, 0)),
            (2, on(q[0].collect, 0)),
            (2, on(q[0].line, 0)),
            (3, on(add_f.line, 1, 1)),
        ))
    work.qkv_grads(2)
    q[2].share(0)
    for core in range(2):
        s.terms_sum[core] = s.term_grads[:, pl.ds(D // 2 * core, D // 2)]
    do(add_t.share)()
    trail_f = Trail(p, sums, ffn, s.ffn_own, s.ffn_line, s.ffn_long, s.ffn_back_send, s.ffn_back_recv)
    trail_a = Trail(p, sums, att, s.att_own, s.att_line, s.att_long, s.att_back_send, s.att_back_recv, s.more_send)
    given_f = lambda core: handed(p, s.ffn_own, core, s.ffn_own_send, s.ffn_own_recv)
    given_a = lambda core: handed(p, s.att_own, core, s.att_own_send, s.att_own_recv)
    add_o.collect(0)
    add_i[1].line(2, 0)
    add_o.line(0)
    q[1].over_a(0)
    work.input_back((
            (0, on(q[2].over_b, 0)),
            (0, on(add_i[1].line, 1, 0)),
            (0, on(q[1].collect, 0)),
            (0, do(add_t.over_b)),
            (2, on(q[2].over_a, 0)),
            (2, on(q[1].line, 0)),
            (2, do(add_t.over_a)),
            (3, on(q[2].collect, 0)),
            (3, do(add_t.line)),
        ))
    put_g = local(work.gin, gin_out, 4)
    add_f.keep()
    q[0].keep()
    add_i[0].keep()
    q[2].line(0)
    add_i[1].keep()
    sums.go(lambda: sums.start(None, lambda: given_f(p.c)))
    add_o.keep()
    q[1].keep()
    given_f(1 - p.c).wait_recv()
    trail_f.lines()
    sums.go(trail_f.pass_back)
    q[2].keep()
    sums.go(lambda: sums.start(None, lambda: given_a(p.c)))
    trail_a.half_lines(0, p.c == 0)
    sums.go(trail_a.early_back)
    trail_a.half_lines(1, p.c == 1)
    do(add_t.hand_over)()
    given_a(1 - p.c).wait_recv()
    trail_a.half_lines(1, p.c == 0)
    trail_a.half_lines(0, p.c == 1)
    final = p.d == att.chips - 1

    def terms_here():
        add_t.take_over()
        trail_f.last_rows(s.terms_all, 8, 7)
        trail_a.last_rows(s.terms_all, 0, 5)

    pl.when(final)(terms_here)
    trail_f.out()
    put_f = local(s.ffn_long.at[pl.ds(0, ffn.held), :], ffn_out, 1)
    trail_a.out()
    put_a = local(s.att_long.at[pl.ds(0, att.held), :], att_out, 0)
    sums.finish()
    for who in (add_f, *add_i, add_o, *q):
        who.finish()
    for copy in (put_g, put_f, put_a):
        copy.wait()


def run_layer(levels, att, ffn, masters, tokens, cotangent, segments, live_count):
    vmem = pl.BlockSpec(memory_space=pltpu.VMEM)
    anywhere = pl.BlockSpec(memory_space=pl.ANY)
    seqs, length = segments.shape
    rows = tokens.shape[0]
    bf16, f32 = jnp.bfloat16, jnp.float32
    shape = jax.ShapeDtypeStruct
    scratch = scratch_shapes(levels, att, ffn, rows, seqs, length)
    return pl.pallas_call(
        functools.partial(layer_kernel, tuple(scratch), levels, att, ffn, seqs, length),
        out_shape=(
            shape(tokens.shape, bf16),
            shape(tokens.shape, bf16),
            shape((att.held, 128), f32),
            shape((ffn.held, 128), f32),
        ),
        in_specs=[anywhere, anywhere, anywhere, vmem, pl.BlockSpec(memory_space=pltpu.SMEM)],
        out_specs=(anywhere, anywhere, anywhere, anywhere),
        scratch_shapes=list(scratch.values()),
        compiler_params=pltpu.CompilerParams(
            collective_id=1, has_side_effects=True, vmem_limit_bytes=64 * 2**20
        ),
        name="layer",
    )(masters, tokens, cotangent, segments, live_count)


def as_lines(flat, vector):
    return jnp.pad(vector, (0, flat.held * 128 - flat.length)).reshape(flat.held, 128)


def fast_body(
    levels,
    tokens,
    cotangent,
    segments,
    live_count,
    att_master,
    att_first,
    att_second,
    ffn_master,
    ffn_first,
    ffn_second,
):
    chips = lax.axis_size("dp")
    att = Flat(att_master.shape[0], chips, 3, 3 * chips // 4, False)
    ffn = Flat(ffn_master.shape[0], chips, 4, chips // 2, True)
    output, input_grad, att_sum, ffn_sum = run_layer(
        levels,
        att,
        ffn,
        jnp.concatenate([as_lines(att, att_master), as_lines(ffn, ffn_master)]),
        tokens,
        cotangent,
        segments,
        live_count,
    )
    att_grad = att_sum.reshape(-1)[: att.length]
    ffn_grad = ffn_sum.reshape(-1)[: ffn.length]
    att_new = adam_update(att_master, att_first, att_second, att_grad)
    ffn_new = adam_update(ffn_master, ffn_first, ffn_second, ffn_grad)
    return (output, input_grad, att_grad, *att_new, ffn_grad, *ffn_new)


def body_for(mesh):
    chips, cores = mesh.shape["dp"], mesh.shape["rep"]
    if chips == 16 and cores == 2:
        return functools.partial(fast_body, chips // 4)
    return general_body


def solution(mesh):
    placed = (
        P(("dp", "rep"), None),
        P(("dp", "rep"), None),
        P(("dp", "rep"), None),
        P(("dp", "rep")),
        P("dp"),
        P("dp"),
        P("dp"),
        P("dp"),
        P("dp"),
        P("dp"),
    )
    return jax.shard_map(
        body_for(mesh),
        mesh=mesh,
        in_specs=placed,
        out_specs=(
            P(("dp", "rep"), None),
            P(("dp", "rep"), None),
            P("dp"),
            P("dp"),
            P("dp"),
            P("dp"),
            P("dp"),
            P("dp"),
            P("dp"),
            P("dp"),
        ),
        check_vma=False,
    )
```
